32 devices in a mesh: seq: 8 (over y, x, core), chan: 4 (over z).
Axes of the slice: x: 2, y: 2, z: 4, core: 2. Of those that a mesh axis runs over, the one named last changes fastest.
Arguments:
- tokens: bfloat16 [4096, 2048], P(('seq', 'chan')), may hold values from -6 to 6
- norm_gains: bfloat16 [2, 2048], replicated, may hold values from 0.5 to 1.5
- conv_weight: bfloat16 [3, 2048], P(None, 'chan'), may hold values from -3 to 3
- in_weight: bfloat16 [3, 2048, 2048], P(None, None, 'chan'), may hold values from -0.125 to 0.125
- out_weight: bfloat16 [2048, 2048], P('chan'), may hold values from -0.125 to 0.125
- gate_up_weight: bfloat16 [2, 2048, 8192], P(None, None, 'chan'), may hold values from -0.125 to 0.125
- down_weight: bfloat16 [8192, 2048], P('chan'), may hold values from -0.0625 to 0.0625
- starts: int32 [10], replicated, may hold values from 0 to 4095, as said below
- cotangent: bfloat16 [4096, 2048], P(('seq', 'chan')), may hold values from -6 to 6
Outputs:
- block_output: bfloat16 [4096, 2048], P(('seq', 'chan'))
- input_grad: float32 [4096, 2048], P(('seq', 'chan'))
- gains_grad: float32 [2, 2048], replicated
- conv_grad: float32 [3, 2048], P(None, 'chan')
- in_weight_grad: float32 [3, 2048, 2048], P(None, 'seq', 'chan')
- out_weight_grad: float32 [2048, 2048], P('chan', 'seq')
- gate_up_grad: float32 [2, 2048, 8192], P(None, 'seq', 'chan')
- down_grad: float32 [8192, 2048], P('chan', 'seq')
The draws below stay inside these ranges and needn't reach their ends.
Inputs may be any that keep to these rules, and one draw needn't show every extreme that they name: Positions where documents start, in no order and possibly repeated; position 0 starts the stream in any case. No document is longer than 2048 tokens and one is exactly 2048 long. No entry p has p % 512 < 2.
All inputs are finite; a program needn't handle non-finite values.
Results may differ from the reference program's by a relative error of at most 0.0099.
Values may be sent and summed in bfloat16 or wider, within the bound.
No kernel may reach another device: no remote copies, remote signals or barrier semaphores. Data moves between devices by JAX's collectives and lax.ppermute only.
A program may use at most 320 MiB of HBM per device.

```python
import jax
import jax.numpy as jnp
from jax import lax

D = 2048
FF = 8192
TOK_DEV = 512
TOKENS = 4096
DOC_MAX = 2048
NSEG = 2
CUTS = 8


def draw_starts(key, part):
    key = jax.random.fold_in(key, 7)
    keys = jax.random.split(key, 5)
    blocks = DOC_MAX // TOK_DEV
    offset = TOK_DEV * jax.random.randint(keys[0], (), 0, blocks) + jax.random.randint(keys[1], (), 2, TOK_DEV)
    regular = offset + DOC_MAX * jnp.arange(NSEG, dtype=jnp.int32)
    whole_doc = jax.random.randint(keys[2], (), 0, NSEG - 1)
    kept_start = offset + DOC_MAX * whole_doc
    shards = TOKENS // TOK_DEV
    extra = TOK_DEV * jax.random.randint(keys[3], (CUTS,), 0, shards) + jax.random.randint(keys[4], (CUTS,), 2, TOK_DEV)
    inside = (extra >= kept_start) & (extra < kept_start + DOC_MAX)
    extra = jnp.where(inside, kept_start, extra)
    return jnp.concatenate([regular, extra]).astype(jnp.int32)


def levels(key, shape, cuts, low, top_value):
    level = 1.0
    for dim, blocks in cuts:
        draws = jax.random.uniform(jax.random.fold_in(jax.random.fold_in(key, 6), dim), (blocks,), jnp.float32, low / len(cuts), top_value / len(cuts))
        level = level * jnp.repeat(jnp.exp(draws), shape[dim] // blocks).reshape((-1,) + (1,) * (len(shape) - 1 - dim))
    return level


def centred(key, dims, deviation, bound, cuts=(), kind=jnp.bfloat16):
    drawn = jax.random.normal(key, dims, jnp.float32) * deviation
    if len(cuts) > 0:
        drawn = levels(key, dims, cuts, -0.22, 0.18) * drawn
    return jnp.clip(drawn, min=-bound, max=bound).astype(kind)


def setup_inputs(seed: int = 0) -> dict:
    splits = jax.random.split(jax.random.key(seed), 10)
    return {
        "tokens": centred(splits[0], (TOKENS, D), 1.0, 6.0, ((0, 32),)),
        "norm_gains": jnp.clip(1.0 + 0.1 * jax.random.normal(splits[1], (2, D), jnp.float32), 0.5, 1.5).astype(jnp.bfloat16),
        "conv_weight": centred(splits[2], (3, D), 0.6, 3.0, ((1, 4),)),
        "in_weight": centred(splits[3], (3, D, D), D ** -0.5, 0.125, ((2, 4),)),
        "out_weight": centred(splits[4], (D, D), D ** -0.5, 0.125, ((0, 4),)),
        "gate_up_weight": centred(splits[5], (2, D, FF), D ** -0.5, 0.125, ((2, 4),)),
        "down_weight": centred(splits[6], (FF, D), FF ** -0.5, 0.0625, ((0, 4),)),
        "starts": draw_starts(jax.random.fold_in(splits[9], 71), 0),
        "cotangent": centred(splits[8], (TOKENS, D), 1.0, 6.0, ((0, 32),)),
    }


EPS = 1e-05

@jax.custom_vjp
def low(v):
    return lax.optimization_barrier(v.astype(jnp.bfloat16)).astype(jnp.float32)

@jax.custom_vjp
def low_back(v):
    return v

def low_keep(v):
    return (low(v), None)

def low_pass(kept, grad):
    return (grad,)

def back_keep(v):
    return (v, None)

def back_low(kept, grad):
    return (low(grad),)
low.defvjp(low_keep, low_pass)
low_back.defvjp(back_keep, back_low)

def normalize(values, gain_row):
    return values * lax.rsqrt(lax.optimization_barrier(jnp.mean(values * values, axis=-1, keepdims=True)) + EPS) * gain_row

def delayed(values, steps):
    padding = jnp.zeros((steps, values.shape[1]), values.dtype)
    return jnp.concatenate([padding, values[:values.shape[0] - steps]], axis=0)

def forward(tokens, norm_gains, conv_weight, in_weight, out_weight, gate_up_weight, down_weight, keep_one, keep_two):
    highest = lax.Precision.HIGHEST
    normed_one = low(normalize(tokens, norm_gains[0]))
    projected = low_back(jnp.einsum('td,kde->kte', normed_one, in_weight, precision=highest))
    mixed_in = low(projected[0] * projected[2])
    conv_out = conv_weight[0] * mixed_in + conv_weight[1] * keep_one * delayed(mixed_in, 1) + conv_weight[2] * keep_two * delayed(mixed_in, 2)
    conv_out = low_back(conv_out)
    gated_mix = low(projected[1] * conv_out)
    mixer_out = low_back(jnp.dot(gated_mix, out_weight, precision=highest))
    hidden_state = tokens + mixer_out
    normed_two = low(normalize(hidden_state, norm_gains[1]))
    gate_up = low_back(jnp.einsum('td,kdf->ktf', normed_two, gate_up_weight, precision=highest))
    hidden = low(jax.nn.silu(gate_up[0]) * gate_up[1])
    return hidden_state + jnp.dot(hidden, down_weight, precision=highest)

def reference(tokens, norm_gains, conv_weight, in_weight, out_weight, gate_up_weight, down_weight, starts, cotangent):
    positions = jnp.arange(TOKENS, dtype=jnp.int32)
    at_start = jnp.any(positions[:, None] == starts[None, :], axis=1)
    prev_start = jnp.any((positions - 1)[:, None] == starts[None, :], axis=1)
    keep_one = ((positions >= 1) & jnp.logical_not(at_start)).astype(jnp.float32)[:, None]
    keep_two = ((positions >= 2) & jnp.logical_not(at_start) & jnp.logical_not(prev_start)).astype(jnp.float32)[:, None]
    params = tuple((argument.astype(jnp.float32) for argument in (tokens, norm_gains, conv_weight, in_weight, out_weight, gate_up_weight, down_weight)))

    def whole_block(*inputs):
        return forward(*inputs, keep_one, keep_two)
    result, pull_back = jax.vjp(whole_block, *params)
    grads = pull_back(cotangent.astype(jnp.float32))
    return (result.astype(jnp.bfloat16), grads[0], grads[1], grads[2], grads[3], grads[4], grads[5], grads[6])
```

```python
import jax
import jax.numpy as jnp
from jax import lax
from jax.sharding import PartitionSpec as P

EPS = 1e-05
BF = jnp.bfloat16
F32 = jnp.float32


def passed_along(block, axis, distance):
    devices = range(lax.axis_size(axis))
    route = [(i - distance, i) for i in devices if i - distance in devices]
    return lax.ppermute(block, axis, route)


def swapped(block, axis, bit):
    return lax.ppermute(block, axis, [(i, i ^ bit) for i in range(lax.axis_size(axis))])


def summed(block, axis):
    bit = 1
    while bit < lax.axis_size(axis):
        block = block + swapped(block, axis, bit)
        bit *= 2
    return block


def keep_masks(positions, starts):
    at_start = jnp.any(positions[:, None] == starts[None, :], axis=1)
    prev_start = jnp.any((positions - 1)[:, None] == starts[None, :], axis=1)
    keep_one = ((positions >= 1) & jnp.logical_not(at_start)).astype(F32)[:, None]
    keep_two = ((positions >= 2) & jnp.logical_not(at_start) & jnp.logical_not(prev_start)).astype(
        F32
    )[:, None]
    return (keep_one, keep_two)


def unit_rows(values):
    inv_scale = lax.rsqrt(jnp.mean(values * values, axis=-1, keepdims=True) + EPS)
    return (values * inv_scale, inv_scale)


def norm_back(grad_normed, unit_vals, inv_scale, gain_row):
    weighted = grad_normed * gain_row
    return inv_scale * (
        weighted - unit_vals * jnp.mean(weighted * unit_vals, axis=-1, keepdims=True)
    )


def both_cores(block):
    return jnp.concatenate([block, swapped(block, "seq", 1)], axis=0)


def own_slices(block):
    count = lax.axis_size("seq")
    rows, width = block.shape
    split = block.reshape(rows, count // 2, 2, width // count)
    core = lax.axis_index("seq") % 2
    mine = lax.dynamic_index_in_dim(split, core, 2, keepdims=False)
    other = lax.dynamic_index_in_dim(split, 1 - core, 2, keepdims=False)
    return jnp.concatenate([mine, swapped(other, "seq", 1)], axis=0)


def scattered(product, slices, order):
    group = lax.axis_index("seq") // 2
    received = []
    for step, bit in enumerate(order):
        own = (group // bit) % 2
        keep = lax.dynamic_index_in_dim(slices, own, 1, keepdims=False)
        send = lax.dynamic_index_in_dim(slices, 1 - own, 1, keepdims=False)
        total = product(send)
        for earlier, owns in received:
            part = earlier
            for place, index in enumerate(owns):
                part = lax.dynamic_index_in_dim(part, index, 0, keepdims=False)
            part = lax.dynamic_index_in_dim(part, 1 - own, 0, keepdims=False)
            total = total + part.astype(F32)
        arrived = swapped(total.astype(BF), "seq", 2 * bit)
        received = [(earlier, owns + [own]) for earlier, owns in received] + [(arrived, [])]
        slices = keep
    total = product(slices)
    for earlier, owns in received:
        part = earlier
        for index in owns:
            part = lax.dynamic_index_in_dim(part, index, 0, keepdims=False)
        total = total + part.astype(F32)
    return total


def ordered(slices, order, bits):
    rows, groups, width = slices.shape
    split = slices.reshape((rows,) + (2,) * len(bits) + (width,))
    return jnp.transpose(split, (0, *[1 + bits.index(bit) for bit in order], len(bits) + 1))


def group_bits():
    groups = lax.axis_size("seq") // 2
    bits = []
    while groups > 1:
        groups //= 2
        bits.append(groups)
    return bits


def on_device(
    tokens,
    norm_gains,
    conv_weight,
    in_weight,
    out_weight,
    gate_up_weight,
    down_weight,
    starts,
    cotangent,
):
    shard_rows = tokens.shape[0]
    chan_count = lax.axis_size("chan")
    seq_rows = shard_rows * chan_count
    chan_cols = conv_weight.shape[1]
    chan_index = lax.axis_index("chan")
    base_pos = lax.axis_index("seq") * seq_rows
    positions = base_pos + jnp.arange(seq_rows, dtype=jnp.int32)
    keep_one, keep_two = keep_masks(positions, starts)
    next_one, unused_one = keep_masks(positions + 1, starts)
    unused_two, next_two = keep_masks(positions + 2, starts)
    gain_one = norm_gains[0].astype(F32)
    gain_two = norm_gains[1].astype(F32)
    conv_taps = conv_weight.astype(F32)
    bits = group_bits()
    orders = (bits[::-1], bits)

    inputs_all = lax.all_gather(tokens, "chan", axis=0, tiled=True)
    grad_out = lax.all_gather(cotangent, "chan", axis=0, tiled=True)
    input_rows = tokens.astype(F32)
    unit_all, scale_all = unit_rows(inputs_all.astype(F32))
    normed_one = (unit_all * gain_one).astype(BF)

    projected = jnp.einsum("td,kde->kte", normed_one, in_weight, preferred_element_type=F32)
    mixed_in = (projected[0] * projected[2]).astype(BF)
    rim_rows = passed_along(mixed_in[seq_rows - 2 :], "seq", 1)
    extended = jnp.concatenate([rim_rows, mixed_in], axis=0).astype(F32)
    lag_one = keep_one * extended[1 : seq_rows + 1]
    lag_two = keep_two * extended[0:seq_rows]
    conv_out = conv_taps[0] * extended[2:] + conv_taps[1] * lag_one + conv_taps[2] * lag_two
    gated_mix = (projected[1] * conv_out).astype(BF)
    mixer_own = lax.psum_scatter(
        jnp.dot(gated_mix, out_weight, preferred_element_type=F32).astype(BF),
        "chan",
        scatter_dimension=0,
        tiled=True,
    ).astype(F32)
    state_own = input_rows + mixer_own
    unit_two, scale_two = unit_rows(state_own)
    normed_two = lax.all_gather((unit_two * gain_two).astype(BF), "chan", axis=0, tiled=True)
    gate_up = jnp.einsum("td,kdf->ktf", normed_two, gate_up_weight, preferred_element_type=F32)
    sigmoid_gate = jax.nn.sigmoid(gate_up[0])
    activated = gate_up[0] * sigmoid_gate
    hidden = (activated * gate_up[1]).astype(BF)
    ffn_own = lax.psum_scatter(
        jnp.dot(hidden, down_weight, preferred_element_type=F32).astype(BF),
        "chan",
        scatter_dimension=0,
        tiled=True,
    ).astype(F32)
    block_output = (state_own + ffn_own).astype(BF)

    grad_hidden = jnp.einsum("td,fd->tf", grad_out, down_weight, preferred_element_type=F32)
    grad_gate = grad_hidden * gate_up[1] * sigmoid_gate * (1.0 + gate_up[0] * (1.0 - sigmoid_gate))
    grad_up = grad_hidden * activated
    grad_pair = jnp.stack([grad_gate, grad_up]).astype(BF)
    grad_two_own = lax.psum_scatter(
        jnp.einsum("ktf,kdf->td", grad_pair, gate_up_weight, preferred_element_type=F32).astype(BF),
        "chan",
        scatter_dimension=0,
        tiled=True,
    ).astype(F32)

    cot_slices = own_slices(grad_out)
    hidden_both = both_cores(hidden)
    half = hidden.shape[1] // 2
    down_parts = []
    for place, order in enumerate(orders):
        units = hidden_both[:, place * half : (place + 1) * half]
        down_parts.append(
            scattered(
                lambda s, u=units: jnp.moveaxis(
                    jnp.einsum("tf,t...d->f...d", u, s, preferred_element_type=F32), 0, -2
                ),
                ordered(cot_slices, order, bits),
                order,
            )
        )
    down_grad = jnp.concatenate(down_parts, axis=0)

    normed_two_slices = own_slices(normed_two)
    gate_up_parts = []
    for place, order in enumerate(orders):
        units = both_cores(grad_pair[place])
        gate_up_parts.append(
            scattered(
                lambda s, u=units: jnp.einsum("t...d,tf->...df", s, u, preferred_element_type=F32),
                ordered(normed_two_slices, order, bits),
                order,
            )
        )
    gate_up_grad = jnp.stack(gate_up_parts)

    grad_state_own = cotangent.astype(F32) + norm_back(grad_two_own, unit_two, scale_two, gain_two)
    gain_two_part = jnp.sum(grad_two_own * unit_two, axis=0)
    grad_mix = lax.all_gather(grad_state_own.astype(BF), "chan", axis=0, tiled=True)

    grad_gated = jnp.einsum("td,ed->te", grad_mix, out_weight, preferred_element_type=F32)
    grad_conv = (grad_gated * projected[1]).astype(BF)
    grad_c = grad_gated * conv_out
    rim_back = passed_along(grad_conv[:2], "seq", -1)
    ext_back = jnp.concatenate([grad_conv, rim_back], axis=0).astype(F32)
    grad_here = ext_back[:seq_rows]
    grad_mixed = (
        conv_taps[0] * grad_here
        + conv_taps[1] * next_one * ext_back[1 : seq_rows + 1]
        + conv_taps[2] * next_two * ext_back[2:]
    )
    tap_part = jnp.stack(
        [
            jnp.sum(grad_here * extended[2:], axis=0),
            jnp.sum(grad_here * lag_one, axis=0),
            jnp.sum(grad_here * lag_two, axis=0),
        ]
    )
    grad_projected = jnp.stack(
        [grad_mixed * projected[2], grad_c, grad_mixed * projected[0]]
    ).astype(BF)
    grad_one_part = jnp.einsum("kte,kde->td", grad_projected, in_weight, preferred_element_type=F32)
    grad_one_own = lax.psum_scatter(
        grad_one_part.astype(BF), "chan", scatter_dimension=0, tiled=True
    ).astype(F32)
    gain_one_part = jnp.sum(grad_one_part * unit_all, axis=0)

    mix_slices = own_slices(grad_mix)
    gated_both = both_cores(gated_mix)
    half = gated_mix.shape[1] // 2
    out_parts = []
    for place, order in enumerate(orders):
        chans = gated_both[:, place * half : (place + 1) * half]
        out_parts.append(
            scattered(
                lambda s, u=chans: jnp.moveaxis(
                    jnp.einsum("te,t...d->e...d", u, s, preferred_element_type=F32), 0, -2
                ),
                ordered(mix_slices, order, bits),
                order,
            )
        )
    out_grad = jnp.concatenate(out_parts, axis=0)

    normed_one_slices = own_slices(normed_one)
    grad_both = jnp.concatenate([grad_projected, swapped(grad_projected, "seq", 1)], axis=1)
    half = chan_cols // 2
    in_parts = []
    for place, order in enumerate(orders):
        chans = grad_both[:, :, place * half : (place + 1) * half]
        in_parts.append(
            scattered(
                lambda s, u=chans: jnp.einsum("t...d,kte->...kde", s, u, preferred_element_type=F32),
                ordered(normed_one_slices, order, bits),
                order,
            )
        )
    in_grad = jnp.concatenate(in_parts, axis=2)

    own_start = chan_index * shard_rows
    unit_one = lax.dynamic_slice_in_dim(unit_all, own_start, shard_rows, 0)
    scale_one = lax.dynamic_slice_in_dim(scale_all, own_start, shard_rows, 0)
    input_grad = grad_state_own + norm_back(grad_one_own, unit_one, scale_one, gain_one)

    small = summed(
        jnp.concatenate([jnp.concatenate([gain_one_part, gain_two_part]), tap_part.reshape(-1)]),
        "seq",
    )
    width = gain_one.shape[0]
    gains_grad = summed(small[: 2 * width], "chan").reshape(2, width)
    conv_grad = small[2 * width :].reshape(3, chan_cols)
    return (
        block_output,
        input_grad,
        gains_grad,
        conv_grad,
        in_grad,
        out_grad,
        gate_up_grad,
        down_grad,
    )


def solution(mesh):
    placed = (
        P(("seq", "chan"), None),
        P(),
        P(None, "chan"),
        P(None, None, "chan"),
        P("chan", None),
        P(None, None, "chan"),
        P("chan", None),
        P(),
        P(("seq", "chan"), None),
    )
    return jax.shard_map(
        on_device,
        mesh=mesh,
        in_specs=placed,
        out_specs=(
            P(("seq", "chan"), None),
            P(("seq", "chan"), None),
            P(),
            P(None, "chan"),
            P(None, "seq", "chan"),
            P("chan", "seq"),
            P(None, "seq", "chan"),
            P("chan", "seq"),
        ),
        check_vma=False,
    )
```

```python
import functools

import jax
import jax.numpy as jnp
from jax import lax
from jax.experimental import pallas as pl
from jax.experimental.pallas import tpu as pltpu
from jax.sharding import PartitionSpec as P

EPS = 1e-05
BF = jnp.bfloat16
F32 = jnp.float32
MIB = 2**20
VMEM = 48


def params(mebibytes):
    return pltpu.CompilerParams(vmem_limit_bytes=mebibytes * MIB)


def cost():
    return pl.CostEstimate(flops=1024, bytes_accessed=1024, transcendentals=0)


def dot(a, b, dim_a, dim_b):
    return lax.dot_general(a, b, (((dim_a,), (dim_b,)), ((), ())), preferred_element_type=F32)


def after(value, *earlier):
    return lax.optimization_barrier((value,) + earlier)[0]


def passed_along(block, axis, distance):
    devices = range(lax.axis_size(axis))
    route = [(i - distance, i) for i in devices if i - distance in devices]
    return lax.ppermute(block, axis, route)


def turned(block, axis, distance):
    count = lax.axis_size(axis)
    return lax.ppermute(block, axis, [(i, (i + distance) % count) for i in range(count)])


def swapped(block, axis, bit):
    return lax.ppermute(block, axis, [(i, i ^ bit) for i in range(lax.axis_size(axis))])


def summed(block, axis, bit=1):
    while bit < lax.axis_size(axis):
        block = block + swapped(block, axis, bit)
        bit *= 2
    return block


def keep_masks(positions, starts):
    at_start = jnp.any(positions[..., None] == starts, axis=-1)
    prev_start = jnp.any((positions - 1)[..., None] == starts, axis=-1)
    keep_one = ((positions >= 1) & jnp.logical_not(at_start)).astype(F32)[..., None]
    keep_two = ((positions >= 2) & jnp.logical_not(at_start) & jnp.logical_not(prev_start)).astype(
        F32
    )[..., None]
    return (keep_one, keep_two)


def unit_rows(values):
    inv_scale = lax.rsqrt(jnp.mean(values * values, axis=-1, keepdims=True) + EPS)
    return (values * inv_scale, inv_scale)


def norm_back(grad_normed, unit_vals, inv_scale, gain_row):
    weighted = grad_normed * gain_row
    return inv_scale * (
        weighted - unit_vals * jnp.mean(weighted * unit_vals, axis=-1, keepdims=True)
    )


def group_bits():
    groups = lax.axis_size("seq") // 2
    bits = []
    while groups > 1:
        groups //= 2
        bits.append(groups)
    return bits


def ffn_body(count, joining, ids, *refs):
    normed = refs[:count]
    cots = refs[count : 2 * count]
    gate_up_w, down_w = refs[2 * count : 2 * count + 2]
    outs = refs[2 * count + 2 + joining :]
    hidden_ref, pair_ref = outs[:2]
    ffn_refs, grad_refs = outs[2 : 2 + count], outs[2 + count : 2 + 2 * count]
    normed_all, cot_all, ffn_acc, grad_acc = outs[2 + 2 * count :]
    step = pl.program_id(0)
    rows = normed[0].shape[0]

    @pl.when(step == 0)
    def _():
        for place in range(count):
            normed_all[pl.ds(place * rows, rows), :] = normed[place][...]
            cot_all[pl.ds(place * rows, rows), :] = cots[place][...]

    gate = dot(normed_all[...], gate_up_w[0], 1, 0)
    up = dot(normed_all[...], gate_up_w[1], 1, 0)
    grad_hidden = dot(cot_all[...], down_w[...], 1, 1)
    sig = jax.nn.sigmoid(gate)
    activated = gate * sig
    hidden = (activated * up).astype(BF)
    hidden_ref[0] = hidden
    grad_gate = (grad_hidden * up * sig * (1.0 + gate * (1.0 - sig))).astype(BF)
    grad_up = (grad_hidden * activated).astype(BF)
    pair_ref[0] = grad_gate
    pair_ref[1] = grad_up
    ffn_part = dot(hidden, down_w[...], 1, 0)
    grad_part = dot(grad_gate, gate_up_w[0], 1, 1) + dot(grad_up, gate_up_w[1], 1, 1)

    @pl.when(step == 0)
    def _():
        ffn_acc[...] = ffn_part
        grad_acc[...] = grad_part

    @pl.when(step > 0)
    def _():
        ffn_acc[...] += ffn_part
        grad_acc[...] += grad_part

    @pl.when(step == pl.num_programs(0) - 1)
    def _():
        for place in range(count):
            own = pl.ds(place * rows, rows)
            ffn_refs[place][...] = ffn_acc[own, :].astype(BF)
            grad_refs[place][...] = grad_acc[own, :].astype(BF)


def feed_forward(owner, normed, cots, gate_up_weight, down_weight, first, total, joined, tile=512):
    count = len(normed)
    rows, width = normed[0].shape
    units = down_weight.shape[0]
    here, all_rows = count * rows, total * rows
    place = first // count
    block = pl.BlockSpec((rows, width), lambda j, ids: (0, 0))
    anywhere = pl.BlockSpec(memory_space=pl.ANY)
    results = pl.pallas_call(
        functools.partial(ffn_body, count, len(joined)),
        grid_spec=pltpu.PrefetchScalarGridSpec(
            num_scalar_prefetch=1,
            grid=(units // tile,),
            in_specs=[block] * count
            + [
                pl.BlockSpec((rows, width), lambda j, ids, r=first + r: (ids[r], 0))
                for r in range(count)
            ]
            + [
                pl.BlockSpec((2, width, tile), lambda j, ids: (0, 0, j)),
                pl.BlockSpec((tile, width), lambda j, ids: (j, 0)),
            ]
            + [anywhere] * len(joined),
            out_specs=[
                pl.BlockSpec((1, here, tile), lambda j, ids: (0, place, j)),
                pl.BlockSpec((2, here, tile), lambda j, ids: (0, place, j)),
            ]
            + [block] * (2 * count),
            scratch_shapes=[
                pltpu.VMEM((here, width), BF),
                pltpu.VMEM((here, width), BF),
                pltpu.VMEM((here, width), F32),
                pltpu.VMEM((here, width), F32),
            ],
        ),
        out_shape=[
            jax.ShapeDtypeStruct((1, all_rows, units), BF),
            jax.ShapeDtypeStruct((2, all_rows, units), BF),
        ]
        + [jax.ShapeDtypeStruct((rows, width), BF)] * (2 * count),
        input_output_aliases={2 * count + 3 + k: k for k in range(len(joined))},
        compiler_params=params(VMEM),
        cost_estimate=cost(),
        name="feed_forward",
    )(owner, *normed, *([cots] * count), gate_up_weight, down_weight, *joined)
    return results[0], results[1], results[2 : 2 + count], results[2 + count :]


def slices_body(count, groups, part, apart, ids, *refs):
    ins, outs = refs[:-2], refs[-2:]
    rows = outs[0].shape[0] // count
    for r in range(count):
        here = pl.ds(r * rows, rows)
        if apart:
            source, there = ins[r], slice(None)
        else:
            source = ins[0]
            there = pl.ds(pl.multiple_of(ids[2 * groups + r] * rows, rows), rows)
        for half in range(2):
            for slot in range(groups):
                start = pl.multiple_of(ids[half * groups + slot] * part, part)
                outs[half][here, slot * part : (slot + 1) * part] = source[
                    there, pl.ds(start, part)
                ]


def own_slices(blocks, owner=None):
    seq = lax.axis_size("seq")
    groups = seq // 2
    place = lax.axis_index("seq")
    core, group = place % 2, place // 2
    chips = jnp.bitwise_xor(group, jnp.arange(groups, dtype=jnp.int32))
    mine, other = 2 * chips + core, 2 * chips + 1 - core
    apart = owner is None
    if apart:
        count = len(blocks)
        owner = jnp.zeros((count,), jnp.int32)
        rows = blocks[0].shape[0]
    else:
        count = owner.shape[0]
        rows = blocks.shape[0] // count
        blocks = [blocks]
    width = blocks[0].shape[1]
    part = width // seq
    if part % 128:
        if apart:
            full = jnp.concatenate(blocks, axis=0)
        else:
            full = jnp.concatenate(
                [
                    lax.dynamic_slice_in_dim(blocks[0], owner[r] * rows, rows, 0)
                    for r in range(count)
                ],
                axis=0,
            )
        full = full.reshape(count * rows, seq, part)
        picked = [
            jnp.take(full, ids, axis=1).reshape(count * rows, groups * part)
            for ids in (mine, other)
        ]
    else:
        ids = jnp.concatenate([mine, other, owner]).astype(jnp.int32)
        picked = pl.pallas_call(
            functools.partial(slices_body, count, groups, part, apart),
            in_specs=[pl.BlockSpec(memory_space=pltpu.SMEM)]
            + [pl.BlockSpec(memory_space=pltpu.VMEM)] * len(blocks),
            out_specs=[pl.BlockSpec(memory_space=pltpu.VMEM)] * 2,
            out_shape=[jax.ShapeDtypeStruct((count * rows, groups * part), BF)] * 2,
            compiler_params=params(VMEM),
            cost_estimate=cost(),
            name="own_slices",
        )(ids, *blocks)
    return picked[0], swapped(picked[1], "seq", 1)


def product_body(slots, part, tiles, tall, *refs):
    own, rec, units_own, units_rec = refs[:4]
    outs = refs[4:]
    step = pl.program_id(0)
    for half in range(2):

        @pl.when((step < tiles) if half == 0 else (step >= tiles))
        def _():
            for kind in range(2):
                out = outs[2 * half + kind]
                for place, slot in enumerate(slots[half][kind]):
                    columns = slice(slot * part, (slot + 1) * part)
                    if tall:
                        total = dot(units_own[0], own[:, columns], 0, 0) + dot(
                            units_rec[0], rec[:, columns], 0, 0
                        )
                    else:
                        total = dot(own[:, columns], units_own[0], 0, 0) + dot(
                            rec[:, columns], units_rec[0], 0, 0
                        )
                    out[place] = total.astype(BF)


class Joined:
    def __init__(self, lhs, units, orders, part, tall=False, piece=0, pieces=1):
        rows, slotted = lhs[0].shape
        groups = slotted // part
        kinds, _, wide = units[0].shape
        wide = wide // pieces
        tile = next(t for t in (512, 256, 128) if (kinds * wide // 2) % t == 0 and wide % t == 0)
        each = wide // tile
        tiles = kinds * each // 2
        slots = tuple(self.slots(order) for order in orders)
        whole = pl.BlockSpec((rows, slotted), lambda j: (0, 0))
        column = pl.BlockSpec((1, rows, tile), lambda j: (j // each, 0, piece * each + j % each))
        here = groups // 2
        shapes, specs = [], []
        for half in range(2):
            for kind in range(2):

                def at(j, half=half):
                    return (
                        jnp.minimum(j, tiles - 1) if half == 0 else jnp.maximum(j - tiles, 0)
                    )

                if tall:
                    shape, block = (here, tiles * tile, part), (here, tile, part)
                    specs.append(pl.BlockSpec(block, lambda j, at=at: (0, at(j), 0)))
                else:
                    shape, block = (here, part, tiles * tile), (here, part, tile)
                    specs.append(pl.BlockSpec(block, lambda j, at=at: (0, 0, at(j))))
                shapes.append(jax.ShapeDtypeStruct(shape, BF))
        outs = pl.pallas_call(
            functools.partial(product_body, slots, part, tiles, tall),
            grid=(2 * tiles,),
            in_specs=[whole, whole, column, column],
            out_specs=specs,
            out_shape=shapes,
            compiler_params=params(VMEM),
            cost_estimate=cost(),
            name="product",
        )(*lhs, *units)
        self.orders, self.tall = orders, tall
        self.sent = [outs[0], outs[2]]
        self.kept = [[outs[1]], [outs[3]]]
        self.made = outs[0]
        self.done = 0

    def slots(self, order):
        slots = [0]
        for bit in reversed(order):
            slots = slots + [slot + bit for slot in slots]
        half = len(slots) // 2
        return tuple(slots[half:]), tuple(slots[:half])

    def send(self, *earlier):
        self.arrived = []
        for half in range(2):
            bit = 2 * self.orders[half][self.done]
            sent = after(self.sent[half], *earlier) if earlier else self.sent[half]
            arrived = swapped(sent, "seq", bit)
            self.arrived.append(arrived)
            self.kept[half].append(arrived)
        self.done += 1

    def add(self, *earlier):
        kept = [list(arrays) for arrays in self.kept]
        if earlier:
            kept[0][0] = after(kept[0][0], *earlier)
        left = len(self.orders[0]) - self.done
        self.sent = upper_sums(kept, 2 ** (left - 1))
        self.made = self.sent[0]

    def finish(self, *earlier):
        while self.done < len(self.orders[0]):
            self.add(*earlier)
            self.send()
        kept = [list(arrays) for arrays in self.kept]
        if earlier:
            kept[0][0] = after(kept[0][0], *earlier)
        return kept


def sums_body(counts, tiles, *refs):
    ins, outs = refs[: sum(counts)], refs[sum(counts) :]
    step = pl.program_id(0)
    start = 0
    for source, count in enumerate(counts):
        arrays = ins[start : start + count]
        start += count
        out = outs[source] if len(outs) > 1 else outs[0]

        @pl.when(step // tiles == source)
        def _():
            total = arrays[0][...].astype(F32)
            for array in arrays[1:]:
                total = total + array[...].astype(F32)
            out[...] = total.reshape(out.shape).astype(out.dtype)


def source_tile(step, source, tiles):
    return jnp.clip(step - source * tiles, 0, tiles - 1)


def upper_sums(sources, here):
    _, rows, columns = sources[0][0].shape
    tiles = 2
    block = (here, rows // tiles, columns)
    in_specs, arrays = [], []
    for source, parts in enumerate(sources):
        for array in parts:
            in_specs.append(
                pl.BlockSpec(block, lambda j, s=source: (1, source_tile(j, s, tiles), 0))
            )
            arrays.append(array)
    return pl.pallas_call(
        functools.partial(sums_body, [len(parts) for parts in sources], tiles),
        grid=(len(sources) * tiles,),
        in_specs=in_specs,
        out_specs=[
            pl.BlockSpec(block, lambda j, s=source: (0, source_tile(j, s, tiles), 0))
            for source in range(len(sources))
        ],
        out_shape=[jax.ShapeDtypeStruct((here, rows, columns), BF)] * len(sources),
        compiler_params=params(VMEM),
        cost_estimate=cost(),
        name="upper_sums",
    )(*arrays)


def final_sums(sources, tall, shape):
    _, rows, columns = sources[0][0].shape
    if tall:
        tile = min(512, rows)
        tiles = rows // tile
        block, out_block = (1, tile, columns), (tile, columns)
        out_spec = pl.BlockSpec(out_block, lambda j: (j, 0))

        def at(j, s):
            return (0, source_tile(j, s, tiles), 0)
    else:
        tile = next(t for t in (512, 256, 128) if columns % t == 0 and shape[2] % t == 0)
        tiles = columns // tile
        each = shape[2] // tile
        block, out_block = (1, rows, tile), (1, rows, tile)
        out_spec = pl.BlockSpec(out_block, lambda j: (j // each, 0, j % each))

        def at(j, s):
            return (0, 0, source_tile(j, s, tiles))

    in_specs, arrays = [], []
    for source, parts in enumerate(sources):
        for array in parts:
            in_specs.append(pl.BlockSpec(block, lambda j, s=source: at(j, s)))
            arrays.append(array)
    return pl.pallas_call(
        functools.partial(sums_body, [len(parts) for parts in sources], tiles),
        grid=(len(sources) * tiles,),
        in_specs=in_specs,
        out_specs=out_spec,
        out_shape=jax.ShapeDtypeStruct(shape, F32),
        compiler_params=params(VMEM),
        cost_estimate=cost(),
        name="final_sums",
    )(*arrays)


def ring_body(a, b, out):
    out[...] = (a[...].astype(F32) + b[...].astype(F32)).astype(BF)


def ring_sum(arrived, own):
    rows, width = own.shape
    spec = pl.BlockSpec((rows // 2, width), lambda j: (j, 0))
    return pl.pallas_call(
        ring_body,
        grid=(2,),
        in_specs=[spec, spec],
        out_specs=spec,
        out_shape=jax.ShapeDtypeStruct((rows, width), BF),
        compiler_params=params(VMEM),
        cost_estimate=cost(),
        name="ring_sum",
    )(arrived, own)


def back_body(count, *refs):
    grads, weights = refs[:2]
    toks = refs[2 : 2 + count]
    scale_ref = refs[2 + count]
    outs = refs[3 + count : 3 + 2 * count]
    gains_ref = refs[3 + 2 * count]
    rows = toks[0].shape[0]
    total = dot(grads[0], weights[0], 1, 1)
    for kind in range(1, grads.shape[0]):
        total = total + dot(grads[kind], weights[kind], 1, 1)
    gains = None
    for place in range(count):
        here = total[place * rows : (place + 1) * rows]
        outs[place][...] = here.astype(BF)
        unit = toks[place][...].astype(F32) * scale_ref[pl.ds(place * rows, rows), :]
        part = jnp.sum(here * unit, axis=0, keepdims=True)
        gains = part if gains is None else gains + part
    gains_ref[...] = gains


def mixer_back(grads, weights, toks, scale, tile=512):
    kinds, all_rows, chans = grads.shape
    width = weights.shape[1]
    count = len(toks)
    rows = all_rows // count
    block = pl.BlockSpec((rows, tile), lambda j: (0, j))
    results = pl.pallas_call(
        functools.partial(back_body, count),
        grid=(width // tile,),
        in_specs=[
            pl.BlockSpec((kinds, all_rows, chans), lambda j: (0, 0, 0)),
            pl.BlockSpec((kinds, tile, chans), lambda j: (0, j, 0)),
        ]
        + [block] * count
        + [pl.BlockSpec((all_rows, 1), lambda j: (0, 0))],
        out_specs=[block] * count + [pl.BlockSpec((1, tile), lambda j: (0, j))],
        out_shape=[jax.ShapeDtypeStruct((rows, width), BF)] * count
        + [jax.ShapeDtypeStruct((1, width), F32)],
        compiler_params=params(VMEM),
        cost_estimate=cost(),
        name="mixer_back",
    )(grads, weights, *toks, scale)
    return results[:count], results[count][0]


def full_others(others):
    seq = lax.axis_size("seq")
    stacked = jnp.stack(others, axis=1)
    stacked = stacked.reshape((seq,) + stacked.shape[2:])
    slots = jnp.bitwise_xor(lax.axis_index("seq"), jnp.arange(seq, dtype=jnp.int32))
    full = jnp.transpose(jnp.take(stacked, slots, axis=0), (1, 2, 0, 3))
    return full.reshape(full.shape[:2] + (-1,))


def plane_ids():
    place = lax.axis_index("seq")
    groups = lax.axis_size("seq") // 2
    chips = jnp.bitwise_xor(place // 2, jnp.arange(groups, dtype=jnp.int32))
    return jnp.concatenate([chips, (place % 2)[None]]).astype(jnp.int32)


def core_columns(ids, groups, kind, part, base=0):
    core = ids[groups]
    offset = jnp.where(core == kind, 0, part)
    return pl.ds(pl.multiple_of(base + offset, part), part)


def mixer_body(count, ids, *refs):
    gated = refs[:count]
    own_w, same_w, cross_w, rows_ref, gain_ref, state_ref, normed_ref, scale_ref = refs[count:]
    step = pl.program_id(0)
    part = same_w.shape[3]
    groups = pl.num_programs(0)
    base = pl.multiple_of(step * 2 * part, 2 * part)
    for kind, other_w in enumerate((same_w, cross_w)):
        inner = core_columns(ids, groups, kind, part)
        total = dot(gated[0][...], own_w[:, inner], 1, 0)
        for place in range(1, count):
            total = total + dot(gated[place][...], other_w[0, count - 1 - place], 1, 0)
        columns = core_columns(ids, groups, kind, part, base)
        state_ref[:, columns] = total + rows_ref[:, columns].astype(F32)

    @pl.when(step == groups - 1)
    def _():
        state = state_ref[...]
        scale = lax.rsqrt(jnp.mean(state * state, axis=-1, keepdims=True) + EPS)
        normed_ref[...] = (state * scale * gain_ref[...]).astype(BF)
        scale_ref[...] = scale


def mixer_rows(gated, own_w, others, input_rows, gain):
    count = len(gated)
    rows, width = input_rows.shape
    chans = gated[0].shape[1]
    groups, _, _, part = others[0].shape
    if part % 128:
        full = full_others(others)
        total = dot(gated[0], own_w, 1, 0)
        for r in range(1, count):
            total = total + dot(gated[r], full[count - 1 - r], 1, 0)
        state = input_rows.astype(F32) + total
        unit, scale = unit_rows(state)
        return state, (unit * gain).astype(BF), scale
    full_rows = pl.BlockSpec((rows, width), lambda t, ids: (0, 0))
    weights = pl.BlockSpec((1, count - 1, chans, part), lambda t, ids: (ids[t], 0, 0, 0))
    return pl.pallas_call(
        functools.partial(mixer_body, count),
        grid_spec=pltpu.PrefetchScalarGridSpec(
            num_scalar_prefetch=1,
            grid=(groups,),
            in_specs=[pl.BlockSpec((rows, chans), lambda t, ids: (0, 0))] * count
            + [
                pl.BlockSpec((chans, 2 * part), lambda t, ids: (0, t)),
                weights,
                weights,
                full_rows,
                pl.BlockSpec((1, width), lambda t, ids: (0, 0)),
            ],
            out_specs=[full_rows, full_rows, pl.BlockSpec((rows, 1), lambda t, ids: (0, 0))],
        ),
        out_shape=[
            jax.ShapeDtypeStruct((rows, width), F32),
            jax.ShapeDtypeStruct((rows, width), BF),
            jax.ShapeDtypeStruct((rows, 1), F32),
        ],
        compiler_params=params(VMEM),
        cost_estimate=cost(),
        name="mixer_rows",
    )(plane_ids(), *gated, own_w, *others, input_rows, gain.reshape(1, width))


def gated_body(count, ids, *refs):
    own_w, same_w, cross_w, arrived, part_own, state_ref, scale_ref, cot_ref, gain_ref = refs[:9]
    outs = refs[9 : 9 + count]
    grad_ref, mix_ref, gains_ref = refs[9 + count : 12 + count]
    accs = refs[12 + count :]
    step = pl.program_id(0)
    part = same_w.shape[3]
    groups = pl.num_programs(0)

    @pl.when(step == 0)
    def _():
        grad_normed = arrived[...].astype(F32) + part_own[...].astype(F32)
        unit = state_ref[...] * scale_ref[...]
        weighted = grad_normed * gain_ref[...]
        grad = cot_ref[...].astype(F32) + scale_ref[...] * (
            weighted - unit * jnp.mean(weighted * unit, axis=-1, keepdims=True)
        )
        grad_ref[...] = grad
        mix_ref[...] = grad.astype(BF)
        gains_ref[...] = jnp.sum(grad_normed * unit, axis=0, keepdims=True)
        for acc in accs:
            acc[...] = jnp.zeros_like(acc)

    base = pl.multiple_of(step * 2 * part, 2 * part)
    mix = [
        mix_ref[:, core_columns(ids, groups, kind, part, base)] for kind in range(2)
    ]
    accs[0][...] += dot(mix_ref[:, pl.ds(base, 2 * part)], own_w[...], 1, 1)
    for place in range(1, count):
        accs[place][...] += dot(mix[0], same_w[0, count - 1 - place], 1, 1) + dot(
            mix[1], cross_w[0, count - 1 - place], 1, 1
        )

    @pl.when(step == groups - 1)
    def _():
        for out, acc in zip(outs, accs):
            out[...] = acc[...].astype(BF)


def gated_rows(arrived, part_own, state, scale, cot, gain, own_w, others):
    rows, width = state.shape
    chans = own_w.shape[0]
    groups, less, _, part = others[0].shape
    count = less + 1
    if part % 128:
        full = full_others(others)
        grad_normed = arrived.astype(F32) + part_own.astype(F32)
        unit = state * scale
        grad = cot.astype(F32) + norm_back(grad_normed, unit, scale, gain)
        mix = grad.astype(BF)
        outs = [dot(mix, own_w, 1, 1).astype(BF)] + [
            dot(mix, full[count - 1 - r], 1, 1).astype(BF) for r in range(1, count)
        ]
        return outs, grad, mix, jnp.sum(grad_normed * unit, axis=0)
    full_rows = pl.BlockSpec((rows, width), lambda t, ids: (0, 0))
    one_row = pl.BlockSpec((1, width), lambda t, ids: (0, 0))
    weights = pl.BlockSpec((1, less, chans, part), lambda t, ids: (ids[t], 0, 0, 0))
    results = pl.pallas_call(
        functools.partial(gated_body, count),
        grid_spec=pltpu.PrefetchScalarGridSpec(
            num_scalar_prefetch=1,
            grid=(groups,),
            in_specs=[
                pl.BlockSpec((chans, 2 * part), lambda t, ids: (0, t)),
                weights,
                weights,
                full_rows,
                full_rows,
                full_rows,
                pl.BlockSpec((rows, 1), lambda t, ids: (0, 0)),
                full_rows,
                one_row,
            ],
            out_specs=[pl.BlockSpec((rows, chans), lambda t, ids: (0, 0))] * count
            + [full_rows, full_rows, one_row],
            scratch_shapes=[pltpu.VMEM((rows, chans), F32)] * count,
        ),
        out_shape=[jax.ShapeDtypeStruct((rows, chans), BF)] * count
        + [
            jax.ShapeDtypeStruct((rows, width), F32),
            jax.ShapeDtypeStruct((rows, width), BF),
            jax.ShapeDtypeStruct((1, width), F32),
        ],
        compiler_params=params(VMEM),
        cost_estimate=cost(),
        name="gated_rows",
    )(plane_ids(), own_w, *others, arrived, part_own, state, scale, cot, gain.reshape(1, width))
    return results[:count], results[count], results[count + 1], results[count + 2][0]


def on_device(
    tokens,
    norm_gains,
    conv_weight,
    in_weight,
    out_weight,
    gate_up_weight,
    down_weight,
    starts,
    cotangent,
):
    shard_rows, width = tokens.shape
    chan_count = lax.axis_size("chan")
    seq_count = lax.axis_size("seq")
    seq_rows = shard_rows * chan_count
    chan_cols = conv_weight.shape[1]
    chan_index = lax.axis_index("chan")
    seq_index = lax.axis_index("seq")
    relative = jnp.arange(chan_count, dtype=jnp.int32)
    owner = (chan_index - relative) % chan_count
    positions = (
        seq_index * seq_rows
        + owner[:, None] * shard_rows
        + jnp.arange(shard_rows, dtype=jnp.int32)[None, :]
    )
    keep_one, keep_two = keep_masks(positions, starts)
    next_one, unused_one = keep_masks(positions + 1, starts)
    unused_two, next_two = keep_masks(positions + 2, starts)
    gain_one = norm_gains[0].astype(F32)
    gain_two = norm_gains[1].astype(F32)
    conv_taps = conv_weight.astype(F32)
    bits = group_bits()
    orders = (bits[::-1], bits)

    part = width // seq_count
    w_own = lax.dynamic_slice_in_dim(out_weight, seq_index * part, part, 1)
    w_one = turned(w_own, "chan", 1)
    w_three = turned(w_own, "chan", 3)
    tok_one = turned(tokens, "chan", 1)
    tok_three = turned(tokens, "chan", 3)
    w_two = turned(w_one, "chan", 1)
    tok_two = turned(after(tok_one, w_three), "chan", 1)
    others = jnp.stack([w_one, w_two, w_three])[None]
    halves = [others[:, :, : chan_cols // 2], others[:, :, chan_cols // 2 :]]
    for place, order in enumerate(orders):
        held = halves[place]
        for bit in order:
            held = jnp.concatenate([held, swapped(held, "seq", 2 * bit)], axis=0)
        split = held.reshape((2,) * len(order) + held.shape[1:])
        axes = [len(order) - 1 - order.index(bit) for bit in bits]
        held = jnp.transpose(split, (*axes, *range(len(order), split.ndim))).reshape(held.shape)
        halves[place] = held
    held = jnp.concatenate(halves, axis=2)
    others = (held, swapped(held, "seq", 1))

    tok_blocks = [tokens, tok_one, tok_two, tok_three]
    inputs_all = jnp.concatenate(tok_blocks, axis=0).astype(F32)
    unit_all, scale_all = unit_rows(inputs_all)
    normed_one = (unit_all * gain_one).astype(BF)
    projected = jnp.einsum("td,kde->kte", normed_one, in_weight, preferred_element_type=F32)
    projected = projected.reshape(3, chan_count, shard_rows, chan_cols)

    grad_out = lax.all_gather(after(cotangent, tok_two, tok_three), "chan", axis=0, tiled=True)

    def at_edge(edge_rows, device):
        return lax.dynamic_index_in_dim(edge_rows, (chan_index - device) % chan_count, 0, False)

    def is_owner(device):
        return (owner == device)[:, None, None]

    mixed_in = (projected[0] * projected[2]).astype(BF)
    ends = mixed_in[:, shard_rows - 2 :]
    rim_rows = passed_along(at_edge(ends, chan_count - 1), "seq", 1)
    before = jnp.where(is_owner(0), rim_rows[None], jnp.roll(ends, -1, axis=0))
    extended = jnp.concatenate([before, mixed_in], axis=1).astype(F32)
    lag_one = keep_one * extended[:, 1 : shard_rows + 1]
    lag_two = keep_two * extended[:, 0:shard_rows]
    conv_out = conv_taps[0] * extended[:, 2:] + conv_taps[1] * lag_one + conv_taps[2] * lag_two
    gated_mix = (projected[1] * conv_out).astype(BF)

    gated_rows_own = [gated_mix[0]] + [
        turned(gated_mix[r], "chan", -r) for r in range(1, chan_count)
    ]
    state_own, normed_two_own, scale_two = mixer_rows(
        gated_rows_own, out_weight, others, tokens, gain_two
    )
    n_one = turned(normed_two_own, "chan", 1)
    normed_one_slices = own_slices(
        [
            after(normed_one[r * shard_rows : (r + 1) * shard_rows], normed_two_own)
            for r in range(chan_count)
        ]
    )
    n_two = turned(n_one, "chan", 1)
    n_three = turned(after(normed_two_own, n_one), "chan", 3)
    hidden, grad_pair, ffn_parts, grad_two_parts = feed_forward(
        owner,
        [after(normed_two_own, normed_one_slices[0]), n_one],
        grad_out,
        gate_up_weight,
        down_weight,
        0,
        chan_count,
        (),
    )
    cot_slices = own_slices(after(grad_out, hidden), owner)
    run = turned(grad_two_parts[1], "chan", 1)
    hidden, grad_pair, ffn_more, grad_more = feed_forward(
        owner,
        [after(n_two, cot_slices[0]), n_three],
        grad_out,
        gate_up_weight,
        down_weight,
        2,
        chan_count,
        (hidden, grad_pair),
    )
    ffn_parts = list(ffn_parts) + list(ffn_more)
    grad_two_parts = list(grad_two_parts) + list(grad_more)

    total = ring_sum(run, grad_two_parts[2])
    hidden_rec = swapped(after(hidden, total), "seq", 1)
    pair_rec = swapped(after(grad_pair, total), "seq", 1)
    run = turned(total, "chan", 1)
    normed_two_slices = own_slices([normed_two_own, n_one, n_two, after(n_three, total)])
    down = Joined(
        (after(cot_slices[0], normed_two_slices[0]), cot_slices[1]),
        (hidden, hidden_rec),
        orders,
        part,
        tall=True,
    )
    down.send()
    total = ring_sum(after(run, down.made), grad_two_parts[3])
    run = turned(total, "chan", 1)
    gate_up_a = Joined(
        (after(normed_two_slices[0], total), normed_two_slices[1]),
        (grad_pair, pair_rec),
        orders,
        part,
        False,
        0,
        2,
    )
    gate_up_a.send()
    run = after(run, gate_up_a.made, *down.arrived)

    grad_gated_rows, grad_state_own, grad_mix_own, gain_two_part = gated_rows(
        run,
        grad_two_parts[0],
        state_own,
        scale_two,
        cotangent,
        gain_two,
        out_weight,
        others,
    )
    gg = [grad_gated_rows[0]] + [
        turned(grad_gated_rows[r], "chan", r) for r in range(1, chan_count)
    ]
    grad_mix = lax.all_gather(after(grad_mix_own, *gg), "chan", axis=0, tiled=True)
    ffn_run = turned(after(ffn_parts[1], *gg), "chan", 1)
    grad_gated = jnp.stack(gg).astype(F32)

    grad_conv = (grad_gated * projected[1]).astype(BF)
    grad_c = grad_gated * conv_out
    heads = after(grad_conv[:, :2], *gate_up_a.arrived)
    rim_back = passed_along(at_edge(heads, 0), "seq", -1)
    behind = jnp.where(is_owner(chan_count - 1), rim_back[None], jnp.roll(heads, 1, axis=0))
    ext_back = jnp.concatenate([grad_conv, behind], axis=1).astype(F32)
    grad_here = ext_back[:, :shard_rows]
    grad_mixed = (
        conv_taps[0] * grad_here
        + conv_taps[1] * next_one * ext_back[:, 1 : shard_rows + 1]
        + conv_taps[2] * next_two * ext_back[:, 2:]
    )
    tap_part = jnp.stack(
        [
            jnp.sum(grad_here * extended[:, 2:], axis=(0, 1)),
            jnp.sum(grad_here * lag_one, axis=(0, 1)),
            jnp.sum(grad_here * lag_two, axis=(0, 1)),
        ]
    )
    grad_triple = jnp.stack(
        [
            v.astype(BF).reshape(seq_rows, chan_cols)
            for v in (grad_mixed * projected[2], grad_c, grad_mixed * projected[0])
        ]
    )
    grad_one_parts, gain_one_part = mixer_back(grad_triple, in_weight, tok_blocks, scale_all)
    run = turned(grad_one_parts[1], "chan", 1)
    triple_rec = swapped(after(grad_triple, grad_one_parts[1]), "seq", 1)
    small = jnp.concatenate([gain_one_part, gain_two_part, tap_part.reshape(-1)])
    small_rec = swapped(small, "seq", 1)
    gate_up_b = Joined(
        (after(normed_two_slices[0], grad_one_parts[1], small), normed_two_slices[1]),
        (grad_pair, pair_rec),
        orders,
        part,
        False,
        1,
        2,
    )
    small = small + after(small_rec, gate_up_b.made)
    small_rec = swapped(small, "seq", 2)
    down.add(small)
    small = summed(small + after(small_rec, down.made), "seq", 4)
    gate_up_b.send(small)
    down.send(small)
    total = ring_sum(after(run, small), grad_one_parts[2])
    run = turned(total, "chan", 1)
    into = Joined(
        (after(normed_one_slices[0], total), normed_one_slices[1]),
        (grad_triple, triple_rec),
        orders,
        part,
    )
    gate_up_a.add(into.made)
    into.send(gate_up_a.made)
    gate_up_a.send()
    total = ring_sum(after(run, gate_up_a.made), grad_one_parts[3])
    run = turned(total, "chan", 1)
    mix_slices = own_slices(after(grad_mix, total), owner)
    gated_all = gated_mix.reshape(1, seq_rows, chan_cols)
    outward = Joined(
        mix_slices, (gated_all, swapped(gated_all, "seq", 1)), orders, part, tall=True
    )
    outward.send()
    small_rec = swapped(after(small[: 2 * width], outward.made), "chan", 1)
    gate_up_b.add(outward.made)
    gate_up_b.send()
    run = after(run, gate_up_b.made)
    ffn_sum = ring_sum(after(ffn_run, gate_up_b.made), ffn_parts[2])
    ffn_run = turned(ffn_sum, "chan", 1)
    down_grad = final_sums(down.finish(ffn_sum), True, (hidden.shape[2], part))
    into.add(down_grad)
    into.send()
    gains = small[: 2 * width] + after(small_rec, into.made)
    small_rec = swapped(gains, "chan", 2)
    ffn_sum = ring_sum(after(ffn_run, into.made), ffn_parts[3])
    ffn_run = turned(ffn_sum, "chan", 1)
    first, third = gate_up_a.finish(ffn_sum)
    second, fourth = gate_up_b.finish()
    gate_up_grad = final_sums(
        [first, second, third, fourth], False, (2, part, hidden.shape[2])
    )
    outward.add(gate_up_grad)
    outward.send()
    gains = gains + after(small_rec, outward.made)
    in_grad = final_sums(into.finish(outward.made), False, (3, part, chan_cols))
    out_grad = final_sums(outward.finish(in_grad), True, (chan_cols, part))

    grad_one_own = run.astype(F32) + grad_one_parts[0].astype(F32)
    input_grad = grad_state_own + norm_back(
        grad_one_own, unit_all[:shard_rows], scale_all[:shard_rows], gain_one
    )
    block_output = (state_own + (ffn_run.astype(F32) + ffn_parts[0].astype(F32))).astype(BF)
    gains_grad = gains.reshape(2, width)
    conv_grad = small[2 * width :].reshape(3, chan_cols)
    return (
        block_output,
        input_grad,
        gains_grad,
        conv_grad,
        in_grad,
        out_grad,
        gate_up_grad,
        down_grad,
    )


def solution(mesh):
    placed = (
        P(("seq", "chan"), None),
        P(),
        P(None, "chan"),
        P(None, None, "chan"),
        P("chan", None),
        P(None, None, "chan"),
        P("chan", None),
        P(),
        P(("seq", "chan"), None),
    )
    return jax.shard_map(
        on_device,
        mesh=mesh,
        in_specs=placed,
        out_specs=(
            P(("seq", "chan"), None),
            P(("seq", "chan"), None),
            P(),
            P(None, "chan"),
            P(None, "seq", "chan"),
            P("chan", "seq"),
            P(None, "seq", "chan"),
            P("chan", "seq"),
        ),
        check_vma=False,
    )
```

```python
import functools

import jax
import jax.numpy as jnp
from jax import lax
from jax.experimental import pallas as pl
from jax.experimental.pallas import tpu as pltpu
from jax.sharding import PartitionSpec as P

EPS = 1e-05
BF = jnp.bfloat16
F32 = jnp.float32
MIB = 2**20
VMEM = 48


def params(mebibytes):
    return pltpu.CompilerParams(vmem_limit_bytes=mebibytes * MIB)


def cost():
    return pl.CostEstimate(flops=1024, bytes_accessed=1024, transcendentals=0)


def dot(a, b, dim_a, dim_b):
    return lax.dot_general(a, b, (((dim_a,), (dim_b,)), ((), ())), preferred_element_type=F32)


def after(value, *earlier):
    return lax.optimization_barrier((value,) + earlier)[0]


def passed_along(block, axis, distance):
    devices = range(lax.axis_size(axis))
    route = [(i - distance, i) for i in devices if i - distance in devices]
    return lax.ppermute(block, axis, route)


def turned(block, axis, distance):
    count = lax.axis_size(axis)
    return lax.ppermute(block, axis, [(i, (i + distance) % count) for i in range(count)])


def swapped(block, axis, bit):
    return lax.ppermute(block, axis, [(i, i ^ bit) for i in range(lax.axis_size(axis))])


def summed(block, axis, bit=1):
    while bit < lax.axis_size(axis):
        block = block + swapped(block, axis, bit)
        bit *= 2
    return block


def keep_masks(positions, starts):
    at_start = jnp.any(positions[..., None] == starts, axis=-1)
    prev_start = jnp.any((positions - 1)[..., None] == starts, axis=-1)
    keep_one = ((positions >= 1) & jnp.logical_not(at_start)).astype(F32)[..., None]
    keep_two = ((positions >= 2) & jnp.logical_not(at_start) & jnp.logical_not(prev_start)).astype(
        F32
    )[..., None]
    return (keep_one, keep_two)


def unit_rows(values):
    inv_scale = lax.rsqrt(jnp.mean(values * values, axis=-1, keepdims=True) + EPS)
    return (values * inv_scale, inv_scale)


def norm_back(grad_normed, unit_vals, inv_scale, gain_row):
    weighted = grad_normed * gain_row
    return inv_scale * (
        weighted - unit_vals * jnp.mean(weighted * unit_vals, axis=-1, keepdims=True)
    )


def group_bits():
    groups = lax.axis_size("seq") // 2
    bits = []
    while groups > 1:
        groups //= 2
        bits.append(groups)
    return bits


def ffn_body(count, ids, *refs):
    normed = refs[:count]
    cots = refs[count : 2 * count]
    gate_up_w, down_w = refs[2 * count : 2 * count + 2]
    outs = refs[2 * count + 2 :]
    hidden_ref, pair_ref = outs[:2]
    ffn_refs, grad_refs = outs[2 : 2 + count], outs[2 + count : 2 + 2 * count]
    normed_all, cot_all, ffn_acc, grad_acc = outs[2 + 2 * count :]
    step = pl.program_id(0)
    rows = normed[0].shape[0]

    @pl.when(step == 0)
    def _():
        for place in range(count):
            normed_all[pl.ds(place * rows, rows), :] = normed[place][...]
            cot_all[pl.ds(place * rows, rows), :] = cots[place][...]

    gate = dot(normed_all[...], gate_up_w[0], 1, 0)
    up = dot(normed_all[...], gate_up_w[1], 1, 0)
    grad_hidden = dot(cot_all[...], down_w[...], 1, 1)
    sig = jax.nn.sigmoid(gate)
    activated = gate * sig
    hidden = (activated * up).astype(BF)
    hidden_ref[0] = hidden
    grad_gate = (grad_hidden * up * sig * (1.0 + gate * (1.0 - sig))).astype(BF)
    grad_up = (grad_hidden * activated).astype(BF)
    pair_ref[0] = grad_gate
    pair_ref[1] = grad_up
    ffn_part = dot(hidden, down_w[...], 1, 0)
    grad_part = dot(grad_gate, gate_up_w[0], 1, 1) + dot(grad_up, gate_up_w[1], 1, 1)

    @pl.when(step == 0)
    def _():
        ffn_acc[...] = ffn_part
        grad_acc[...] = grad_part

    @pl.when(step > 0)
    def _():
        ffn_acc[...] += ffn_part
        grad_acc[...] += grad_part

    @pl.when(step == pl.num_programs(0) - 1)
    def _():
        for place in range(count):
            own = pl.ds(place * rows, rows)
            ffn_refs[place][...] = ffn_acc[own, :].astype(BF)
            grad_refs[place][...] = grad_acc[own, :].astype(BF)


def feed_forward(owner, normed, cots, gate_up_weight, down_weight, first, tile=512):
    count = len(normed)
    rows, width = normed[0].shape
    units = down_weight.shape[0]
    here = count * rows
    block = pl.BlockSpec((rows, width), lambda j, ids: (0, 0))
    results = pl.pallas_call(
        functools.partial(ffn_body, count),
        grid_spec=pltpu.PrefetchScalarGridSpec(
            num_scalar_prefetch=1,
            grid=(units // tile,),
            in_specs=[block] * count
            + [
                pl.BlockSpec((rows, width), lambda j, ids, r=first + r: (ids[r], 0))
                for r in range(count)
            ]
            + [
                pl.BlockSpec((2, width, tile), lambda j, ids: (0, 0, j)),
                pl.BlockSpec((tile, width), lambda j, ids: (j, 0)),
            ],
            out_specs=[
                pl.BlockSpec((1, here, tile), lambda j, ids: (0, 0, j)),
                pl.BlockSpec((2, here, tile), lambda j, ids: (0, 0, j)),
            ]
            + [block] * (2 * count),
            scratch_shapes=[
                pltpu.VMEM((here, width), BF),
                pltpu.VMEM((here, width), BF),
                pltpu.VMEM((here, width), F32),
                pltpu.VMEM((here, width), F32),
            ],
        ),
        out_shape=[
            jax.ShapeDtypeStruct((1, here, units), BF),
            jax.ShapeDtypeStruct((2, here, units), BF),
        ]
        + [jax.ShapeDtypeStruct((rows, width), BF)] * (2 * count),
        compiler_params=params(VMEM),
        cost_estimate=cost(),
        name="feed_forward",
    )(owner, *normed, *([cots] * count), gate_up_weight, down_weight)
    return results[0], results[1], results[2 : 2 + count], results[2 + count :]


def slices_body(count, groups, part, apart, ids, *refs):
    ins, outs = refs[:-2], refs[-2:]
    rows = outs[0].shape[0] // count
    for r in range(count):
        here = pl.ds(r * rows, rows)
        if apart:
            source, there = ins[r], slice(None)
        else:
            source = ins[0]
            there = pl.ds(pl.multiple_of(ids[2 * groups + r] * rows, rows), rows)
        for half in range(2):
            for slot in range(groups):
                start = pl.multiple_of(ids[half * groups + slot] * part, part)
                outs[half][here, slot * part : (slot + 1) * part] = source[
                    there, pl.ds(start, part)
                ]


def own_slices(blocks, owner=None, relative=True):
    seq = lax.axis_size("seq")
    groups = seq // 2
    place = lax.axis_index("seq")
    core, group = place % 2, place // 2
    chips = jnp.arange(groups, dtype=jnp.int32)
    if relative:
        chips = jnp.bitwise_xor(group, chips)
    mine, other = 2 * chips + core, 2 * chips + 1 - core
    apart = owner is None
    if apart:
        count = len(blocks)
        owner = jnp.zeros((count,), jnp.int32)
        rows = blocks[0].shape[0]
    else:
        count = owner.shape[0]
        rows = blocks.shape[0] // count
        blocks = [blocks]
    width = blocks[0].shape[1]
    part = width // seq
    if part % 128:
        if apart:
            full = jnp.concatenate(blocks, axis=0)
        else:
            full = jnp.concatenate(
                [
                    lax.dynamic_slice_in_dim(blocks[0], owner[r] * rows, rows, 0)
                    for r in range(count)
                ],
                axis=0,
            )
        full = full.reshape(count * rows, seq, part)
        picked = [
            jnp.take(full, ids, axis=1).reshape(count * rows, groups * part)
            for ids in (mine, other)
        ]
    else:
        ids = jnp.concatenate([mine, other, owner]).astype(jnp.int32)
        picked = pl.pallas_call(
            functools.partial(slices_body, count, groups, part, apart),
            in_specs=[pl.BlockSpec(memory_space=pltpu.SMEM)]
            + [pl.BlockSpec(memory_space=pltpu.VMEM)] * len(blocks),
            out_specs=[pl.BlockSpec(memory_space=pltpu.VMEM)] * 2,
            out_shape=[jax.ShapeDtypeStruct((count * rows, groups * part), BF)] * 2,
            compiler_params=params(VMEM),
            cost_estimate=cost(),
            name="own_slices",
        )(ids, *blocks)
    return picked[0], swapped(picked[1], "seq", 1)


def rows_dot(lhs, columns, units, swap):
    total, start = None, 0
    for piece in units:
        here = lhs[start : start + piece.shape[1], columns]
        start += piece.shape[1]
        part = dot(piece[0], here, 0, 0) if swap else dot(here, piece[0], 0, 0)
        total = part if total is None else total + part
    return total


def product_body(slots, part, tiles, tall, pieces, *refs):
    own, rec = refs[:2]
    units_own, units_rec = refs[2 : 2 + pieces], refs[2 + pieces : 2 + 2 * pieces]
    outs = refs[2 + 2 * pieces :]
    step = pl.program_id(0)
    for half in range(2):

        @pl.when((step < tiles) if half == 0 else (step >= tiles))
        def _():
            for kind in range(2):
                out = outs[2 * half + kind]
                for place, slot in enumerate(slots[half][kind]):
                    columns = slice(slot * part, (slot + 1) * part)
                    out[place] = (
                        rows_dot(own, columns, units_own, tall)
                        + rows_dot(rec, columns, units_rec, tall)
                    ).astype(BF)


class Joined:
    def __init__(self, lhs, units, orders, part, tall=False):
        rows, slotted = lhs[0].shape
        groups = slotted // part
        kinds, _, wide = units[0][0].shape
        tile = next(t for t in (512, 256, 128) if (kinds * wide // 2) % t == 0 and wide % t == 0)
        each = wide // tile
        tiles = kinds * each // 2
        slots = tuple(self.slots(order) for order in orders)
        whole = pl.BlockSpec((rows, slotted), lambda j: (0, 0))
        columns = [
            pl.BlockSpec((1, piece.shape[1], tile), lambda j: (j // each, 0, j % each))
            for piece in (*units[0], *units[1])
        ]
        here = groups // 2
        shapes, specs = [], []
        for half in range(2):
            for kind in range(2):

                def at(j, half=half):
                    return (
                        jnp.minimum(j, tiles - 1) if half == 0 else jnp.maximum(j - tiles, 0)
                    )

                if tall:
                    shape, block = (here, tiles * tile, part), (here, tile, part)
                    specs.append(pl.BlockSpec(block, lambda j, at=at: (0, at(j), 0)))
                else:
                    shape, block = (here, part, tiles * tile), (here, part, tile)
                    specs.append(pl.BlockSpec(block, lambda j, at=at: (0, 0, at(j))))
                shapes.append(jax.ShapeDtypeStruct(shape, BF))
        outs = pl.pallas_call(
            functools.partial(product_body, slots, part, tiles, tall, len(units[0])),
            grid=(2 * tiles,),
            in_specs=[whole, whole, *columns],
            out_specs=specs,
            out_shape=shapes,
            compiler_params=params(58),
            cost_estimate=cost(),
            name="product",
        )(*lhs, *units[0], *units[1])
        self.orders, self.tall = orders, tall
        self.sent = [outs[0], outs[2]]
        self.kept = [[outs[1]], [outs[3]]]
        self.made = outs[0]
        self.done = 0

    def slots(self, order):
        slots = [0]
        for bit in reversed(order):
            slots = slots + [slot + bit for slot in slots]
        half = len(slots) // 2
        return tuple(slots[half:]), tuple(slots[:half])

    def send(self, *earlier):
        self.arrived = []
        for half in range(2):
            bit = 2 * self.orders[half][self.done]
            sent = after(self.sent[half], *earlier) if earlier else self.sent[half]
            arrived = swapped(sent, "seq", bit)
            self.arrived.append(arrived)
            self.kept[half].append(arrived)
        self.done += 1

    def add(self, *earlier):
        kept = [list(arrays) for arrays in self.kept]
        if earlier:
            kept[0][0] = after(kept[0][0], *earlier)
        left = len(self.orders[0]) - self.done
        self.sent = upper_sums(kept, 2 ** (left - 1))
        self.made = self.sent[0]

    def finish(self, *earlier):
        while self.done < len(self.orders[0]):
            self.add(*earlier)
            self.send()
        kept = [list(arrays) for arrays in self.kept]
        if earlier:
            kept[0][0] = after(kept[0][0], *earlier)
        return kept


def whole_body(part, pieces, own, rec, *refs):
    units_own, units_rec, out = refs[:pieces], refs[pieces : 2 * pieces], refs[2 * pieces]
    for slot in range(out.shape[0]):
        columns = slice(slot * part, (slot + 1) * part)
        out[slot, 0] = (
            rows_dot(own, columns, units_own, False) + rows_dot(rec, columns, units_rec, False)
        ).astype(BF)


def whole_product(lhs, units, part):
    rows, slotted = lhs[0].shape
    groups = slotted // part
    kinds, _, wide = units[0][0].shape
    tile = min(512, wide)
    each = wide // tile
    whole = pl.BlockSpec((rows, slotted), lambda j: (0, 0))
    columns = [
        pl.BlockSpec((1, piece.shape[1], tile), lambda j: (j // each, 0, j % each))
        for piece in (*units[0], *units[1])
    ]
    return pl.pallas_call(
        functools.partial(whole_body, part, len(units[0])),
        grid=(kinds * each,),
        in_specs=[whole, whole, *columns],
        out_specs=pl.BlockSpec(
            (groups, 1, part, tile), lambda j: (0, j // each, 0, j % each)
        ),
        out_shape=jax.ShapeDtypeStruct((groups, kinds, part, wide), BF),
        compiler_params=params(58),
        cost_estimate=cost(),
        name="whole_product",
    )(*lhs, *units[0], *units[1])


def plane_sum(products):
    groups = products.shape[0]
    flat = products.reshape(-1, products.shape[-1])
    members = [[2 * group + core for group in range(groups)] for core in range(2)]
    mine = lax.psum_scatter(
        flat, "seq", scatter_dimension=0, axis_index_groups=members, tiled=True
    )
    return mine.reshape(products.shape[1:])


def sums_body(counts, tiles, *refs):
    ins, outs = refs[: sum(counts)], refs[sum(counts) :]
    step = pl.program_id(0)
    start = 0
    for source, count in enumerate(counts):
        arrays = ins[start : start + count]
        start += count
        out = outs[source] if len(outs) > 1 else outs[0]

        @pl.when(step // tiles == source)
        def _():
            total = arrays[0][...].astype(F32)
            for array in arrays[1:]:
                total = total + array[...].astype(F32)
            out[...] = total.reshape(out.shape).astype(out.dtype)


def source_tile(step, source, tiles):
    return jnp.clip(step - source * tiles, 0, tiles - 1)


def upper_sums(sources, here):
    _, rows, columns = sources[0][0].shape
    tiles = 2
    block = (here, rows // tiles, columns)
    in_specs, arrays = [], []
    for source, parts in enumerate(sources):
        for array in parts:
            in_specs.append(
                pl.BlockSpec(block, lambda j, s=source: (1, source_tile(j, s, tiles), 0))
            )
            arrays.append(array)
    return pl.pallas_call(
        functools.partial(sums_body, [len(parts) for parts in sources], tiles),
        grid=(len(sources) * tiles,),
        in_specs=in_specs,
        out_specs=[
            pl.BlockSpec(block, lambda j, s=source: (0, source_tile(j, s, tiles), 0))
            for source in range(len(sources))
        ],
        out_shape=[jax.ShapeDtypeStruct((here, rows, columns), BF)] * len(sources),
        compiler_params=params(58),
        cost_estimate=cost(),
        name="upper_sums",
    )(*arrays)


def final_sums(sources, tall, shape):
    sources = [[part if isinstance(part, tuple) else (part, 0) for part in parts] for parts in sources]
    _, rows, columns = sources[0][0][0].shape
    if tall:
        tile = min(512, rows)
        tiles = rows // tile
        block, out_block = (1, tile, columns), (tile, columns)
        out_spec = pl.BlockSpec(out_block, lambda j: (j, 0))

        def at(j, s, slot):
            return (slot, source_tile(j, s, tiles), 0)
    else:
        tile = next(t for t in (512, 256, 128) if columns % t == 0 and shape[2] % t == 0)
        tiles = columns // tile
        each = shape[2] // tile
        block, out_block = (1, rows, tile), (1, rows, tile)
        out_spec = pl.BlockSpec(out_block, lambda j: (j // each, 0, j % each))

        def at(j, s, slot):
            return (slot, 0, source_tile(j, s, tiles))

    in_specs, arrays = [], []
    for source, parts in enumerate(sources):
        for array, slot in parts:
            in_specs.append(pl.BlockSpec(block, lambda j, s=source, slot=slot: at(j, s, slot)))
            arrays.append(array)
    return pl.pallas_call(
        functools.partial(sums_body, [len(parts) for parts in sources], tiles),
        grid=(len(sources) * tiles,),
        in_specs=in_specs,
        out_specs=out_spec,
        out_shape=jax.ShapeDtypeStruct(shape, F32),
        compiler_params=params(58),
        cost_estimate=cost(),
        name="final_sums",
    )(*arrays)


def ring_body(a, b, out):
    out[...] = (a[...].astype(F32) + b[...].astype(F32)).astype(BF)


def ring_sum(arrived, own):
    rows, width = own.shape
    spec = pl.BlockSpec((rows // 2, width), lambda j: (j, 0))
    return pl.pallas_call(
        ring_body,
        grid=(2,),
        in_specs=[spec, spec],
        out_specs=spec,
        out_shape=jax.ShapeDtypeStruct((rows, width), BF),
        compiler_params=params(VMEM),
        cost_estimate=cost(),
        name="ring_sum",
    )(arrived, own)


def rows_body(count, rows, ids, gated, *refs):
    mixes, out, mix_all = refs[:count], refs[count], refs[count + 1]

    @pl.when(pl.program_id(0) == 0)
    def _():
        for place in range(count):
            there = pl.ds(pl.multiple_of(ids[place] * rows, rows), rows)
            mix_all[there, :] = mixes[place][...]

    out[0] = dot(gated[...], mix_all[...], 0, 0).astype(BF)


def rows_product(gated_plane, mixes, count):
    rows, part = mixes[0].shape
    chans = gated_plane.shape[1] // count
    ids = jnp.bitwise_xor(
        lax.axis_index("seq"), jnp.arange(len(mixes), dtype=jnp.int32)
    ).astype(jnp.int32)
    all_rows = rows * len(mixes)
    return pl.pallas_call(
        functools.partial(rows_body, len(mixes), rows),
        grid_spec=pltpu.PrefetchScalarGridSpec(
            num_scalar_prefetch=1,
            grid=(count,),
            in_specs=[pl.BlockSpec((all_rows, chans), lambda r, ids: (0, r))]
            + [pl.BlockSpec((rows, part), lambda r, ids: (0, 0))] * len(mixes),
            out_specs=pl.BlockSpec((1, chans, part), lambda r, ids: (r, 0, 0)),
            scratch_shapes=[pltpu.VMEM((all_rows, part), BF)],
        ),
        out_shape=jax.ShapeDtypeStruct((count, chans, part), BF),
        compiler_params=params(60),
        cost_estimate=cost(),
        name="rows_product",
    )(ids, gated_plane, *mixes)


def spread_body(slots, part, ids, rows_ref, *outs):
    for slot in range(slots):
        start = pl.multiple_of(ids[slot] * part, part)
        outs[slot][...] = rows_ref[:, pl.ds(start, part)]


def spread_slices(rows):
    seq = lax.axis_size("seq")
    part = rows.shape[1] // seq
    ids = jnp.bitwise_xor(lax.axis_index("seq"), jnp.arange(seq, dtype=jnp.int32))
    ids = ids.astype(jnp.int32)
    if part % 128:
        slices = [lax.dynamic_slice_in_dim(rows, ids[q] * part, part, 1) for q in range(seq)]
    else:
        slices = pl.pallas_call(
            functools.partial(spread_body, seq, part),
            in_specs=[
                pl.BlockSpec(memory_space=pltpu.SMEM),
                pl.BlockSpec(memory_space=pltpu.VMEM),
            ],
            out_specs=[pl.BlockSpec(memory_space=pltpu.VMEM)] * seq,
            out_shape=[jax.ShapeDtypeStruct((rows.shape[0], part), BF)] * seq,
            compiler_params=params(VMEM),
            cost_estimate=cost(),
            name="spread_slices",
        )(ids, rows)
    return slices


def project_body(count, *refs):
    toks = refs[:count]
    gain_ref, weights, first_ref, second_ref, third_ref, mixed, normed, scale_ref = refs[count:]
    rows = toks[0].shape[0]

    @pl.when(pl.program_id(0) == 0)
    def _():
        for place in range(count):
            here = pl.ds(place * rows, rows)
            values = toks[place][...].astype(F32)
            scale = lax.rsqrt(jnp.mean(values * values, axis=-1, keepdims=True) + EPS)
            normed[here, :] = (values * scale * gain_ref[...]).astype(BF)
            scale_ref[here, :] = scale

    first = dot(normed[...], weights[0], 1, 0)
    third = dot(normed[...], weights[2], 1, 0)
    first_ref[...] = first
    second_ref[...] = dot(normed[...], weights[1], 1, 0)
    third_ref[...] = third
    mixed[...] = (first * third).astype(BF)


def in_projection(toks, gain, weights, tile=256):
    count = len(toks)
    rows, width = toks[0].shape
    kinds, _, chans = weights.shape
    all_rows = count * rows
    block = pl.BlockSpec((rows, width), lambda j: (0, 0))
    return pl.pallas_call(
        functools.partial(project_body, count),
        grid=(chans // tile,),
        in_specs=[block] * count
        + [
            pl.BlockSpec((1, width), lambda j: (0, 0)),
            pl.BlockSpec((kinds, width, tile), lambda j: (0, 0, j)),
        ],
        out_specs=[
            *([pl.BlockSpec((all_rows, tile), lambda j: (0, j))] * (kinds + 1)),
            pl.BlockSpec((all_rows, width), lambda j: (0, 0)),
            pl.BlockSpec((all_rows, 1), lambda j: (0, 0)),
        ],
        out_shape=[
            *([jax.ShapeDtypeStruct((all_rows, chans), F32)] * kinds),
            jax.ShapeDtypeStruct((all_rows, chans), BF),
            jax.ShapeDtypeStruct((all_rows, width), BF),
            jax.ShapeDtypeStruct((all_rows, 1), F32),
        ],
        compiler_params=params(VMEM),
        cost_estimate=cost(),
        name="in_projection",
    )(*toks, gain.reshape(1, width), weights)


def shifted(values, steps, edge):
    rows = values.shape[0]
    moved = pltpu.roll(values, steps % rows, 0)
    place = lax.broadcasted_iota(jnp.int32, values.shape, 0)
    for k in range(abs(steps)):
        at = k if steps > 0 else rows - 1 - k
        row = edge[k : k + 1] if steps > 0 else edge[abs(steps) - 1 - k : abs(steps) - k]
        moved = jnp.where(place == at, row, moved)
    return moved


def conv_body(count, second, mixed, before, taps, masks, conv_ref, *gated):
    rows = second.shape[0] // count
    for place in range(count):
        here = pl.ds(place * rows, rows)
        values = mixed[here, :].astype(F32)
        edge = before[place]
        lag_one = masks[here, 0:1] * shifted(values, 1, edge[1:2])
        lag_two = masks[here, 1:2] * shifted(values, 2, edge)
        conv = taps[0:1, :] * values + taps[1:2, :] * lag_one + taps[2:3, :] * lag_two
        conv_ref[here, :] = conv
        gated[place][...] = (second[here, :] * conv).astype(BF)


def conv_forward(second, mixed, before, taps, masks, count, tile=128):
    all_rows, chans = mixed.shape
    rows = all_rows // count
    wide = pl.BlockSpec((all_rows, tile), lambda j: (0, j))
    results = pl.pallas_call(
        functools.partial(conv_body, count),
        grid=(chans // tile,),
        in_specs=[
            wide,
            wide,
            pl.BlockSpec((count, 2, tile), lambda j: (0, 0, j)),
            pl.BlockSpec((3, tile), lambda j: (0, j)),
            pl.BlockSpec(masks.shape, lambda j: (0, 0)),
        ],
        out_specs=[wide] + [pl.BlockSpec((rows, tile), lambda j: (0, j))] * count,
        out_shape=[jax.ShapeDtypeStruct((all_rows, chans), F32)]
        + [jax.ShapeDtypeStruct((rows, chans), BF)] * count,
        compiler_params=params(60),
        cost_estimate=cost(),
        name="conv_forward",
    )(second, mixed, before, taps, masks)
    return results[0], results[1:]


def conv_back_body(count, *refs):
    grads = refs[:count]
    first, second, third, conv, mixed, before, behind, taps = refs[count : count + 8]
    masks, triple, tap_ref = refs[count + 8 :]
    rows = grads[0].shape[0]
    sums = [None] * 3
    for place in range(count):
        here = pl.ds(place * rows, rows)
        grad = grads[place][...].astype(F32)
        grad_conv = (grad * second[here, :]).astype(BF).astype(F32)
        edge = behind[place]
        grad_mixed = (
            taps[0:1, :] * grad_conv
            + taps[1:2, :] * masks[here, 2:3] * shifted(grad_conv, -1, edge[0:1])
            + taps[2:3, :] * masks[here, 3:4] * shifted(grad_conv, -2, edge)
        )
        triple[0, here, :] = (grad_mixed * third[here, :]).astype(BF)
        triple[1, here, :] = (grad * conv[here, :]).astype(BF)
        triple[2, here, :] = (grad_mixed * first[here, :]).astype(BF)
        values = mixed[here, :].astype(F32)
        lags = before[place]
        for tap, lagged in enumerate(
            (
                values,
                masks[here, 0:1] * shifted(values, 1, lags[1:2]),
                masks[here, 1:2] * shifted(values, 2, lags),
            )
        ):
            part = jnp.sum(grad_conv * lagged, axis=0, keepdims=True)
            sums[tap] = part if sums[tap] is None else sums[tap] + part
    tap_ref[...] = jnp.concatenate(sums, axis=0)


def conv_backward(grads, first, second, third, conv, mixed, before, behind, taps, masks, tile=128):
    count = len(grads)
    all_rows, chans = mixed.shape
    rows = all_rows // count
    wide = pl.BlockSpec((all_rows, tile), lambda j: (0, j))
    edge = pl.BlockSpec((count, 2, tile), lambda j: (0, 0, j))
    three = pl.BlockSpec((3, tile), lambda j: (0, j))
    return pl.pallas_call(
        functools.partial(conv_back_body, count),
        grid=(chans // tile,),
        in_specs=[pl.BlockSpec((rows, tile), lambda j: (0, j))] * count
        + [wide] * 5
        + [edge, edge, three]
        + [pl.BlockSpec(masks.shape, lambda j: (0, 0))],
        out_specs=[pl.BlockSpec((3, all_rows, tile), lambda j: (0, 0, j)), three],
        out_shape=[
            jax.ShapeDtypeStruct((3, all_rows, chans), BF),
            jax.ShapeDtypeStruct((3, chans), F32),
        ],
        compiler_params=params(60),
        cost_estimate=cost(),
        name="conv_backward",
    )(*grads, first, second, third, conv, mixed, before, behind, taps, masks)


def back_body(count, *refs):
    grads, weights = refs[:2]
    toks = refs[2 : 2 + count]
    scale_ref = refs[2 + count]
    outs = refs[3 + count : 3 + 2 * count]
    gains_ref = refs[3 + 2 * count]
    rows = toks[0].shape[0]
    total = dot(grads[0], weights[0], 1, 1)
    for kind in range(1, grads.shape[0]):
        total = total + dot(grads[kind], weights[kind], 1, 1)
    gains = None
    for place in range(count):
        here = total[place * rows : (place + 1) * rows]
        outs[place][...] = here.astype(BF)
        unit = toks[place][...].astype(F32) * scale_ref[pl.ds(place * rows, rows), :]
        part = jnp.sum(here * unit, axis=0, keepdims=True)
        gains = part if gains is None else gains + part
    gains_ref[...] = gains


def mixer_back(grads, weights, toks, scale, tile=512):
    kinds, all_rows, chans = grads.shape
    width = weights.shape[1]
    count = len(toks)
    rows = all_rows // count
    block = pl.BlockSpec((rows, tile), lambda j: (0, j))
    results = pl.pallas_call(
        functools.partial(back_body, count),
        grid=(width // tile,),
        in_specs=[
            pl.BlockSpec((kinds, all_rows, chans), lambda j: (0, 0, 0)),
            pl.BlockSpec((kinds, tile, chans), lambda j: (0, j, 0)),
        ]
        + [block] * count
        + [pl.BlockSpec((all_rows, 1), lambda j: (0, 0))],
        out_specs=[block] * count + [pl.BlockSpec((1, tile), lambda j: (0, j))],
        out_shape=[jax.ShapeDtypeStruct((rows, width), BF)] * count
        + [jax.ShapeDtypeStruct((1, width), F32)],
        compiler_params=params(60),
        cost_estimate=cost(),
        name="mixer_back",
    )(grads, weights, *toks, scale)
    return results[:count], results[count][0]


def full_others(others):
    seq = lax.axis_size("seq")
    stacked = jnp.stack(others, axis=1)
    stacked = stacked.reshape((seq,) + stacked.shape[2:])
    slots = jnp.bitwise_xor(lax.axis_index("seq"), jnp.arange(seq, dtype=jnp.int32))
    full = jnp.transpose(jnp.take(stacked, slots, axis=0), (1, 2, 0, 3))
    return full.reshape(full.shape[:2] + (-1,))


def plane_ids():
    place = lax.axis_index("seq")
    groups = lax.axis_size("seq") // 2
    chips = jnp.bitwise_xor(place // 2, jnp.arange(groups, dtype=jnp.int32))
    return jnp.concatenate([chips, (place % 2)[None]]).astype(jnp.int32)


def core_columns(ids, groups, kind, part, base=0):
    core = ids[groups]
    offset = jnp.where(core == kind, 0, part)
    return pl.ds(pl.multiple_of(base + offset, part), part)


def mixer_body(count, ids, *refs):
    gated = refs[:count]
    own_w, same_w, cross_w, rows_ref, gain_ref, state_ref, normed_ref, scale_ref = refs[count:]
    step = pl.program_id(0)
    part = same_w.shape[3]
    groups = pl.num_programs(0)
    base = pl.multiple_of(step * 2 * part, 2 * part)
    for kind, other_w in enumerate((same_w, cross_w)):
        inner = core_columns(ids, groups, kind, part)
        total = dot(gated[0][...], own_w[:, inner], 1, 0)
        for place in range(1, count):
            total = total + dot(gated[place][...], other_w[0, count - 1 - place], 1, 0)
        columns = core_columns(ids, groups, kind, part, base)
        state_ref[:, columns] = total + rows_ref[:, columns].astype(F32)

    @pl.when(step == groups - 1)
    def _():
        state = state_ref[...]
        scale = lax.rsqrt(jnp.mean(state * state, axis=-1, keepdims=True) + EPS)
        normed_ref[...] = (state * scale * gain_ref[...]).astype(BF)
        scale_ref[...] = scale


def mixer_rows(gated, own_w, others, input_rows, gain):
    count = len(gated)
    rows, width = input_rows.shape
    chans = gated[0].shape[1]
    groups, _, _, part = others[0].shape
    if part % 128:
        full = full_others(others)
        total = dot(gated[0], own_w, 1, 0)
        for r in range(1, count):
            total = total + dot(gated[r], full[count - 1 - r], 1, 0)
        state = input_rows.astype(F32) + total
        unit, scale = unit_rows(state)
        return state, (unit * gain).astype(BF), scale
    full_rows = pl.BlockSpec((rows, width), lambda t, ids: (0, 0))
    weights = pl.BlockSpec((1, count - 1, chans, part), lambda t, ids: (ids[t], 0, 0, 0))
    return pl.pallas_call(
        functools.partial(mixer_body, count),
        grid_spec=pltpu.PrefetchScalarGridSpec(
            num_scalar_prefetch=1,
            grid=(groups,),
            in_specs=[pl.BlockSpec((rows, chans), lambda t, ids: (0, 0))] * count
            + [
                pl.BlockSpec((chans, 2 * part), lambda t, ids: (0, t)),
                weights,
                weights,
                full_rows,
                pl.BlockSpec((1, width), lambda t, ids: (0, 0)),
            ],
            out_specs=[full_rows, full_rows, pl.BlockSpec((rows, 1), lambda t, ids: (0, 0))],
        ),
        out_shape=[
            jax.ShapeDtypeStruct((rows, width), F32),
            jax.ShapeDtypeStruct((rows, width), BF),
            jax.ShapeDtypeStruct((rows, 1), F32),
        ],
        compiler_params=params(60),
        cost_estimate=cost(),
        name="mixer_rows",
    )(plane_ids(), *gated, own_w, *others, input_rows, gain.reshape(1, width))


def gated_body(count, ids, *refs):
    own_w, same_w, cross_w, arrived, part_own, state_ref, scale_ref, cot_ref, gain_ref = refs[:9]
    outs = refs[9 : 9 + count]
    grad_ref, mix_ref, gains_ref = refs[9 + count : 12 + count]
    accs = refs[12 + count :]
    step = pl.program_id(0)
    part = same_w.shape[3]
    groups = pl.num_programs(0)

    @pl.when(step == 0)
    def _():
        grad_normed = arrived[...].astype(F32) + part_own[...].astype(F32)
        unit = state_ref[...] * scale_ref[...]
        weighted = grad_normed * gain_ref[...]
        grad = cot_ref[...].astype(F32) + scale_ref[...] * (
            weighted - unit * jnp.mean(weighted * unit, axis=-1, keepdims=True)
        )
        grad_ref[...] = grad
        mix_ref[...] = grad.astype(BF)
        gains_ref[...] = jnp.sum(grad_normed * unit, axis=0, keepdims=True)
        for acc in accs:
            acc[...] = jnp.zeros_like(acc)

    base = pl.multiple_of(step * 2 * part, 2 * part)
    mix = [
        mix_ref[:, core_columns(ids, groups, kind, part, base)] for kind in range(2)
    ]
    accs[0][...] += dot(mix_ref[:, pl.ds(base, 2 * part)], own_w[...], 1, 1)
    for place in range(1, count):
        accs[place][...] += dot(mix[0], same_w[0, count - 1 - place], 1, 1) + dot(
            mix[1], cross_w[0, count - 1 - place], 1, 1
        )

    @pl.when(step == groups - 1)
    def _():
        for out, acc in zip(outs, accs):
            out[...] = acc[...].astype(BF)


def gated_rows(arrived, part_own, state, scale, cot, gain, own_w, others):
    rows, width = state.shape
    chans = own_w.shape[0]
    groups, less, _, part = others[0].shape
    count = less + 1
    if part % 128:
        full = full_others(others)
        grad_normed = arrived.astype(F32) + part_own.astype(F32)
        unit = state * scale
        grad = cot.astype(F32) + norm_back(grad_normed, unit, scale, gain)
        mix = grad.astype(BF)
        outs = [dot(mix, own_w, 1, 1).astype(BF)] + [
            dot(mix, full[count - 1 - r], 1, 1).astype(BF) for r in range(1, count)
        ]
        return outs, grad, mix, jnp.sum(grad_normed * unit, axis=0)
    full_rows = pl.BlockSpec((rows, width), lambda t, ids: (0, 0))
    one_row = pl.BlockSpec((1, width), lambda t, ids: (0, 0))
    weights = pl.BlockSpec((1, less, chans, part), lambda t, ids: (ids[t], 0, 0, 0))
    results = pl.pallas_call(
        functools.partial(gated_body, count),
        grid_spec=pltpu.PrefetchScalarGridSpec(
            num_scalar_prefetch=1,
            grid=(groups,),
            in_specs=[
                pl.BlockSpec((chans, 2 * part), lambda t, ids: (0, t)),
                weights,
                weights,
                full_rows,
                full_rows,
                full_rows,
                pl.BlockSpec((rows, 1), lambda t, ids: (0, 0)),
                full_rows,
                one_row,
            ],
            out_specs=[pl.BlockSpec((rows, chans), lambda t, ids: (0, 0))] * count
            + [full_rows, full_rows, one_row],
            scratch_shapes=[pltpu.VMEM((rows, chans), F32)] * count,
        ),
        out_shape=[jax.ShapeDtypeStruct((rows, chans), BF)] * count
        + [
            jax.ShapeDtypeStruct((rows, width), F32),
            jax.ShapeDtypeStruct((rows, width), BF),
            jax.ShapeDtypeStruct((1, width), F32),
        ],
        compiler_params=params(60),
        cost_estimate=cost(),
        name="gated_rows",
    )(plane_ids(), own_w, *others, arrived, part_own, state, scale, cot, gain.reshape(1, width))
    return results[:count], results[count], results[count + 1], results[count + 2][0]


def on_device(
    tokens,
    norm_gains,
    conv_weight,
    in_weight,
    out_weight,
    gate_up_weight,
    down_weight,
    starts,
    cotangent,
):
    shard_rows, width = tokens.shape
    chan_count = lax.axis_size("chan")
    seq_count = lax.axis_size("seq")
    seq_rows = shard_rows * chan_count
    chan_cols = conv_weight.shape[1]
    chan_index = lax.axis_index("chan")
    seq_index = lax.axis_index("seq")
    relative = jnp.arange(chan_count, dtype=jnp.int32)
    owner = (chan_index - relative) % chan_count
    positions = (
        seq_index * seq_rows
        + owner[:, None] * shard_rows
        + jnp.arange(shard_rows, dtype=jnp.int32)[None, :]
    )
    keep_one, keep_two = keep_masks(positions, starts)
    next_one, unused_one = keep_masks(positions + 1, starts)
    unused_two, next_two = keep_masks(positions + 2, starts)
    gain_one = norm_gains[0].astype(F32)
    gain_two = norm_gains[1].astype(F32)
    conv_taps = conv_weight.astype(F32)
    bits = group_bits()
    orders = (bits[::-1], bits)

    part = width // seq_count
    w_own = lax.dynamic_slice_in_dim(out_weight, seq_index * part, part, 1)
    w_one = turned(w_own, "chan", 1)
    w_three = turned(w_own, "chan", 3)
    tok_one = turned(tokens, "chan", 1)
    w_two = turned(after(w_one, w_three), "chan", 1)
    tok_three = turned(after(tokens, w_three), "chan", 3)
    others = jnp.stack([w_one, w_two, w_three])[None]
    halves = [others[:, :, : chan_cols // 2], others[:, :, chan_cols // 2 :]]
    first_arrived = [
        swapped(half, "seq", 2 * order[0]) for half, order in zip(halves, orders)
    ]
    tok_two = turned(after(tok_one, w_two), "chan", 1)
    second_arrived = []
    for place, order in enumerate(orders):
        held = jnp.concatenate([halves[place], first_arrived[place]], axis=0)
        for bit in order[1:-1]:
            held = jnp.concatenate([held, swapped(held, "seq", 2 * bit)], axis=0)
        halves[place] = held
        second_arrived.append(swapped(held, "seq", 2 * order[-1]))
    grad_out = lax.all_gather(after(cotangent, tok_two, tok_three), "chan", axis=0, tiled=True)
    tok_blocks = [tokens, tok_one, tok_two, tok_three]
    for place, order in enumerate(orders):
        held = jnp.concatenate([halves[place], second_arrived[place]], axis=0)
        split = held.reshape((2,) * len(order) + held.shape[1:])
        axes = [len(order) - 1 - order.index(bit) for bit in bits]
        held = jnp.transpose(split, (*axes, *range(len(order), split.ndim))).reshape(held.shape)
        halves[place] = held
    held = jnp.concatenate(halves, axis=2)
    others = (held, swapped(held, "seq", 1))
    masks = jnp.concatenate(
        [
            mask.reshape(seq_rows, 1)
            for mask in (keep_one, keep_two, next_one, next_two)
        ]
        + [jnp.zeros((seq_rows, 124), F32)],
        axis=1,
    )
    *projected, mixed_in, normed_one, scale_all = in_projection(
        [after(tokens, held, masks)] + tok_blocks[1:], gain_one, in_weight
    )
    def at_edge(edge_rows, device):
        return lax.dynamic_index_in_dim(edge_rows, (chan_index - device) % chan_count, 0, False)

    def is_owner(device):
        return (owner == device)[:, None, None]

    ends = jnp.stack(
        [mixed_in[(r + 1) * shard_rows - 2 : (r + 1) * shard_rows] for r in range(chan_count)]
    )
    rim_rows = passed_along(at_edge(ends, chan_count - 1), "seq", 1)
    before = jnp.where(is_owner(0), rim_rows[None], jnp.roll(ends, -1, axis=0)).astype(F32)
    conv_out, gated_mix = conv_forward(
        projected[1], mixed_in, before, conv_taps, masks, chan_count
    )
    gated_rows_own = [gated_mix[0]] + [
        turned(gated_mix[r], "chan", -r) for r in range(1, chan_count)
    ]
    state_own, normed_two_own, scale_two = mixer_rows(
        gated_rows_own, out_weight, others, tokens, gain_two
    )
    gated_plane = lax.all_gather(
        jnp.concatenate([after(gated_rows_own[0], normed_two_own)] + gated_rows_own[1:], axis=1),
        "seq",
        axis=0,
        tiled=True,
    )
    n_one = turned(normed_two_own, "chan", 1)
    normed_one_slices = own_slices(
        [
            after(normed_one[r * shard_rows : (r + 1) * shard_rows], normed_two_own)
            for r in range(chan_count)
        ]
    )
    n_two = turned(n_one, "chan", 1)
    n_three = turned(after(normed_two_own, n_one), "chan", 3)
    hidden_a, pair_a, ffn_parts, grad_two_parts = feed_forward(
        owner,
        [after(normed_two_own, normed_one_slices[0]), n_one],
        grad_out,
        gate_up_weight,
        down_weight,
        0,
    )
    ffn_parts, grad_two_parts, hidden_a, pair_a = [
        after(value, n_two, n_three)
        if not isinstance(value, (list, tuple))
        else [after(one, n_two, n_three) for one in value]
        for value in (ffn_parts, grad_two_parts, hidden_a, pair_a)
    ]
    cot_slices = own_slices(after(grad_out, hidden_a), owner)
    run = turned(grad_two_parts[1], "chan", 1)
    ffn_one = turned(ffn_parts[1], "chan", -1)
    hidden_a_rec = swapped(hidden_a, "seq", 1)
    pair_a_rec = swapped(pair_a, "seq", 1)
    hidden_b, pair_b, ffn_more, grad_more = feed_forward(
        owner,
        [after(n_two, cot_slices[0]), n_three],
        grad_out,
        gate_up_weight,
        down_weight,
        2,
    )
    ffn_parts = list(ffn_parts) + list(ffn_more)
    grad_two_parts = list(grad_two_parts) + list(grad_more)

    total = ring_sum(run, grad_two_parts[2])
    hidden_b, pair_b = [
        after(units, total, ffn_one, hidden_a_rec, pair_a_rec) for units in (hidden_b, pair_b)
    ]
    hidden_b_rec = swapped(hidden_b, "seq", 1)
    pair_b_rec = swapped(pair_b, "seq", 1)
    run = turned(total, "chan", 1)
    normed_two_slices = own_slices(
        [normed_two_own, n_one, n_two, after(n_three, total)], None, False
    )
    down = Joined(
        (after(cot_slices[0], normed_two_slices[0]), cot_slices[1]),
        ([hidden_a, hidden_b], [hidden_a_rec, hidden_b_rec]),
        orders,
        part,
        tall=True,
    )
    total = ring_sum(after(run, down.made), grad_two_parts[3])
    down.send(total)
    run = turned(total, "chan", 1)
    gate_up = whole_product(
        (after(normed_two_slices[0], total), normed_two_slices[1]),
        ([pair_a, pair_b], [pair_a_rec, pair_b_rec]),
        part,
    )
    ffn_three = turned(after(ffn_parts[3], total), "chan", -3)
    run = after(run, gate_up, ffn_three, *down.arrived)
    gate_up_mine = plane_sum(after(gate_up, gated_plane, run))
    ffn_two = turned(after(ffn_parts[2], run), "chan", -1)

    grad_gated_rows, grad_state_own, grad_mix_own, gain_two_part = gated_rows(
        run,
        grad_two_parts[0],
        state_own,
        scale_two,
        cotangent,
        gain_two,
        out_weight,
        others,
    )
    grad_gated_rows = list(grad_gated_rows)
    grad_gated_rows[1:] = [
        after(rows, ffn_two) for rows in grad_gated_rows[1:]
    ]
    gg = [grad_gated_rows[0]] + [
        turned(grad_gated_rows[r], "chan", r) for r in range(1, chan_count)
    ]
    mixes = spread_slices(after(grad_mix_own, *grad_gated_rows[1:]))
    mixes = [mixes[0]] + [swapped(mixes[q], "seq", q) for q in range(1, seq_count)]
    down.add(*grad_gated_rows[1:])
    ffn_two = turned(after(ffn_two, *gg), "chan", -1)
    heads = jnp.stack(
        [
            (
                gg[r][:2].astype(F32) * projected[1][r * shard_rows : r * shard_rows + 2]
            ).astype(BF)
            for r in range(chan_count)
        ]
    )
    heads = after(heads, down.made)
    rim_back = passed_along(at_edge(heads, 0), "seq", -1)
    rim_back = after(rim_back, *mixes)
    behind = jnp.where(is_owner(chan_count - 1), rim_back[None], jnp.roll(heads, 1, axis=0))
    down.send(rim_back)
    grad_triple, tap_part = conv_backward(
        gg, *projected, conv_out, mixed_in, before, behind.astype(F32), conv_taps, masks
    )
    grad_one_parts, gain_one_part = mixer_back(grad_triple, in_weight, tok_blocks, scale_all)
    grad_one_parts = [after(rows, ffn_two, *down.arrived) for rows in grad_one_parts]
    run = turned(grad_one_parts[1], "chan", 1)
    small = after(
        jnp.concatenate([gain_one_part, gain_two_part, tap_part.reshape(-1)]), grad_one_parts[1]
    )
    small_rec = swapped(small, "seq", 1)
    triple_rec = swapped(after(grad_triple, grad_one_parts[1]), "seq", 1)
    out_parts = rows_product(
        after(gated_plane, grad_one_parts[1]), mixes, chan_count
    )
    out_run = turned(out_parts[3], "chan", 1)
    into = Joined(
        (after(normed_one_slices[0], out_parts), normed_one_slices[1]),
        ([grad_triple], [triple_rec]),
        orders,
        part,
    )
    small = small + after(small_rec, into.made)
    small_rec = swapped(small, "seq", 2)
    small = small + small_rec
    into.send(small)
    total = ring_sum(after(run, small), grad_one_parts[2])
    run = turned(total, "chan", 1)
    small_rec = swapped(after(small, total), "seq", 4)
    total = ring_sum(run, grad_one_parts[3])
    out_total = ring_sum(after(out_run, total), out_parts[2])
    run = turned(total, "chan", 1)
    out_run = turned(out_total, "chan", 1)
    down_grad = final_sums(down.finish(total), True, (hidden_a.shape[2], part))
    into.add(down_grad)
    run = after(run, into.made)
    into.send(run)
    out_total = ring_sum(after(out_run, run), out_parts[1])
    out_run = turned(out_total, "chan", 1)
    small = small + after(small_rec, run)
    if seq_count > 8:
        small = summed(small, "seq", 8)
    gains = small[: 2 * width]
    gains_rec = swapped(gains, "chan", 1)
    gate_up_grad = final_sums(
        [[(gate_up_mine, 0)], [(gate_up_mine, 1)]], False, (2, part, hidden_a.shape[2])
    )
    gains = gains + after(gains_rec, gate_up_grad)
    gains = gains + swapped(gains, "chan", 2)
    in_grad = final_sums(into.finish(gate_up_grad), False, (3, part, chan_cols))
    out_grad = out_run.astype(F32) + out_parts[0].astype(F32)

    grad_one_own = run.astype(F32) + grad_one_parts[0].astype(F32)
    input_grad = grad_state_own + norm_back(
        grad_one_own, tokens.astype(F32) * scale_all[:shard_rows], scale_all[:shard_rows], gain_one
    )
    block_output = (state_own + ((ffn_one.astype(F32) + ffn_two.astype(F32)) + (ffn_three.astype(F32) + ffn_parts[0].astype(F32)))).astype(BF)
    gains_grad = gains.reshape(2, width)
    conv_grad = small[2 * width :].reshape(3, chan_cols)
    return (
        block_output,
        input_grad,
        gains_grad,
        conv_grad,
        in_grad,
        out_grad,
        gate_up_grad,
        down_grad,
    )


def solution(mesh):
    placed = (
        P(("seq", "chan"), None),
        P(),
        P(None, "chan"),
        P(None, None, "chan"),
        P("chan", None),
        P(None, None, "chan"),
        P("chan", None),
        P(),
        P(("seq", "chan"), None),
    )
    return jax.shard_map(
        on_device,
        mesh=mesh,
        in_specs=placed,
        out_specs=(
            P(("seq", "chan"), None),
            P(("seq", "chan"), None),
            P(),
            P(None, "chan"),
            P(None, "seq", "chan"),
            P("chan", "seq"),
            P(None, "seq", "chan"),
            P("chan", "seq"),
        ),
        check_vma=False,
    )
```

```python
import functools

import jax
import jax.numpy as jnp
from jax import lax
from jax.experimental import pallas as pl
from jax.experimental.pallas import tpu as pltpu
from jax.sharding import PartitionSpec as P

EPS = 1e-05
BF = jnp.bfloat16
F32 = jnp.float32
MIB = 2**20
VMEM = 48


def params(mebibytes):
    return pltpu.CompilerParams(vmem_limit_bytes=mebibytes * MIB)


def cost():
    return pl.CostEstimate(flops=1024, bytes_accessed=1024, transcendentals=0)


def dot(a, b, dim_a, dim_b):
    return lax.dot_general(a, b, (((dim_a,), (dim_b,)), ((), ())), preferred_element_type=F32)


def after(value, *earlier):
    return lax.optimization_barrier((value,) + earlier)[0]


def passed_along(block, axis, distance):
    devices = range(lax.axis_size(axis))
    route = [(i - distance, i) for i in devices if i - distance in devices]
    return lax.ppermute(block, axis, route)


def turned(block, axis, distance):
    count = lax.axis_size(axis)
    return lax.ppermute(block, axis, [(i, (i + distance) % count) for i in range(count)])


def swapped(block, axis, bit):
    return lax.ppermute(block, axis, [(i, i ^ bit) for i in range(lax.axis_size(axis))])


def summed(block, axis, bit=1):
    while bit < lax.axis_size(axis):
        block = block + swapped(block, axis, bit)
        bit *= 2
    return block


def keep_masks(positions, starts):
    at_start = jnp.any(positions[..., None] == starts, axis=-1)
    prev_start = jnp.any((positions - 1)[..., None] == starts, axis=-1)
    keep_one = ((positions >= 1) & jnp.logical_not(at_start)).astype(F32)[..., None]
    keep_two = ((positions >= 2) & jnp.logical_not(at_start) & jnp.logical_not(prev_start)).astype(
        F32
    )[..., None]
    return (keep_one, keep_two)


def unit_rows(values):
    inv_scale = lax.rsqrt(jnp.mean(values * values, axis=-1, keepdims=True) + EPS)
    return (values * inv_scale, inv_scale)


def norm_back(grad_normed, unit_vals, inv_scale, gain_row):
    weighted = grad_normed * gain_row
    return inv_scale * (
        weighted - unit_vals * jnp.mean(weighted * unit_vals, axis=-1, keepdims=True)
    )


def group_bits():
    groups = lax.axis_size("seq") // 2
    bits = []
    while groups > 1:
        groups //= 2
        bits.append(groups)
    return bits


def ffn_body(count, ids, *refs):
    normed = refs[:count]
    cots = refs[count : 2 * count]
    gate_up_w, down_w = refs[2 * count : 2 * count + 2]
    outs = refs[2 * count + 2 :]
    hidden_ref, pair_ref = outs[:2]
    ffn_refs, grad_refs = outs[2 : 2 + count], outs[2 + count : 2 + 2 * count]
    normed_all, cot_all, ffn_acc, grad_acc = outs[2 + 2 * count :]
    step = pl.program_id(0)
    rows = normed[0].shape[0]

    @pl.when(step == 0)
    def _():
        for place in range(count):
            normed_all[pl.ds(place * rows, rows), :] = normed[place][...]
            cot_all[pl.ds(place * rows, rows), :] = cots[place][...]

    gate = dot(normed_all[...], gate_up_w[0], 1, 0)
    up = dot(normed_all[...], gate_up_w[1], 1, 0)
    grad_hidden = dot(cot_all[...], down_w[...], 1, 1)
    sig = jax.nn.sigmoid(gate)
    activated = gate * sig
    hidden = (activated * up).astype(BF)
    hidden_ref[0] = hidden
    grad_gate = (grad_hidden * up * sig * (1.0 + gate * (1.0 - sig))).astype(BF)
    grad_up = (grad_hidden * activated).astype(BF)
    pair_ref[0] = grad_gate
    pair_ref[1] = grad_up
    ffn_part = dot(hidden, down_w[...], 1, 0)
    grad_part = dot(grad_gate, gate_up_w[0], 1, 1) + dot(grad_up, gate_up_w[1], 1, 1)

    @pl.when(step == 0)
    def _():
        ffn_acc[...] = ffn_part
        grad_acc[...] = grad_part

    @pl.when(step > 0)
    def _():
        ffn_acc[...] += ffn_part
        grad_acc[...] += grad_part

    @pl.when(step == pl.num_programs(0) - 1)
    def _():
        for place in range(count):
            own = pl.ds(place * rows, rows)
            ffn_refs[place][...] = ffn_acc[own, :].astype(BF)
            grad_refs[place][...] = grad_acc[own, :].astype(BF)


def feed_forward(owner, normed, cots, gate_up_weight, down_weight, first, tile=512):
    count = len(normed)
    rows, width = normed[0].shape
    units = down_weight.shape[0]
    here = count * rows
    block = pl.BlockSpec((rows, width), lambda j, ids: (0, 0))
    results = pl.pallas_call(
        functools.partial(ffn_body, count),
        grid_spec=pltpu.PrefetchScalarGridSpec(
            num_scalar_prefetch=1,
            grid=(units // tile,),
            in_specs=[block] * count
            + [
                pl.BlockSpec((rows, width), lambda j, ids, r=first + r: (ids[r], 0))
                for r in range(count)
            ]
            + [
                pl.BlockSpec((2, width, tile), lambda j, ids: (0, 0, j)),
                pl.BlockSpec((tile, width), lambda j, ids: (j, 0)),
            ],
            out_specs=[
                pl.BlockSpec((1, here, tile), lambda j, ids: (0, 0, j)),
                pl.BlockSpec((2, here, tile), lambda j, ids: (0, 0, j)),
            ]
            + [block] * (2 * count),
            scratch_shapes=[
                pltpu.VMEM((here, width), BF),
                pltpu.VMEM((here, width), BF),
                pltpu.VMEM((here, width), F32),
                pltpu.VMEM((here, width), F32),
            ],
        ),
        out_shape=[
            jax.ShapeDtypeStruct((1, here, units), BF),
            jax.ShapeDtypeStruct((2, here, units), BF),
        ]
        + [jax.ShapeDtypeStruct((rows, width), BF)] * (2 * count),
        compiler_params=params(VMEM),
        cost_estimate=cost(),
        name="feed_forward",
    )(owner, *normed, *([cots] * count), gate_up_weight, down_weight)
    return results[0], results[1], results[2 : 2 + count], results[2 + count :]


def slices_body(count, groups, part, apart, ids, *refs):
    ins, outs = refs[:-2], refs[-2:]
    rows = outs[0].shape[0] // count
    for r in range(count):
        here = pl.ds(r * rows, rows)
        if apart:
            source, there = ins[r], slice(None)
        else:
            source = ins[0]
            there = pl.ds(pl.multiple_of(ids[2 * groups + r] * rows, rows), rows)
        for half in range(2):
            for slot in range(groups):
                start = pl.multiple_of(ids[half * groups + slot] * part, part)
                outs[half][here, slot * part : (slot + 1) * part] = source[
                    there, pl.ds(start, part)
                ]


def own_slices(blocks, owner=None, relative=True):
    seq = lax.axis_size("seq")
    groups = seq // 2
    place = lax.axis_index("seq")
    core, group = place % 2, place // 2
    chips = jnp.arange(groups, dtype=jnp.int32)
    if relative:
        chips = jnp.bitwise_xor(group, chips)
    mine, other = 2 * chips + core, 2 * chips + 1 - core
    apart = owner is None
    if apart:
        count = len(blocks)
        owner = jnp.zeros((count,), jnp.int32)
        rows = blocks[0].shape[0]
    else:
        count = owner.shape[0]
        rows = blocks.shape[0] // count
        blocks = [blocks]
    width = blocks[0].shape[1]
    part = width // seq
    if part % 128:
        if apart:
            full = jnp.concatenate(blocks, axis=0)
        else:
            full = jnp.concatenate(
                [
                    lax.dynamic_slice_in_dim(blocks[0], owner[r] * rows, rows, 0)
                    for r in range(count)
                ],
                axis=0,
            )
        full = full.reshape(count * rows, seq, part)
        picked = [
            jnp.take(full, ids, axis=1).reshape(count * rows, groups * part)
            for ids in (mine, other)
        ]
    else:
        ids = jnp.concatenate([mine, other, owner]).astype(jnp.int32)
        picked = pl.pallas_call(
            functools.partial(slices_body, count, groups, part, apart),
            in_specs=[pl.BlockSpec(memory_space=pltpu.SMEM)]
            + [pl.BlockSpec(memory_space=pltpu.VMEM)] * len(blocks),
            out_specs=[pl.BlockSpec(memory_space=pltpu.VMEM)] * 2,
            out_shape=[jax.ShapeDtypeStruct((count * rows, groups * part), BF)] * 2,
            compiler_params=params(VMEM),
            cost_estimate=cost(),
            name="own_slices",
        )(ids, *blocks)
    return picked[0], swapped(picked[1], "seq", 1)


def rows_dot(lhs, columns, units, swap):
    total, start = None, 0
    for piece in units:
        here = lhs[start : start + piece.shape[1], columns]
        start += piece.shape[1]
        part = dot(piece[0], here, 0, 0) if swap else dot(here, piece[0], 0, 0)
        total = part if total is None else total + part
    return total


def product_body(slots, part, tiles, tall, pieces, *refs):
    own, rec = refs[:2]
    units_own, units_rec = refs[2 : 2 + pieces], refs[2 + pieces : 2 + 2 * pieces]
    outs = refs[2 + 2 * pieces :]
    step = pl.program_id(0)
    for half in range(2):

        @pl.when((step < tiles) if half == 0 else (step >= tiles))
        def _():
            for kind in range(2):
                out = outs[2 * half + kind]
                for place, slot in enumerate(slots[half][kind]):
                    columns = slice(slot * part, (slot + 1) * part)
                    out[place] = (
                        rows_dot(own, columns, units_own, tall)
                        + rows_dot(rec, columns, units_rec, tall)
                    ).astype(BF)


class Joined:
    def __init__(self, lhs, units, orders, part, tall=False):
        rows, slotted = lhs[0].shape
        groups = slotted // part
        kinds, _, wide = units[0][0].shape
        tile = next(t for t in (512, 256, 128) if (kinds * wide // 2) % t == 0 and wide % t == 0)
        each = wide // tile
        tiles = kinds * each // 2
        slots = tuple(self.slots(order) for order in orders)
        whole = pl.BlockSpec((rows, slotted), lambda j: (0, 0))
        columns = [
            pl.BlockSpec((1, piece.shape[1], tile), lambda j: (j // each, 0, j % each))
            for piece in (*units[0], *units[1])
        ]
        here = groups // 2
        shapes, specs = [], []
        for half in range(2):
            for kind in range(2):

                def at(j, half=half):
                    return (
                        jnp.minimum(j, tiles - 1) if half == 0 else jnp.maximum(j - tiles, 0)
                    )

                if tall:
                    shape, block = (here, tiles * tile, part), (here, tile, part)
                    specs.append(pl.BlockSpec(block, lambda j, at=at: (0, at(j), 0)))
                else:
                    shape, block = (here, part, tiles * tile), (here, part, tile)
                    specs.append(pl.BlockSpec(block, lambda j, at=at: (0, 0, at(j))))
                shapes.append(jax.ShapeDtypeStruct(shape, BF))
        outs = pl.pallas_call(
            functools.partial(product_body, slots, part, tiles, tall, len(units[0])),
            grid=(2 * tiles,),
            in_specs=[whole, whole, *columns],
            out_specs=specs,
            out_shape=shapes,
            compiler_params=params(58),
            cost_estimate=cost(),
            name="product",
        )(*lhs, *units[0], *units[1])
        self.orders, self.tall = orders, tall
        self.sent = [outs[0], outs[2]]
        self.kept = [[outs[1]], [outs[3]]]
        self.made = outs[0]
        self.done = 0

    def slots(self, order):
        slots = [0]
        for bit in reversed(order):
            slots = slots + [slot + bit for slot in slots]
        half = len(slots) // 2
        return tuple(slots[half:]), tuple(slots[:half])

    def send(self, *earlier):
        self.arrived = []
        for half in range(2):
            bit = 2 * self.orders[half][self.done]
            sent = after(self.sent[half], *earlier) if earlier else self.sent[half]
            arrived = swapped(sent, "seq", bit)
            self.arrived.append(arrived)
            self.kept[half].append(arrived)
        self.done += 1

    def add(self, *earlier):
        kept = [list(arrays) for arrays in self.kept]
        if earlier:
            kept[0][0] = after(kept[0][0], *earlier)
        left = len(self.orders[0]) - self.done
        self.sent = upper_sums(kept, 2 ** (left - 1))
        self.made = self.sent[0]

    def finish(self, *earlier):
        while self.done < len(self.orders[0]):
            self.add(*earlier)
            self.send()
        kept = [list(arrays) for arrays in self.kept]
        if earlier:
            kept[0][0] = after(kept[0][0], *earlier)
        return kept


def whole_body(part, pieces, own, rec, *refs):
    units_own, units_rec, out = refs[:pieces], refs[pieces : 2 * pieces], refs[2 * pieces]
    for slot in range(out.shape[0]):
        columns = slice(slot * part, (slot + 1) * part)
        out[slot, 0] = (
            rows_dot(own, columns, units_own, False) + rows_dot(rec, columns, units_rec, False)
        ).astype(BF)


def whole_product(lhs, units, part):
    rows, slotted = lhs[0].shape
    groups = slotted // part
    kinds, _, wide = units[0][0].shape
    tile = min(512, wide)
    each = wide // tile
    whole = pl.BlockSpec((rows, slotted), lambda j: (0, 0))
    columns = [
        pl.BlockSpec((1, piece.shape[1], tile), lambda j: (j // each, 0, j % each))
        for piece in (*units[0], *units[1])
    ]
    return pl.pallas_call(
        functools.partial(whole_body, part, len(units[0])),
        grid=(kinds * each,),
        in_specs=[whole, whole, *columns],
        out_specs=pl.BlockSpec(
            (groups, 1, part, tile), lambda j: (0, j // each, 0, j % each)
        ),
        out_shape=jax.ShapeDtypeStruct((groups, kinds, part, wide), BF),
        compiler_params=params(58),
        cost_estimate=cost(),
        name="whole_product",
    )(*lhs, *units[0], *units[1])


def plane_sum(products):
    groups = products.shape[0]
    flat = products.reshape(-1, products.shape[-1])
    members = [[2 * group + core for group in range(groups)] for core in range(2)]
    mine = lax.psum_scatter(
        flat, "seq", scatter_dimension=0, axis_index_groups=members, tiled=True
    )
    return mine.reshape(products.shape[1:])


def sums_body(counts, tiles, *refs):
    ins, outs = refs[: sum(counts)], refs[sum(counts) :]
    step = pl.program_id(0)
    start = 0
    for source, count in enumerate(counts):
        arrays = ins[start : start + count]
        start += count
        out = outs[source] if len(outs) > 1 else outs[0]

        @pl.when(step // tiles == source)
        def _():
            total = arrays[0][...].astype(F32)
            for array in arrays[1:]:
                total = total + array[...].astype(F32)
            out[...] = total.reshape(out.shape).astype(out.dtype)


def source_tile(step, source, tiles):
    return jnp.clip(step - source * tiles, 0, tiles - 1)


def upper_sums(sources, here):
    _, rows, columns = sources[0][0].shape
    tiles = 2
    block = (here, rows // tiles, columns)
    in_specs, arrays = [], []
    for source, parts in enumerate(sources):
        for array in parts:
            in_specs.append(
                pl.BlockSpec(block, lambda j, s=source: (1, source_tile(j, s, tiles), 0))
            )
            arrays.append(array)
    return pl.pallas_call(
        functools.partial(sums_body, [len(parts) for parts in sources], tiles),
        grid=(len(sources) * tiles,),
        in_specs=in_specs,
        out_specs=[
            pl.BlockSpec(block, lambda j, s=source: (0, source_tile(j, s, tiles), 0))
            for source in range(len(sources))
        ],
        out_shape=[jax.ShapeDtypeStruct((here, rows, columns), BF)] * len(sources),
        compiler_params=params(58),
        cost_estimate=cost(),
        name="upper_sums",
    )(*arrays)


def final_sums(sources, tall, shape):
    sources = [[part if isinstance(part, tuple) else (part, 0) for part in parts] for parts in sources]
    _, rows, columns = sources[0][0][0].shape
    if tall:
        tile = min(512, rows)
        tiles = rows // tile
        block, out_block = (1, tile, columns), (tile, columns)
        out_spec = pl.BlockSpec(out_block, lambda j: (j, 0))

        def at(j, s, slot):
            return (slot, source_tile(j, s, tiles), 0)
    else:
        tile = next(
            t for t in (2048, 1024, 512, 256, 128) if columns % t == 0 and shape[2] % t == 0
        )
        tiles = columns // tile
        each = shape[2] // tile
        block, out_block = (1, rows, tile), (1, rows, tile)
        out_spec = pl.BlockSpec(out_block, lambda j: (j // each, 0, j % each))

        def at(j, s, slot):
            return (slot, 0, source_tile(j, s, tiles))

    in_specs, arrays = [], []
    for source, parts in enumerate(sources):
        for array, slot in parts:
            in_specs.append(pl.BlockSpec(block, lambda j, s=source, slot=slot: at(j, s, slot)))
            arrays.append(array)
    return pl.pallas_call(
        functools.partial(sums_body, [len(parts) for parts in sources], tiles),
        grid=(len(sources) * tiles,),
        in_specs=in_specs,
        out_specs=out_spec,
        out_shape=jax.ShapeDtypeStruct(shape, F32),
        compiler_params=params(58),
        cost_estimate=cost(),
        name="final_sums",
    )(*arrays)


def triple_body(counts, *refs):
    out = refs[-1]
    kinds, _, wide = out.shape
    start = 0
    column = 0
    for count in counts:
        arrays = refs[start : start + count]
        start += count
        width = arrays[0].shape[2]
        done = 0
        while done < width:
            kind, at = column // wide, column % wide
            step = min(width - done, wide - at)
            total = arrays[0][0, :, done : done + step].astype(F32)
            for array in arrays[1:]:
                total = total + array[0, :, done : done + step].astype(F32)
            out[kind, :, at : at + step] = total
            done += step
            column += step


def triple_sums(sources, shape):
    arrays = [array for parts in sources for array in parts]
    return pl.pallas_call(
        functools.partial(triple_body, [len(parts) for parts in sources]),
        grid=(1,),
        in_specs=[
            pl.BlockSpec((1,) + array.shape[1:], lambda j: (0, 0, 0)) for array in arrays
        ],
        out_specs=pl.BlockSpec(shape, lambda j: (0, 0, 0)),
        out_shape=jax.ShapeDtypeStruct(shape, F32),
        compiler_params=params(VMEM),
        cost_estimate=cost(),
        name="triple_sums",
    )(*arrays)


def ring_body(a, b, out):
    out[...] = (a[...].astype(F32) + b[...].astype(F32)).astype(BF)


def ring_sum(arrived, own):
    rows, width = own.shape
    spec = pl.BlockSpec((rows // 2, width), lambda j: (j, 0))
    return pl.pallas_call(
        ring_body,
        grid=(2,),
        in_specs=[spec, spec],
        out_specs=spec,
        out_shape=jax.ShapeDtypeStruct((rows, width), BF),
        compiler_params=params(VMEM),
        cost_estimate=cost(),
        name="ring_sum",
    )(arrived, own)


def rows_body(count, rows, ids, gated, *refs):
    mixes, out, mix_all = refs[:count], refs[count], refs[count + 1]

    @pl.when(pl.program_id(0) == 0)
    def _():
        for place in range(count):
            there = pl.ds(pl.multiple_of(ids[place] * rows, rows), rows)
            mix_all[there, :] = mixes[place][...]

    out[0] = dot(gated[...], mix_all[...], 0, 0).astype(BF)


def rows_product(gated_plane, mixes, count):
    rows, part = mixes[0].shape
    chans = gated_plane.shape[1] // count
    ids = jnp.bitwise_xor(
        lax.axis_index("seq"), jnp.arange(len(mixes), dtype=jnp.int32)
    ).astype(jnp.int32)
    all_rows = rows * len(mixes)
    return pl.pallas_call(
        functools.partial(rows_body, len(mixes), rows),
        grid_spec=pltpu.PrefetchScalarGridSpec(
            num_scalar_prefetch=1,
            grid=(count,),
            in_specs=[pl.BlockSpec((all_rows, chans), lambda r, ids: (0, r))]
            + [pl.BlockSpec((rows, part), lambda r, ids: (0, 0))] * len(mixes),
            out_specs=pl.BlockSpec((1, chans, part), lambda r, ids: (r, 0, 0)),
            scratch_shapes=[pltpu.VMEM((all_rows, part), BF)],
        ),
        out_shape=jax.ShapeDtypeStruct((count, chans, part), BF),
        compiler_params=params(60),
        cost_estimate=cost(),
        name="rows_product",
    )(ids, gated_plane, *mixes)


def spread_body(slots, part, ids, rows_ref, *outs):
    for slot in range(slots):
        start = pl.multiple_of(ids[slot] * part, part)
        outs[slot][...] = rows_ref[:, pl.ds(start, part)]


def spread_slices(rows):
    seq = lax.axis_size("seq")
    part = rows.shape[1] // seq
    ids = jnp.bitwise_xor(lax.axis_index("seq"), jnp.arange(seq, dtype=jnp.int32))
    ids = ids.astype(jnp.int32)
    if part % 128:
        slices = [lax.dynamic_slice_in_dim(rows, ids[q] * part, part, 1) for q in range(seq)]
    else:
        slices = pl.pallas_call(
            functools.partial(spread_body, seq, part),
            in_specs=[
                pl.BlockSpec(memory_space=pltpu.SMEM),
                pl.BlockSpec(memory_space=pltpu.VMEM),
            ],
            out_specs=[pl.BlockSpec(memory_space=pltpu.VMEM)] * seq,
            out_shape=[jax.ShapeDtypeStruct((rows.shape[0], part), BF)] * seq,
            compiler_params=params(VMEM),
            cost_estimate=cost(),
            name="spread_slices",
        )(ids, rows)
    return slices


def project_body(count, *refs):
    toks = refs[:count]
    gain_ref, weights, first_ref, second_ref, third_ref, mixed, normed, scale_ref = refs[count:]
    rows = toks[0].shape[0]

    @pl.when(pl.program_id(0) == 0)
    def _():
        for place in range(count):
            here = pl.ds(place * rows, rows)
            values = toks[place][...].astype(F32)
            scale = lax.rsqrt(jnp.mean(values * values, axis=-1, keepdims=True) + EPS)
            normed[here, :] = (values * scale * gain_ref[...]).astype(BF)
            scale_ref[here, :] = scale

    first = dot(normed[...], weights[0], 1, 0)
    third = dot(normed[...], weights[2], 1, 0)
    first_ref[...] = first
    second_ref[...] = dot(normed[...], weights[1], 1, 0)
    third_ref[...] = third
    mixed[...] = (first * third).astype(BF)


def in_projection(toks, gain, weights, tile=256):
    count = len(toks)
    rows, width = toks[0].shape
    kinds, _, chans = weights.shape
    all_rows = count * rows
    block = pl.BlockSpec((rows, width), lambda j: (0, 0))
    return pl.pallas_call(
        functools.partial(project_body, count),
        grid=(chans // tile,),
        in_specs=[block] * count
        + [
            pl.BlockSpec((1, width), lambda j: (0, 0)),
            pl.BlockSpec((kinds, width, tile), lambda j: (0, 0, j)),
        ],
        out_specs=[
            *([pl.BlockSpec((all_rows, tile), lambda j: (0, j))] * (kinds + 1)),
            pl.BlockSpec((all_rows, width), lambda j: (0, 0)),
            pl.BlockSpec((all_rows, 1), lambda j: (0, 0)),
        ],
        out_shape=[
            *([jax.ShapeDtypeStruct((all_rows, chans), F32)] * kinds),
            jax.ShapeDtypeStruct((all_rows, chans), BF),
            jax.ShapeDtypeStruct((all_rows, width), BF),
            jax.ShapeDtypeStruct((all_rows, 1), F32),
        ],
        compiler_params=params(60),
        cost_estimate=cost(),
        name="in_projection",
    )(*toks, gain.reshape(1, width), weights)


def shifted(values, steps, edge):
    rows = values.shape[0]
    moved = pltpu.roll(values, steps % rows, 0)
    place = lax.broadcasted_iota(jnp.int32, values.shape, 0)
    for k in range(abs(steps)):
        at = k if steps > 0 else rows - 1 - k
        row = edge[k : k + 1] if steps > 0 else edge[abs(steps) - 1 - k : abs(steps) - k]
        moved = jnp.where(place == at, row, moved)
    return moved


def conv_body(count, second, mixed, before, taps, masks, conv_ref, *gated):
    rows = second.shape[0] // count
    for place in range(count):
        here = pl.ds(place * rows, rows)
        values = mixed[here, :].astype(F32)
        edge = before[place]
        lag_one = masks[here, 0:1] * shifted(values, 1, edge[1:2])
        lag_two = masks[here, 1:2] * shifted(values, 2, edge)
        conv = taps[0:1, :] * values + taps[1:2, :] * lag_one + taps[2:3, :] * lag_two
        conv_ref[here, :] = conv
        gated[place][...] = (second[here, :] * conv).astype(BF)


def conv_forward(second, mixed, before, taps, masks, count, tile=256):
    all_rows, chans = mixed.shape
    rows = all_rows // count
    wide = pl.BlockSpec((all_rows, tile), lambda j: (0, j))
    results = pl.pallas_call(
        functools.partial(conv_body, count),
        grid=(chans // tile,),
        in_specs=[
            wide,
            wide,
            pl.BlockSpec((count, 2, tile), lambda j: (0, 0, j)),
            pl.BlockSpec((3, tile), lambda j: (0, j)),
            pl.BlockSpec(masks.shape, lambda j: (0, 0)),
        ],
        out_specs=[wide] + [pl.BlockSpec((rows, tile), lambda j: (0, j))] * count,
        out_shape=[jax.ShapeDtypeStruct((all_rows, chans), F32)]
        + [jax.ShapeDtypeStruct((rows, chans), BF)] * count,
        compiler_params=params(60),
        cost_estimate=cost(),
        name="conv_forward",
    )(second, mixed, before, taps, masks)
    return results[0], results[1:]


def conv_back_body(count, *refs):
    grads = refs[:count]
    first, second, third, conv, mixed, before, behind, taps = refs[count : count + 8]
    masks, triple, tap_ref = refs[count + 8 :]
    rows = grads[0].shape[0]
    sums = [None] * 3
    for place in range(count):
        here = pl.ds(place * rows, rows)
        grad = grads[place][...].astype(F32)
        grad_conv = (grad * second[here, :]).astype(BF).astype(F32)
        edge = behind[place]
        grad_mixed = (
            taps[0:1, :] * grad_conv
            + taps[1:2, :] * masks[here, 2:3] * shifted(grad_conv, -1, edge[0:1])
            + taps[2:3, :] * masks[here, 3:4] * shifted(grad_conv, -2, edge)
        )
        triple[0, here, :] = (grad_mixed * third[here, :]).astype(BF)
        triple[1, here, :] = (grad * conv[here, :]).astype(BF)
        triple[2, here, :] = (grad_mixed * first[here, :]).astype(BF)
        values = mixed[here, :].astype(F32)
        lags = before[place]
        for tap, lagged in enumerate(
            (
                values,
                masks[here, 0:1] * shifted(values, 1, lags[1:2]),
                masks[here, 1:2] * shifted(values, 2, lags),
            )
        ):
            part = jnp.sum(grad_conv * lagged, axis=0, keepdims=True)
            sums[tap] = part if sums[tap] is None else sums[tap] + part
    tap_ref[...] = jnp.concatenate(sums, axis=0)


def conv_backward(grads, first, second, third, conv, mixed, before, behind, taps, masks, tile=128):
    count = len(grads)
    all_rows, chans = mixed.shape
    rows = all_rows // count
    wide = pl.BlockSpec((all_rows, tile), lambda j: (0, j))
    edge = pl.BlockSpec((count, 2, tile), lambda j: (0, 0, j))
    three = pl.BlockSpec((3, tile), lambda j: (0, j))
    return pl.pallas_call(
        functools.partial(conv_back_body, count),
        grid=(chans // tile,),
        in_specs=[pl.BlockSpec((rows, tile), lambda j: (0, j))] * count
        + [wide] * 5
        + [edge, edge, three]
        + [pl.BlockSpec(masks.shape, lambda j: (0, 0))],
        out_specs=[pl.BlockSpec((3, all_rows, tile), lambda j: (0, 0, j)), three],
        out_shape=[
            jax.ShapeDtypeStruct((3, all_rows, chans), BF),
            jax.ShapeDtypeStruct((3, chans), F32),
        ],
        compiler_params=params(60),
        cost_estimate=cost(),
        name="conv_backward",
    )(*grads, first, second, third, conv, mixed, before, behind, taps, masks)


def back_body(count, *refs):
    grads, weights = refs[:2]
    toks = refs[2 : 2 + count]
    scale_ref = refs[2 + count]
    outs = refs[3 + count : 3 + 2 * count]
    gains_ref = refs[3 + 2 * count]
    rows = toks[0].shape[0]
    total = dot(grads[0], weights[0], 1, 1)
    for kind in range(1, grads.shape[0]):
        total = total + dot(grads[kind], weights[kind], 1, 1)
    gains = None
    for place in range(count):
        here = total[place * rows : (place + 1) * rows]
        outs[place][...] = here.astype(BF)
        unit = toks[place][...].astype(F32) * scale_ref[pl.ds(place * rows, rows), :]
        part = jnp.sum(here * unit, axis=0, keepdims=True)
        gains = part if gains is None else gains + part
    gains_ref[...] = gains


def mixer_back(grads, weights, toks, scale, tile=512):
    kinds, all_rows, chans = grads.shape
    width = weights.shape[1]
    count = len(toks)
    rows = all_rows // count
    block = pl.BlockSpec((rows, tile), lambda j: (0, j))
    results = pl.pallas_call(
        functools.partial(back_body, count),
        grid=(width // tile,),
        in_specs=[
            pl.BlockSpec((kinds, all_rows, chans), lambda j: (0, 0, 0)),
            pl.BlockSpec((kinds, tile, chans), lambda j: (0, j, 0)),
        ]
        + [block] * count
        + [pl.BlockSpec((all_rows, 1), lambda j: (0, 0))],
        out_specs=[block] * count + [pl.BlockSpec((1, tile), lambda j: (0, j))],
        out_shape=[jax.ShapeDtypeStruct((rows, width), BF)] * count
        + [jax.ShapeDtypeStruct((1, width), F32)],
        compiler_params=params(60),
        cost_estimate=cost(),
        name="mixer_back",
    )(grads, weights, *toks, scale)
    return results[:count], results[count][0]


def full_others(others):
    seq = lax.axis_size("seq")
    stacked = jnp.stack(others, axis=1)
    stacked = stacked.reshape((seq,) + stacked.shape[2:])
    slots = jnp.bitwise_xor(lax.axis_index("seq"), jnp.arange(seq, dtype=jnp.int32))
    full = jnp.transpose(jnp.take(stacked, slots, axis=0), (1, 2, 0, 3))
    return full.reshape(full.shape[:2] + (-1,))


def plane_ids():
    place = lax.axis_index("seq")
    groups = lax.axis_size("seq") // 2
    chips = jnp.bitwise_xor(place // 2, jnp.arange(groups, dtype=jnp.int32))
    return jnp.concatenate([chips, (place % 2)[None]]).astype(jnp.int32)


def core_columns(ids, groups, kind, part, base=0):
    core = ids[groups]
    offset = jnp.where(core == kind, 0, part)
    return pl.ds(pl.multiple_of(base + offset, part), part)


def mixer_body(count, ids, *refs):
    gated = refs[:count]
    own_w, same_w, cross_w, rows_ref, gain_ref = refs[count : count + 5]
    state_ref, normed_ref, scale_ref, joined_ref = refs[count + 5 :]
    step = pl.program_id(0)
    part = same_w.shape[3]
    groups = pl.num_programs(0)
    base = pl.multiple_of(step * 2 * part, 2 * part)
    for kind, other_w in enumerate((same_w, cross_w)):
        inner = core_columns(ids, groups, kind, part)
        total = dot(gated[0][...], own_w[:, inner], 1, 0)
        for place in range(1, count):
            total = total + dot(gated[place][...], other_w[0, count - 1 - place], 1, 0)
        columns = core_columns(ids, groups, kind, part, base)
        state_ref[:, columns] = total + rows_ref[:, columns].astype(F32)

    @pl.when(step == groups - 1)
    def _():
        state = state_ref[...]
        scale = lax.rsqrt(jnp.mean(state * state, axis=-1, keepdims=True) + EPS)
        normed_ref[...] = (state * scale * gain_ref[...]).astype(BF)
        scale_ref[...] = scale
        chans = gated[0].shape[1]
        for place in range(count):
            joined_ref[:, place * chans : (place + 1) * chans] = gated[place][...]


def mixer_rows(gated, own_w, others, input_rows, gain):
    count = len(gated)
    rows, width = input_rows.shape
    chans = gated[0].shape[1]
    groups, _, _, part = others[0].shape
    if part % 128:
        full = full_others(others)
        total = dot(gated[0], own_w, 1, 0)
        for r in range(1, count):
            total = total + dot(gated[r], full[count - 1 - r], 1, 0)
        state = input_rows.astype(F32) + total
        unit, scale = unit_rows(state)
        return state, (unit * gain).astype(BF), scale, jnp.concatenate(gated, axis=1)
    full_rows = pl.BlockSpec((rows, width), lambda t, ids: (0, 0))
    weights = pl.BlockSpec((1, count - 1, chans, part), lambda t, ids: (ids[t], 0, 0, 0))
    return pl.pallas_call(
        functools.partial(mixer_body, count),
        grid_spec=pltpu.PrefetchScalarGridSpec(
            num_scalar_prefetch=1,
            grid=(groups,),
            in_specs=[pl.BlockSpec((rows, chans), lambda t, ids: (0, 0))] * count
            + [
                pl.BlockSpec((chans, 2 * part), lambda t, ids: (0, t)),
                weights,
                weights,
                full_rows,
                pl.BlockSpec((1, width), lambda t, ids: (0, 0)),
            ],
            out_specs=[
                full_rows,
                full_rows,
                pl.BlockSpec((rows, 1), lambda t, ids: (0, 0)),
                pl.BlockSpec((rows, count * chans), lambda t, ids: (0, 0)),
            ],
        ),
        out_shape=[
            jax.ShapeDtypeStruct((rows, width), F32),
            jax.ShapeDtypeStruct((rows, width), BF),
            jax.ShapeDtypeStruct((rows, 1), F32),
            jax.ShapeDtypeStruct((rows, count * chans), BF),
        ],
        compiler_params=params(VMEM),
        cost_estimate=cost(),
        name="mixer_rows",
    )(plane_ids(), *gated, own_w, *others, input_rows, gain.reshape(1, width))


def gated_body(count, ids, *refs):
    own_w, same_w, cross_w, arrived, part_own, state_ref, scale_ref, cot_ref, gain_ref = refs[:9]
    outs = refs[9 : 9 + count]
    grad_ref, mix_ref, gains_ref = refs[9 + count : 12 + count]
    accs = refs[12 + count :]
    step = pl.program_id(0)
    part = same_w.shape[3]
    groups = pl.num_programs(0)

    @pl.when(step == 0)
    def _():
        grad_normed = arrived[...].astype(F32) + part_own[...].astype(F32)
        unit = state_ref[...] * scale_ref[...]
        weighted = grad_normed * gain_ref[...]
        grad = cot_ref[...].astype(F32) + scale_ref[...] * (
            weighted - unit * jnp.mean(weighted * unit, axis=-1, keepdims=True)
        )
        grad_ref[...] = grad
        mix_ref[...] = grad.astype(BF)
        gains_ref[...] = jnp.sum(grad_normed * unit, axis=0, keepdims=True)
        for acc in accs:
            acc[...] = jnp.zeros_like(acc)

    base = pl.multiple_of(step * 2 * part, 2 * part)
    mix = [
        mix_ref[:, core_columns(ids, groups, kind, part, base)] for kind in range(2)
    ]
    accs[0][...] += dot(mix_ref[:, pl.ds(base, 2 * part)], own_w[...], 1, 1)
    for place in range(1, count):
        accs[place][...] += dot(mix[0], same_w[0, count - 1 - place], 1, 1) + dot(
            mix[1], cross_w[0, count - 1 - place], 1, 1
        )

    @pl.when(step == groups - 1)
    def _():
        for out, acc in zip(outs, accs):
            out[...] = acc[...].astype(BF)


def gated_rows(arrived, part_own, state, scale, cot, gain, own_w, others):
    rows, width = state.shape
    chans = own_w.shape[0]
    groups, less, _, part = others[0].shape
    count = less + 1
    if part % 128:
        full = full_others(others)
        grad_normed = arrived.astype(F32) + part_own.astype(F32)
        unit = state * scale
        grad = cot.astype(F32) + norm_back(grad_normed, unit, scale, gain)
        mix = grad.astype(BF)
        outs = [dot(mix, own_w, 1, 1).astype(BF)] + [
            dot(mix, full[count - 1 - r], 1, 1).astype(BF) for r in range(1, count)
        ]
        return outs, grad, mix, jnp.sum(grad_normed * unit, axis=0)
    full_rows = pl.BlockSpec((rows, width), lambda t, ids: (0, 0))
    one_row = pl.BlockSpec((1, width), lambda t, ids: (0, 0))
    weights = pl.BlockSpec((1, less, chans, part), lambda t, ids: (ids[t], 0, 0, 0))
    results = pl.pallas_call(
        functools.partial(gated_body, count),
        grid_spec=pltpu.PrefetchScalarGridSpec(
            num_scalar_prefetch=1,
            grid=(groups,),
            in_specs=[
                pl.BlockSpec((chans, 2 * part), lambda t, ids: (0, t)),
                weights,
                weights,
                full_rows,
                full_rows,
                full_rows,
                pl.BlockSpec((rows, 1), lambda t, ids: (0, 0)),
                full_rows,
                one_row,
            ],
            out_specs=[pl.BlockSpec((rows, chans), lambda t, ids: (0, 0))] * count
            + [full_rows, full_rows, one_row],
            scratch_shapes=[pltpu.VMEM((rows, chans), F32)] * count,
        ),
        out_shape=[jax.ShapeDtypeStruct((rows, chans), BF)] * count
        + [
            jax.ShapeDtypeStruct((rows, width), F32),
            jax.ShapeDtypeStruct((rows, width), BF),
            jax.ShapeDtypeStruct((1, width), F32),
        ],
        compiler_params=params(60),
        cost_estimate=cost(),
        name="gated_rows",
    )(plane_ids(), own_w, *others, arrived, part_own, state, scale, cot, gain.reshape(1, width))
    return results[:count], results[count], results[count + 1], results[count + 2][0]


def on_device(
    tokens,
    norm_gains,
    conv_weight,
    in_weight,
    out_weight,
    gate_up_weight,
    down_weight,
    starts,
    cotangent,
):
    shard_rows, width = tokens.shape
    chan_count = lax.axis_size("chan")
    seq_count = lax.axis_size("seq")
    seq_rows = shard_rows * chan_count
    chan_cols = conv_weight.shape[1]
    chan_index = lax.axis_index("chan")
    seq_index = lax.axis_index("seq")
    relative = jnp.arange(chan_count, dtype=jnp.int32)
    owner = (chan_index - relative) % chan_count
    positions = (
        seq_index * seq_rows
        + owner[:, None] * shard_rows
        + jnp.arange(shard_rows, dtype=jnp.int32)[None, :]
    )
    keep_one, keep_two = keep_masks(positions, starts)
    next_one, unused_one = keep_masks(positions + 1, starts)
    unused_two, next_two = keep_masks(positions + 2, starts)
    gain_one = norm_gains[0].astype(F32)
    gain_two = norm_gains[1].astype(F32)
    conv_taps = conv_weight.astype(F32)
    bits = group_bits()
    orders = (bits[::-1], bits)

    part = width // seq_count
    w_own = lax.dynamic_slice_in_dim(out_weight, seq_index * part, part, 1)
    w_one = turned(w_own, "chan", 1)
    w_three = turned(w_own, "chan", 3)
    tok_one = turned(tokens, "chan", 1)
    w_two = turned(after(w_one, w_three, tok_one), "chan", 1)
    tok_three = turned(after(tokens, w_three, tok_one), "chan", 3)
    others = jnp.stack([w_one, w_two, w_three])[None]
    halves = [others[:, :, : chan_cols // 2], others[:, :, chan_cols // 2 :]]
    first_arrived = [
        swapped(half, "seq", 2 * order[0]) for half, order in zip(halves, orders)
    ]
    tok_two = turned(after(tok_one, w_two), "chan", 1)
    second_arrived = []
    for place, order in enumerate(orders):
        held = jnp.concatenate(
            [halves[place], after(first_arrived[place], tok_three)], axis=0
        )
        for bit in order[1:-1]:
            held = jnp.concatenate([held, swapped(held, "seq", 2 * bit)], axis=0)
        halves[place] = held
        second_arrived.append(swapped(held, "seq", 2 * order[-1]))
    grad_out = lax.all_gather(after(cotangent, tok_two, tok_three), "chan", axis=0, tiled=True)
    tok_blocks = [tokens, tok_one, tok_two, tok_three]
    for place, order in enumerate(orders):
        held = jnp.concatenate([halves[place], after(second_arrived[place], tok_two)], axis=0)
        split = held.reshape((2,) * len(order) + held.shape[1:])
        axes = [len(order) - 1 - order.index(bit) for bit in bits]
        held = jnp.transpose(split, (*axes, *range(len(order), split.ndim))).reshape(held.shape)
        halves[place] = held
    held = jnp.concatenate(halves, axis=2)
    others = (held, swapped(held, "seq", 1))
    masks = jnp.concatenate(
        [
            mask.reshape(seq_rows, 1)
            for mask in (keep_one, keep_two, next_one, next_two)
        ]
        + [jnp.zeros((seq_rows, 124), F32)],
        axis=1,
    )
    *projected, mixed_in, normed_one, scale_all = in_projection(
        [after(tokens, held, masks)] + tok_blocks[1:], gain_one, in_weight
    )

    def at_edge(edge_rows, device):
        return lax.dynamic_index_in_dim(edge_rows, (chan_index - device) % chan_count, 0, False)

    def is_owner(device):
        return (owner == device)[:, None, None]

    ends = jnp.stack(
        [mixed_in[(r + 1) * shard_rows - 2 : (r + 1) * shard_rows] for r in range(chan_count)]
    )
    rim_rows = passed_along(at_edge(ends, chan_count - 1), "seq", 1)
    before = jnp.where(is_owner(0), rim_rows[None], jnp.roll(ends, -1, axis=0)).astype(F32)
    conv_out, gated_mix = conv_forward(
        projected[1], mixed_in, before, conv_taps, masks, chan_count
    )
    gated_rows_own = [gated_mix[0]] + [
        turned(gated_mix[r], "chan", -r) for r in range(1, chan_count)
    ]
    state_own, normed_two_own, scale_two, gated_joined = mixer_rows(
        gated_rows_own, out_weight, others, tokens, gain_two
    )
    n_one = turned(normed_two_own, "chan", 1)
    normed_one_slices = own_slices(
        after(normed_one, normed_two_own), jnp.arange(chan_count, dtype=jnp.int32)
    )
    cot_slices = own_slices(after(grad_out, normed_two_own), owner)
    n_one = after(n_one, normed_one_slices[0], cot_slices[0])
    gated_plane = lax.all_gather(
        after(gated_joined, n_one),
        "seq",
        axis=0,
        tiled=True,
    )
    n_two = turned(n_one, "chan", 1)
    n_three = turned(after(normed_two_own, n_one), "chan", 3)
    hidden_a, pair_a, ffn_parts, grad_two_parts = feed_forward(
        owner,
        [normed_two_own, n_one],
        grad_out,
        gate_up_weight,
        down_weight,
        0,
    )
    ffn_parts, grad_two_parts, hidden_a, pair_a = [
        after(value, n_two, n_three)
        if not isinstance(value, (list, tuple))
        else [after(one, n_two, n_three) for one in value]
        for value in (ffn_parts, grad_two_parts, hidden_a, pair_a)
    ]
    run = turned(grad_two_parts[1], "chan", 1)
    ffn_one = turned(ffn_parts[1], "chan", -1)
    hidden_a_rec = swapped(hidden_a, "seq", 1)
    pair_a_rec = swapped(pair_a, "seq", 1)
    hidden_b, pair_b, ffn_more, grad_more = feed_forward(
        owner,
        [n_two, n_three],
        grad_out,
        gate_up_weight,
        down_weight,
        2,
    )
    ffn_parts = list(ffn_parts) + list(ffn_more)
    grad_two_parts = list(grad_two_parts) + list(grad_more)

    total = ring_sum(run, grad_two_parts[2])
    hidden_b, pair_b = [
        after(units, total, ffn_one, hidden_a_rec, pair_a_rec) for units in (hidden_b, pair_b)
    ]
    hidden_b_rec = swapped(hidden_b, "seq", 1)
    pair_b_rec = swapped(after(pair_b, hidden_b_rec), "seq", 1)
    run = turned(total, "chan", 1)
    normed_two_slices = own_slices(
        [normed_two_own, n_one, n_two, after(n_three, total)], None, False
    )
    down = Joined(
        (after(cot_slices[0], normed_two_slices[0]), cot_slices[1]),
        ([hidden_a, hidden_b], [hidden_a_rec, hidden_b_rec]),
        orders,
        part,
        tall=True,
    )
    total = ring_sum(after(run, down.made), grad_two_parts[3])
    down.send()
    run = turned(total, "chan", 1)
    gate_up = whole_product(
        (after(normed_two_slices[0], total), normed_two_slices[1]),
        ([pair_a, pair_b], [pair_a_rec, pair_b_rec]),
        part,
    )
    run = after(run, gate_up, *down.arrived)
    gate_up_mine = plane_sum(after(gate_up, gated_plane, run))
    ffn_two = turned(after(ffn_parts[2], run), "chan", -1)

    grad_gated_rows, grad_state_own, grad_mix_own, gain_two_part = gated_rows(
        run,
        grad_two_parts[0],
        state_own,
        scale_two,
        cotangent,
        gain_two,
        out_weight,
        others,
    )
    grad_gated_rows = list(grad_gated_rows)
    grad_gated_rows[1:] = [
        after(rows, ffn_two) for rows in grad_gated_rows[1:]
    ]
    gg = [grad_gated_rows[0]] + [
        turned(grad_gated_rows[r], "chan", r) for r in range(1, chan_count)
    ]
    mixes = spread_slices(after(grad_mix_own, *grad_gated_rows[1:]))
    mixes = [mixes[0]] + [swapped(mixes[q], "seq", q) for q in range(1, seq_count)]
    ffn_two = turned(after(ffn_two, *gg), "chan", -1)
    ffn_three = turned(after(ffn_parts[3], *gg), "chan", -3)
    heads = jnp.stack(
        [
            (
                gg[r][:2].astype(F32) * projected[1][r * shard_rows : r * shard_rows + 2]
            ).astype(BF)
            for r in range(chan_count)
        ]
    )
    rim_back = passed_along(at_edge(heads, 0), "seq", -1)
    rim_back = after(rim_back, *mixes)
    behind = jnp.where(is_owner(chan_count - 1), rim_back[None], jnp.roll(heads, 1, axis=0))
    grad_triple, tap_part = conv_backward(
        gg, *projected, conv_out, mixed_in, before, behind.astype(F32), conv_taps, masks
    )
    grad_one_parts, gain_one_part = mixer_back(grad_triple, in_weight, tok_blocks, scale_all)
    grad_one_parts = [after(rows, ffn_two, ffn_three) for rows in grad_one_parts]
    run = turned(grad_one_parts[1], "chan", 1)
    small = after(
        jnp.concatenate([gain_one_part, gain_two_part, tap_part.reshape(-1)]), grad_one_parts[1]
    )
    small_rec = swapped(small, "seq", 1)
    triple_rec = swapped(after(grad_triple, grad_one_parts[1]), "seq", 1)
    into = Joined(
        (after(normed_one_slices[0], grad_one_parts[1]), normed_one_slices[1]),
        ([grad_triple], [triple_rec]),
        orders,
        part,
    )
    small = small + small_rec
    small_rec = swapped(small, "seq", 2)
    small = small + after(small_rec, into.made)
    into.send(small)
    total = ring_sum(after(run, small), grad_one_parts[2])
    run = turned(total, "chan", 1)
    small_rec = swapped(after(small, total), "seq", 4)
    out_parts = rows_product(after(gated_plane, total), mixes, chan_count)
    out_run = turned(out_parts[3], "chan", 1)
    down.add(out_parts)
    total = ring_sum(after(run, down.made, out_run), grad_one_parts[3])
    out_total = ring_sum(after(out_run, total), out_parts[2])
    run = turned(total, "chan", 1)
    out_run = turned(out_total, "chan", 1)
    down.send(total)
    into.add(out_total)
    into.send()
    gate_up_grad = final_sums(
        [[(after(gate_up_mine, into.made), 0)], [(gate_up_mine, 1)]],
        False,
        (2, part, hidden_a.shape[2]),
    )
    run = after(run, gate_up_grad)
    out_total = ring_sum(after(out_run, gate_up_grad), out_parts[1])
    out_run = turned(out_total, "chan", 1)
    small = small + after(small_rec, out_total)
    if seq_count > 8:
        small = summed(small, "seq", 8)
    gains = small[: 2 * width]
    gains_rec = swapped(gains, "chan", 1)
    down_grad = final_sums(down.finish(out_total), True, (hidden_a.shape[2], part))
    gains = gains + after(gains_rec, down_grad)
    gains = gains + swapped(gains, "chan", 2)
    in_grad = triple_sums(into.finish(down_grad), (3, part, chan_cols))
    out_grad = out_run.astype(F32) + out_parts[0].astype(F32)

    grad_one_own = run.astype(F32) + grad_one_parts[0].astype(F32)
    input_grad = grad_state_own + norm_back(
        grad_one_own, tokens.astype(F32) * scale_all[:shard_rows], scale_all[:shard_rows], gain_one
    )
    block_output = (state_own + ((ffn_one.astype(F32) + ffn_two.astype(F32)) + (ffn_three.astype(F32) + ffn_parts[0].astype(F32)))).astype(BF)
    gains_grad = gains.reshape(2, width)
    conv_grad = small[2 * width :].reshape(3, chan_cols)
    return (
        block_output,
        input_grad,
        gains_grad,
        conv_grad,
        in_grad,
        out_grad,
        gate_up_grad,
        down_grad,
    )


def solution(mesh):
    placed = (
        P(("seq", "chan"), None),
        P(),
        P(None, "chan"),
        P(None, None, "chan"),
        P("chan", None),
        P(None, None, "chan"),
        P("chan", None),
        P(),
        P(("seq", "chan"), None),
    )
    return jax.shard_map(
        on_device,
        mesh=mesh,
        in_specs=placed,
        out_specs=(
            P(("seq", "chan"), None),
            P(("seq", "chan"), None),
            P(),
            P(None, "chan"),
            P(None, "seq", "chan"),
            P("chan", "seq"),
            P(None, "seq", "chan"),
            P("chan", "seq"),
        ),
        check_vma=False,
    )
```

```python
import functools

import jax
import jax.numpy as jnp
from jax import lax
from jax.experimental import pallas as pl
from jax.experimental.pallas import tpu as pltpu
from jax.sharding import PartitionSpec as P

EPS = 1e-05
BF = jnp.bfloat16
F32 = jnp.float32
MIB = 2**20
VMEM = 48


def params(mebibytes):
    return pltpu.CompilerParams(vmem_limit_bytes=mebibytes * MIB)


def cost():
    return pl.CostEstimate(flops=1024, bytes_accessed=1024, transcendentals=0)


def dot(a, b, dim_a, dim_b):
    return lax.dot_general(a, b, (((dim_a,), (dim_b,)), ((), ())), preferred_element_type=F32)


def after(value, *earlier):
    return lax.optimization_barrier((value,) + earlier)[0]


def passed_along(block, axis, distance):
    devices = range(lax.axis_size(axis))
    route = [(i - distance, i) for i in devices if i - distance in devices]
    return lax.ppermute(block, axis, route)


def turned(block, axis, distance):
    count = lax.axis_size(axis)
    return lax.ppermute(block, axis, [(i, (i + distance) % count) for i in range(count)])


def swapped(block, axis, bit):
    return lax.ppermute(block, axis, [(i, i ^ bit) for i in range(lax.axis_size(axis))])


def summed(block, axis, bit=1):
    while bit < lax.axis_size(axis):
        block = block + swapped(block, axis, bit)
        bit *= 2
    return block


def keep_masks(positions, starts):
    at_start = jnp.any(positions[..., None] == starts, axis=-1)
    prev_start = jnp.any((positions - 1)[..., None] == starts, axis=-1)
    keep_one = ((positions >= 1) & jnp.logical_not(at_start)).astype(F32)[..., None]
    keep_two = ((positions >= 2) & jnp.logical_not(at_start) & jnp.logical_not(prev_start)).astype(
        F32
    )[..., None]
    return (keep_one, keep_two)


def unit_rows(values):
    inv_scale = lax.rsqrt(jnp.mean(values * values, axis=-1, keepdims=True) + EPS)
    return (values * inv_scale, inv_scale)


def norm_back(grad_normed, unit_vals, inv_scale, gain_row):
    weighted = grad_normed * gain_row
    return inv_scale * (
        weighted - unit_vals * jnp.mean(weighted * unit_vals, axis=-1, keepdims=True)
    )


def group_bits():
    groups = lax.axis_size("seq") // 2
    bits = []
    while groups > 1:
        groups //= 2
        bits.append(groups)
    return bits


def ffn_body(count, ids, *refs):
    normed = refs[:count]
    cots = refs[count : 2 * count]
    gate_up_w, down_w = refs[2 * count : 2 * count + 2]
    outs = refs[2 * count + 2 :]
    hidden_ref, pair_ref = outs[:2]
    ffn_refs, grad_refs = outs[2 : 2 + count], outs[2 + count : 2 + 2 * count]
    normed_all, cot_all, ffn_acc, grad_acc = outs[2 + 2 * count :]
    step = pl.program_id(0)
    rows = normed[0].shape[0]

    @pl.when(step == 0)
    def _():
        for place in range(count):
            normed_all[pl.ds(place * rows, rows), :] = normed[place][...]
            cot_all[pl.ds(place * rows, rows), :] = cots[place][...]

    gate = dot(normed_all[...], gate_up_w[0], 1, 0)
    up = dot(normed_all[...], gate_up_w[1], 1, 0)
    grad_hidden = dot(cot_all[...], down_w[...], 1, 1)
    sig = jax.nn.sigmoid(gate)
    activated = gate * sig
    hidden = (activated * up).astype(BF)
    hidden_ref[0] = hidden
    grad_gate = (grad_hidden * up * sig * (1.0 + gate * (1.0 - sig))).astype(BF)
    grad_up = (grad_hidden * activated).astype(BF)
    pair_ref[0] = grad_gate
    pair_ref[1] = grad_up
    ffn_part = dot(hidden, down_w[...], 1, 0)
    grad_part = dot(grad_gate, gate_up_w[0], 1, 1) + dot(grad_up, gate_up_w[1], 1, 1)

    @pl.when(step == 0)
    def _():
        ffn_acc[...] = ffn_part
        grad_acc[...] = grad_part

    @pl.when(step > 0)
    def _():
        ffn_acc[...] += ffn_part
        grad_acc[...] += grad_part

    @pl.when(step == pl.num_programs(0) - 1)
    def _():
        for place in range(count):
            own = pl.ds(place * rows, rows)
            ffn_refs[place][...] = ffn_acc[own, :].astype(BF)
            grad_refs[place][...] = grad_acc[own, :].astype(BF)


def feed_forward(owner, normed, cots, gate_up_weight, down_weight, first, tile=512):
    count = len(normed)
    rows, width = normed[0].shape
    units = down_weight.shape[0]
    here = count * rows
    block = pl.BlockSpec((rows, width), lambda j, ids: (0, 0))
    results = pl.pallas_call(
        functools.partial(ffn_body, count),
        grid_spec=pltpu.PrefetchScalarGridSpec(
            num_scalar_prefetch=1,
            grid=(units // tile,),
            in_specs=[block] * count
            + [
                pl.BlockSpec((rows, width), lambda j, ids, r=first + r: (ids[r], 0))
                for r in range(count)
            ]
            + [
                pl.BlockSpec((2, width, tile), lambda j, ids: (0, 0, j)),
                pl.BlockSpec((tile, width), lambda j, ids: (j, 0)),
            ],
            out_specs=[
                pl.BlockSpec((1, here, tile), lambda j, ids: (0, 0, j)),
                pl.BlockSpec((2, here, tile), lambda j, ids: (0, 0, j)),
            ]
            + [block] * (2 * count),
            scratch_shapes=[
                pltpu.VMEM((here, width), BF),
                pltpu.VMEM((here, width), BF),
                pltpu.VMEM((here, width), F32),
                pltpu.VMEM((here, width), F32),
            ],
        ),
        out_shape=[
            jax.ShapeDtypeStruct((1, here, units), BF),
            jax.ShapeDtypeStruct((2, here, units), BF),
        ]
        + [jax.ShapeDtypeStruct((rows, width), BF)] * (2 * count),
        compiler_params=params(VMEM),
        cost_estimate=cost(),
        name="feed_forward",
    )(owner, *normed, *([cots] * count), gate_up_weight, down_weight)
    return results[0], results[1], results[2 : 2 + count], results[2 + count :]


def slices_body(count, groups, part, apart, ids, *refs):
    ins, outs = refs[:-2], refs[-2:]
    rows = outs[0].shape[0] // count
    for r in range(count):
        here = pl.ds(r * rows, rows)
        if apart:
            source, there = ins[r], slice(None)
        else:
            source = ins[0]
            there = pl.ds(pl.multiple_of(ids[2 * groups + r] * rows, rows), rows)
        for half in range(2):
            for slot in range(groups):
                start = pl.multiple_of(ids[half * groups + slot] * part, part)
                outs[half][here, slot * part : (slot + 1) * part] = source[
                    there, pl.ds(start, part)
                ]


def own_slices(blocks, owner=None, relative=True):
    seq = lax.axis_size("seq")
    groups = seq // 2
    place = lax.axis_index("seq")
    core, group = place % 2, place // 2
    chips = jnp.arange(groups, dtype=jnp.int32)
    if relative:
        chips = jnp.bitwise_xor(group, chips)
    mine, other = 2 * chips + core, 2 * chips + 1 - core
    apart = owner is None
    if apart:
        count = len(blocks)
        owner = jnp.zeros((count,), jnp.int32)
        rows = blocks[0].shape[0]
    else:
        count = owner.shape[0]
        rows = blocks.shape[0] // count
        blocks = [blocks]
    width = blocks[0].shape[1]
    part = width // seq
    if part % 128:
        if apart:
            full = jnp.concatenate(blocks, axis=0)
        else:
            full = jnp.concatenate(
                [
                    lax.dynamic_slice_in_dim(blocks[0], owner[r] * rows, rows, 0)
                    for r in range(count)
                ],
                axis=0,
            )
        full = full.reshape(count * rows, seq, part)
        picked = [
            jnp.take(full, ids, axis=1).reshape(count * rows, groups * part)
            for ids in (mine, other)
        ]
    else:
        ids = jnp.concatenate([mine, other, owner]).astype(jnp.int32)
        picked = pl.pallas_call(
            functools.partial(slices_body, count, groups, part, apart),
            in_specs=[pl.BlockSpec(memory_space=pltpu.SMEM)]
            + [pl.BlockSpec(memory_space=pltpu.VMEM)] * len(blocks),
            out_specs=[pl.BlockSpec(memory_space=pltpu.VMEM)] * 2,
            out_shape=[jax.ShapeDtypeStruct((count * rows, groups * part), BF)] * 2,
            compiler_params=params(VMEM),
            cost_estimate=cost(),
            name="own_slices",
        )(ids, *blocks)
    return picked[0], swapped(picked[1], "seq", 1)


def turn_rows(lhs, turned_lhs, part):
    for start in range(0, lhs.shape[1], part):
        columns = slice(start, start + part)
        turned_lhs[columns, :] = lhs[:, columns].astype(F32).T.astype(BF)


def wide_dot(turned_lhs, columns, units):
    total, start = None, 0
    for piece in units:
        end = start + piece.shape[1]
        part = dot(turned_lhs[columns, start:end], piece[0], 1, 0)
        total = part if total is None else total + part
        start = end
    return total


def tall_dot(lhs, units):
    total, start = None, 0
    for piece in units:
        end = start + piece.shape[1]
        part = dot(piece[0], lhs[start:end, :], 0, 0)
        total = part if total is None else total + part
        start = end
    return total


def product_body(slots, part, tiles, tall, pieces, *refs):
    own, rec = refs[:2]
    units_own, units_rec = refs[2 : 2 + pieces], refs[2 + pieces : 2 + 2 * pieces]
    outs = refs[2 + 2 * pieces : 6 + 2 * pieces]
    step = pl.program_id(0)
    if not tall:
        own_t, rec_t = refs[6 + 2 * pieces :]

        @pl.when(step == 0)
        def _():
            turn_rows(own, own_t, part)
            turn_rows(rec, rec_t, part)

    for half in range(2):

        @pl.when((step < tiles) if half == 0 else (step >= tiles))
        def _():
            if tall:
                total = tall_dot(own, units_own) + tall_dot(rec, units_rec)
            for kind in range(2):
                out = outs[2 * half + kind]
                for place, slot in enumerate(slots[half][kind]):
                    columns = slice(slot * part, (slot + 1) * part)
                    if tall:
                        out[place] = total[:, columns].astype(BF)
                    else:
                        out[place] = (
                            wide_dot(own_t, columns, units_own)
                            + wide_dot(rec_t, columns, units_rec)
                        ).astype(BF)


class Joined:
    def __init__(self, lhs, units, orders, part, tall=False):
        rows, slotted = lhs[0].shape
        groups = slotted // part
        kinds, _, wide = units[0][0].shape
        tile = next(t for t in (512, 256, 128) if (kinds * wide // 2) % t == 0 and wide % t == 0)
        each = wide // tile
        tiles = kinds * each // 2
        slots = tuple(self.slots(order) for order in orders)
        whole = pl.BlockSpec((rows, slotted), lambda j: (0, 0))
        columns = [
            pl.BlockSpec((1, piece.shape[1], tile), lambda j: (j // each, 0, j % each))
            for piece in (*units[0], *units[1])
        ]
        here = groups // 2
        shapes, specs = [], []
        for half in range(2):
            for kind in range(2):

                def at(j, half=half):
                    return (
                        jnp.minimum(j, tiles - 1) if half == 0 else jnp.maximum(j - tiles, 0)
                    )

                if tall:
                    shape, block = (here, tiles * tile, part), (here, tile, part)
                    specs.append(pl.BlockSpec(block, lambda j, at=at: (0, at(j), 0)))
                else:
                    shape, block = (here, part, tiles * tile), (here, part, tile)
                    specs.append(pl.BlockSpec(block, lambda j, at=at: (0, 0, at(j))))
                shapes.append(jax.ShapeDtypeStruct(shape, BF))
        outs = pl.pallas_call(
            functools.partial(product_body, slots, part, tiles, tall, len(units[0])),
            grid=(2 * tiles,),
            in_specs=[whole, whole, *columns],
            out_specs=specs,
            out_shape=shapes,
            scratch_shapes=[] if tall else [pltpu.VMEM((slotted, rows), BF)] * 2,
            compiler_params=params(58),
            cost_estimate=cost(),
            name="product",
        )(*lhs, *units[0], *units[1])
        self.orders, self.tall = orders, tall
        self.sent = [outs[0], outs[2]]
        self.kept = [[outs[1]], [outs[3]]]
        self.made = outs[0]
        self.done = 0

    def slots(self, order):
        slots = [0]
        for bit in reversed(order):
            slots = slots + [slot + bit for slot in slots]
        half = len(slots) // 2
        return tuple(slots[half:]), tuple(slots[:half])

    def send(self, *earlier):
        self.arrived = []
        for half in range(2):
            bit = 2 * self.orders[half][self.done]
            sent = after(self.sent[half], *earlier) if earlier else self.sent[half]
            arrived = swapped(sent, "seq", bit)
            self.arrived.append(arrived)
            self.kept[half].append(arrived)
        self.done += 1

    def add(self, *earlier):
        kept = [list(arrays) for arrays in self.kept]
        if earlier:
            kept[0][0] = after(kept[0][0], *earlier)
        left = len(self.orders[0]) - self.done
        self.sent = upper_sums(kept, 2 ** (left - 1))
        self.made = self.sent[0]

    def finish(self, *earlier):
        while self.done < len(self.orders[0]):
            self.add(*earlier)
            self.send()
        kept = [list(arrays) for arrays in self.kept]
        if earlier:
            kept[0][0] = after(kept[0][0], *earlier)
        return kept


def whole_body(part, pieces, own, rec, *refs):
    units_own, units_rec = refs[:pieces], refs[pieces : 2 * pieces]
    out, own_t, rec_t = refs[2 * pieces :]

    @pl.when(pl.program_id(0) == 0)
    def _():
        turn_rows(own, own_t, part)
        turn_rows(rec, rec_t, part)

    for slot in range(out.shape[0]):
        columns = slice(slot * part, (slot + 1) * part)
        out[slot, 0] = (
            wide_dot(own_t, columns, units_own) + wide_dot(rec_t, columns, units_rec)
        ).astype(BF)


def whole_product(lhs, units, part):
    rows, slotted = lhs[0].shape
    groups = slotted // part
    kinds, _, wide = units[0][0].shape
    tile = min(512, wide)
    each = wide // tile
    whole = pl.BlockSpec((rows, slotted), lambda j: (0, 0))
    columns = [
        pl.BlockSpec((1, piece.shape[1], tile), lambda j: (j // each, 0, j % each))
        for piece in (*units[0], *units[1])
    ]
    return pl.pallas_call(
        functools.partial(whole_body, part, len(units[0])),
        grid=(kinds * each,),
        in_specs=[whole, whole, *columns],
        out_specs=pl.BlockSpec(
            (groups, 1, part, tile), lambda j: (0, j // each, 0, j % each)
        ),
        out_shape=jax.ShapeDtypeStruct((groups, kinds, part, wide), BF),
        scratch_shapes=[pltpu.VMEM((slotted, rows), BF)] * 2,
        compiler_params=params(58),
        cost_estimate=cost(),
        name="whole_product",
    )(*lhs, *units[0], *units[1])


def plane_sum(products):
    groups = products.shape[0]
    flat = products.reshape(-1, products.shape[-1])
    members = [[2 * group + core for group in range(groups)] for core in range(2)]
    mine = lax.psum_scatter(
        flat, "seq", scatter_dimension=0, axis_index_groups=members, tiled=True
    )
    return mine.reshape(products.shape[1:])


def sums_body(counts, tiles, *refs):
    ins, outs = refs[: sum(counts)], refs[sum(counts) :]
    step = pl.program_id(0)
    start = 0
    for source, count in enumerate(counts):
        arrays = ins[start : start + count]
        start += count
        out = outs[source] if len(outs) > 1 else outs[0]

        @pl.when(step // tiles == source)
        def _():
            total = arrays[0][...].astype(F32)
            for array in arrays[1:]:
                total = total + array[...].astype(F32)
            out[...] = total.reshape(out.shape).astype(out.dtype)


def source_tile(step, source, tiles):
    return jnp.clip(step - source * tiles, 0, tiles - 1)


def upper_sums(sources, here):
    _, rows, columns = sources[0][0].shape
    tiles = 2
    block = (here, rows // tiles, columns)
    in_specs, arrays = [], []
    for source, parts in enumerate(sources):
        for array in parts:
            in_specs.append(
                pl.BlockSpec(block, lambda j, s=source: (1, source_tile(j, s, tiles), 0))
            )
            arrays.append(array)
    return pl.pallas_call(
        functools.partial(sums_body, [len(parts) for parts in sources], tiles),
        grid=(len(sources) * tiles,),
        in_specs=in_specs,
        out_specs=[
            pl.BlockSpec(block, lambda j, s=source: (0, source_tile(j, s, tiles), 0))
            for source in range(len(sources))
        ],
        out_shape=[jax.ShapeDtypeStruct((here, rows, columns), BF)] * len(sources),
        compiler_params=params(58),
        cost_estimate=cost(),
        name="upper_sums",
    )(*arrays)


def final_sums(sources, tall, shape):
    sources = [[part if isinstance(part, tuple) else (part, 0) for part in parts] for parts in sources]
    _, rows, columns = sources[0][0][0].shape
    if tall:
        tile = min(512, rows)
        tiles = rows // tile
        block, out_block = (1, tile, columns), (tile, columns)
        out_spec = pl.BlockSpec(out_block, lambda j: (j, 0))

        def at(j, s, slot):
            return (slot, source_tile(j, s, tiles), 0)
    else:
        tile = next(
            t for t in (2048, 1024, 512, 256, 128) if columns % t == 0 and shape[2] % t == 0
        )
        tiles = columns // tile
        each = shape[2] // tile
        block, out_block = (1, rows, tile), (1, rows, tile)
        out_spec = pl.BlockSpec(out_block, lambda j: (j // each, 0, j % each))

        def at(j, s, slot):
            return (slot, 0, source_tile(j, s, tiles))

    in_specs, arrays = [], []
    for source, parts in enumerate(sources):
        for array, slot in parts:
            in_specs.append(pl.BlockSpec(block, lambda j, s=source, slot=slot: at(j, s, slot)))
            arrays.append(array)
    return pl.pallas_call(
        functools.partial(sums_body, [len(parts) for parts in sources], tiles),
        grid=(len(sources) * tiles,),
        in_specs=in_specs,
        out_specs=out_spec,
        out_shape=jax.ShapeDtypeStruct(shape, F32),
        compiler_params=params(58),
        cost_estimate=cost(),
        name="final_sums",
    )(*arrays)


def triple_body(counts, *refs):
    out = refs[-1]
    kinds, _, wide = out.shape
    start = 0
    column = 0
    for count in counts:
        arrays = refs[start : start + count]
        start += count
        width = arrays[0].shape[2]
        done = 0
        while done < width:
            kind, at = column // wide, column % wide
            step = min(width - done, wide - at)
            total = arrays[0][0, :, done : done + step].astype(F32)
            for array in arrays[1:]:
                total = total + array[0, :, done : done + step].astype(F32)
            out[kind, :, at : at + step] = total
            done += step
            column += step


def triple_sums(sources, shape):
    arrays = [array for parts in sources for array in parts]
    return pl.pallas_call(
        functools.partial(triple_body, [len(parts) for parts in sources]),
        grid=(1,),
        in_specs=[
            pl.BlockSpec((1,) + array.shape[1:], lambda j: (0, 0, 0)) for array in arrays
        ],
        out_specs=pl.BlockSpec(shape, lambda j: (0, 0, 0)),
        out_shape=jax.ShapeDtypeStruct(shape, F32),
        compiler_params=params(VMEM),
        cost_estimate=cost(),
        name="triple_sums",
    )(*arrays)


def ring_body(a, b, out):
    out[...] = (a[...].astype(F32) + b[...].astype(F32)).astype(BF)


def ring_sum(arrived, own):
    rows, width = own.shape
    spec = pl.BlockSpec((rows // 2, width), lambda j: (j, 0))
    return pl.pallas_call(
        ring_body,
        grid=(2,),
        in_specs=[spec, spec],
        out_specs=spec,
        out_shape=jax.ShapeDtypeStruct((rows, width), BF),
        compiler_params=params(VMEM),
        cost_estimate=cost(),
        name="ring_sum",
    )(arrived, own)


def rows_body(count, rows, ids, gated, *refs):
    mixes, out, mix_all = refs[:count], refs[count], refs[count + 1]

    @pl.when(pl.program_id(0) == 0)
    def _():
        for place in range(count):
            there = pl.ds(pl.multiple_of(ids[place] * rows, rows), rows)
            mix_all[there, :] = mixes[place][...]

    out[0] = dot(gated[...], mix_all[...], 0, 0).astype(BF)


def rows_product(gated_plane, mixes, count):
    rows, part = mixes[0].shape
    chans = gated_plane.shape[1] // count
    ids = jnp.bitwise_xor(
        lax.axis_index("seq"), jnp.arange(len(mixes), dtype=jnp.int32)
    ).astype(jnp.int32)
    all_rows = rows * len(mixes)
    return pl.pallas_call(
        functools.partial(rows_body, len(mixes), rows),
        grid_spec=pltpu.PrefetchScalarGridSpec(
            num_scalar_prefetch=1,
            grid=(count,),
            in_specs=[pl.BlockSpec((all_rows, chans), lambda r, ids: (0, r))]
            + [pl.BlockSpec((rows, part), lambda r, ids: (0, 0))] * len(mixes),
            out_specs=pl.BlockSpec((1, chans, part), lambda r, ids: (r, 0, 0)),
            scratch_shapes=[pltpu.VMEM((all_rows, part), BF)],
        ),
        out_shape=jax.ShapeDtypeStruct((count, chans, part), BF),
        compiler_params=params(60),
        cost_estimate=cost(),
        name="rows_product",
    )(ids, gated_plane, *mixes)


def spread_body(slots, part, ids, rows_ref, *outs):
    for slot in range(slots):
        start = pl.multiple_of(ids[slot] * part, part)
        outs[slot][...] = rows_ref[:, pl.ds(start, part)]


def spread_slices(rows):
    seq = lax.axis_size("seq")
    part = rows.shape[1] // seq
    ids = jnp.bitwise_xor(lax.axis_index("seq"), jnp.arange(seq, dtype=jnp.int32))
    ids = ids.astype(jnp.int32)
    if part % 128:
        slices = [lax.dynamic_slice_in_dim(rows, ids[q] * part, part, 1) for q in range(seq)]
    else:
        slices = pl.pallas_call(
            functools.partial(spread_body, seq, part),
            in_specs=[
                pl.BlockSpec(memory_space=pltpu.SMEM),
                pl.BlockSpec(memory_space=pltpu.VMEM),
            ],
            out_specs=[pl.BlockSpec(memory_space=pltpu.VMEM)] * seq,
            out_shape=[jax.ShapeDtypeStruct((rows.shape[0], part), BF)] * seq,
            compiler_params=params(VMEM),
            cost_estimate=cost(),
            name="spread_slices",
        )(ids, rows)
    return slices


def project_body(count, *refs):
    toks = refs[:count]
    gain_ref, weights, first_ref, second_ref, third_ref, mixed, normed, scale_ref = refs[count:]
    rows = toks[0].shape[0]

    @pl.when(pl.program_id(0) == 0)
    def _():
        for place in range(count):
            here = pl.ds(place * rows, rows)
            values = toks[place][...].astype(F32)
            scale = lax.rsqrt(jnp.mean(values * values, axis=-1, keepdims=True) + EPS)
            normed[here, :] = (values * scale * gain_ref[...]).astype(BF)
            scale_ref[here, :] = scale

    first = dot(normed[...], weights[0], 1, 0)
    third = dot(normed[...], weights[2], 1, 0)
    first_ref[...] = first
    second_ref[...] = dot(normed[...], weights[1], 1, 0)
    third_ref[...] = third
    mixed[...] = (first * third).astype(BF)


def in_projection(toks, gain, weights, tile=256):
    count = len(toks)
    rows, width = toks[0].shape
    kinds, _, chans = weights.shape
    all_rows = count * rows
    block = pl.BlockSpec((rows, width), lambda j: (0, 0))
    return pl.pallas_call(
        functools.partial(project_body, count),
        grid=(chans // tile,),
        in_specs=[block] * count
        + [
            pl.BlockSpec((1, width), lambda j: (0, 0)),
            pl.BlockSpec((kinds, width, tile), lambda j: (0, 0, j)),
        ],
        out_specs=[
            *([pl.BlockSpec((all_rows, tile), lambda j: (0, j))] * (kinds + 1)),
            pl.BlockSpec((all_rows, width), lambda j: (0, 0)),
            pl.BlockSpec((all_rows, 1), lambda j: (0, 0)),
        ],
        out_shape=[
            *([jax.ShapeDtypeStruct((all_rows, chans), F32)] * kinds),
            jax.ShapeDtypeStruct((all_rows, chans), BF),
            jax.ShapeDtypeStruct((all_rows, width), BF),
            jax.ShapeDtypeStruct((all_rows, 1), F32),
        ],
        compiler_params=params(60),
        cost_estimate=cost(),
        name="in_projection",
    )(*toks, gain.reshape(1, width), weights)


def shifted(values, steps, edge):
    rows = values.shape[0]
    moved = pltpu.roll(values, steps % rows, 0)
    place = lax.broadcasted_iota(jnp.int32, values.shape, 0)
    for k in range(abs(steps)):
        at = k if steps > 0 else rows - 1 - k
        row = edge[k : k + 1] if steps > 0 else edge[abs(steps) - 1 - k : abs(steps) - k]
        moved = jnp.where(place == at, row, moved)
    return moved


def conv_body(count, second, mixed, before, taps, masks, conv_ref, *gated):
    rows = second.shape[0] // count
    for place in range(count):
        here = pl.ds(place * rows, rows)
        values = mixed[here, :].astype(F32)
        edge = before[place]
        lag_one = masks[here, 0:1] * shifted(values, 1, edge[1:2])
        lag_two = masks[here, 1:2] * shifted(values, 2, edge)
        conv = taps[0:1, :] * values + taps[1:2, :] * lag_one + taps[2:3, :] * lag_two
        conv_ref[here, :] = conv
        gated[place][...] = (second[here, :] * conv).astype(BF)


def conv_forward(second, mixed, before, taps, masks, count, tile=256):
    all_rows, chans = mixed.shape
    rows = all_rows // count
    wide = pl.BlockSpec((all_rows, tile), lambda j: (0, j))
    results = pl.pallas_call(
        functools.partial(conv_body, count),
        grid=(chans // tile,),
        in_specs=[
            wide,
            wide,
            pl.BlockSpec((count, 2, tile), lambda j: (0, 0, j)),
            pl.BlockSpec((3, tile), lambda j: (0, j)),
            pl.BlockSpec(masks.shape, lambda j: (0, 0)),
        ],
        out_specs=[wide] + [pl.BlockSpec((rows, tile), lambda j: (0, j))] * count,
        out_shape=[jax.ShapeDtypeStruct((all_rows, chans), F32)]
        + [jax.ShapeDtypeStruct((rows, chans), BF)] * count,
        compiler_params=params(60),
        cost_estimate=cost(),
        name="conv_forward",
    )(second, mixed, before, taps, masks)
    return results[0], results[1:]


def conv_back_body(count, *refs):
    grads = refs[:count]
    first, second, third, conv, mixed, before, behind, taps = refs[count : count + 8]
    masks, triple, tap_ref = refs[count + 8 :]
    rows = grads[0].shape[0]
    sums = [None] * 3
    for place in range(count):
        here = pl.ds(place * rows, rows)
        grad = grads[place][...].astype(F32)
        grad_conv = (grad * second[here, :]).astype(BF).astype(F32)
        edge = behind[place]
        grad_mixed = (
            taps[0:1, :] * grad_conv
            + taps[1:2, :] * masks[here, 2:3] * shifted(grad_conv, -1, edge[0:1])
            + taps[2:3, :] * masks[here, 3:4] * shifted(grad_conv, -2, edge)
        )
        triple[0, here, :] = (grad_mixed * third[here, :]).astype(BF)
        triple[1, here, :] = (grad * conv[here, :]).astype(BF)
        triple[2, here, :] = (grad_mixed * first[here, :]).astype(BF)
        values = mixed[here, :].astype(F32)
        lags = before[place]
        for tap, lagged in enumerate(
            (
                values,
                masks[here, 0:1] * shifted(values, 1, lags[1:2]),
                masks[here, 1:2] * shifted(values, 2, lags),
            )
        ):
            part = jnp.sum(grad_conv * lagged, axis=0, keepdims=True)
            sums[tap] = part if sums[tap] is None else sums[tap] + part
    tap_ref[...] = jnp.concatenate(sums, axis=0)


def conv_backward(grads, first, second, third, conv, mixed, before, behind, taps, masks, tile=128):
    count = len(grads)
    all_rows, chans = mixed.shape
    rows = all_rows // count
    wide = pl.BlockSpec((all_rows, tile), lambda j: (0, j))
    edge = pl.BlockSpec((count, 2, tile), lambda j: (0, 0, j))
    three = pl.BlockSpec((3, tile), lambda j: (0, j))
    return pl.pallas_call(
        functools.partial(conv_back_body, count),
        grid=(chans // tile,),
        in_specs=[pl.BlockSpec((rows, tile), lambda j: (0, j))] * count
        + [wide] * 5
        + [edge, edge, three]
        + [pl.BlockSpec(masks.shape, lambda j: (0, 0))],
        out_specs=[pl.BlockSpec((3, all_rows, tile), lambda j: (0, 0, j)), three],
        out_shape=[
            jax.ShapeDtypeStruct((3, all_rows, chans), BF),
            jax.ShapeDtypeStruct((3, chans), F32),
        ],
        compiler_params=params(60),
        cost_estimate=cost(),
        name="conv_backward",
    )(*grads, first, second, third, conv, mixed, before, behind, taps, masks)


def back_body(count, *refs):
    grads, weights = refs[:2]
    toks = refs[2 : 2 + count]
    scale_ref = refs[2 + count]
    outs = refs[3 + count : 3 + 2 * count]
    gains_ref = refs[3 + 2 * count]
    rows = toks[0].shape[0]
    total = dot(grads[0], weights[0], 1, 1)
    for kind in range(1, grads.shape[0]):
        total = total + dot(grads[kind], weights[kind], 1, 1)
    gains = None
    for place in range(count):
        here = total[place * rows : (place + 1) * rows]
        outs[place][...] = here.astype(BF)
        unit = toks[place][...].astype(F32) * scale_ref[pl.ds(place * rows, rows), :]
        part = jnp.sum(here * unit, axis=0, keepdims=True)
        gains = part if gains is None else gains + part
    gains_ref[...] = gains


def mixer_back(grads, weights, toks, scale, tile=512):
    kinds, all_rows, chans = grads.shape
    width = weights.shape[1]
    count = len(toks)
    rows = all_rows // count
    block = pl.BlockSpec((rows, tile), lambda j: (0, j))
    results = pl.pallas_call(
        functools.partial(back_body, count),
        grid=(width // tile,),
        in_specs=[
            pl.BlockSpec((kinds, all_rows, chans), lambda j: (0, 0, 0)),
            pl.BlockSpec((kinds, tile, chans), lambda j: (0, j, 0)),
        ]
        + [block] * count
        + [pl.BlockSpec((all_rows, 1), lambda j: (0, 0))],
        out_specs=[block] * count + [pl.BlockSpec((1, tile), lambda j: (0, j))],
        out_shape=[jax.ShapeDtypeStruct((rows, width), BF)] * count
        + [jax.ShapeDtypeStruct((1, width), F32)],
        compiler_params=params(60),
        cost_estimate=cost(),
        name="mixer_back",
    )(grads, weights, *toks, scale)
    return results[:count], results[count][0]


def full_others(others):
    seq = lax.axis_size("seq")
    stacked = jnp.stack(others, axis=1)
    stacked = stacked.reshape((seq,) + stacked.shape[2:])
    slots = jnp.bitwise_xor(lax.axis_index("seq"), jnp.arange(seq, dtype=jnp.int32))
    full = jnp.transpose(jnp.take(stacked, slots, axis=0), (1, 2, 0, 3))
    return full.reshape(full.shape[:2] + (-1,))


def plane_ids():
    place = lax.axis_index("seq")
    groups = lax.axis_size("seq") // 2
    chips = jnp.bitwise_xor(place // 2, jnp.arange(groups, dtype=jnp.int32))
    return jnp.concatenate([chips, (place % 2)[None]]).astype(jnp.int32)


def core_columns(ids, groups, kind, part, base=0):
    core = ids[groups]
    offset = jnp.where(core == kind, 0, part)
    return pl.ds(pl.multiple_of(base + offset, part), part)


def mixer_body(count, ids, *refs):
    gated = refs[:count]
    own_w, same_w, cross_w, rows_ref, gain_ref = refs[count : count + 5]
    state_ref, normed_ref, scale_ref, joined_ref = refs[count + 5 :]
    step = pl.program_id(0)
    part = same_w.shape[3]
    groups = pl.num_programs(0)
    base = pl.multiple_of(step * 2 * part, 2 * part)
    for kind, other_w in enumerate((same_w, cross_w)):
        inner = core_columns(ids, groups, kind, part)
        total = dot(gated[0][...], own_w[:, inner], 1, 0)
        for place in range(1, count):
            total = total + dot(gated[place][...], other_w[0, count - 1 - place], 1, 0)
        columns = core_columns(ids, groups, kind, part, base)
        state_ref[:, columns] = total + rows_ref[:, columns].astype(F32)

    @pl.when(step == groups - 1)
    def _():
        state = state_ref[...]
        scale = lax.rsqrt(jnp.mean(state * state, axis=-1, keepdims=True) + EPS)
        normed_ref[...] = (state * scale * gain_ref[...]).astype(BF)
        scale_ref[...] = scale
        chans = gated[0].shape[1]
        for place in range(count):
            joined_ref[:, place * chans : (place + 1) * chans] = gated[place][...]


def mixer_rows(gated, own_w, others, input_rows, gain):
    count = len(gated)
    rows, width = input_rows.shape
    chans = gated[0].shape[1]
    groups, _, _, part = others[0].shape
    if part % 128:
        full = full_others(others)
        total = dot(gated[0], own_w, 1, 0)
        for r in range(1, count):
            total = total + dot(gated[r], full[count - 1 - r], 1, 0)
        state = input_rows.astype(F32) + total
        unit, scale = unit_rows(state)
        return state, (unit * gain).astype(BF), scale, jnp.concatenate(gated, axis=1)
    full_rows = pl.BlockSpec((rows, width), lambda t, ids: (0, 0))
    weights = pl.BlockSpec((1, count - 1, chans, part), lambda t, ids: (ids[t], 0, 0, 0))
    return pl.pallas_call(
        functools.partial(mixer_body, count),
        grid_spec=pltpu.PrefetchScalarGridSpec(
            num_scalar_prefetch=1,
            grid=(groups,),
            in_specs=[pl.BlockSpec((rows, chans), lambda t, ids: (0, 0))] * count
            + [
                pl.BlockSpec((chans, 2 * part), lambda t, ids: (0, t)),
                weights,
                weights,
                full_rows,
                pl.BlockSpec((1, width), lambda t, ids: (0, 0)),
            ],
            out_specs=[
                full_rows,
                full_rows,
                pl.BlockSpec((rows, 1), lambda t, ids: (0, 0)),
                pl.BlockSpec((rows, count * chans), lambda t, ids: (0, 0)),
            ],
        ),
        out_shape=[
            jax.ShapeDtypeStruct((rows, width), F32),
            jax.ShapeDtypeStruct((rows, width), BF),
            jax.ShapeDtypeStruct((rows, 1), F32),
            jax.ShapeDtypeStruct((rows, count * chans), BF),
        ],
        compiler_params=params(VMEM),
        cost_estimate=cost(),
        name="mixer_rows",
    )(plane_ids(), *gated, own_w, *others, input_rows, gain.reshape(1, width))


def gated_body(count, ids, *refs):
    own_w, same_w, cross_w, arrived, part_own, state_ref, scale_ref, cot_ref, gain_ref = refs[:9]
    outs = refs[9 : 9 + count]
    grad_ref, mix_ref, gains_ref = refs[9 + count : 12 + count]
    accs = refs[12 + count :]
    step = pl.program_id(0)
    part = same_w.shape[3]
    groups = pl.num_programs(0)

    @pl.when(step == 0)
    def _():
        grad_normed = arrived[...].astype(F32) + part_own[...].astype(F32)
        unit = state_ref[...] * scale_ref[...]
        weighted = grad_normed * gain_ref[...]
        grad = cot_ref[...].astype(F32) + scale_ref[...] * (
            weighted - unit * jnp.mean(weighted * unit, axis=-1, keepdims=True)
        )
        grad_ref[...] = grad
        mix_ref[...] = grad.astype(BF)
        gains_ref[...] = jnp.sum(grad_normed * unit, axis=0, keepdims=True)
        for acc in accs:
            acc[...] = jnp.zeros_like(acc)

    base = pl.multiple_of(step * 2 * part, 2 * part)
    mix = [
        mix_ref[:, core_columns(ids, groups, kind, part, base)] for kind in range(2)
    ]
    accs[0][...] += dot(mix_ref[:, pl.ds(base, 2 * part)], own_w[...], 1, 1)
    for place in range(1, count):
        accs[place][...] += dot(mix[0], same_w[0, count - 1 - place], 1, 1) + dot(
            mix[1], cross_w[0, count - 1 - place], 1, 1
        )

    @pl.when(step == groups - 1)
    def _():
        for out, acc in zip(outs, accs):
            out[...] = acc[...].astype(BF)


def gated_rows(arrived, part_own, state, scale, cot, gain, own_w, others):
    rows, width = state.shape
    chans = own_w.shape[0]
    groups, less, _, part = others[0].shape
    count = less + 1
    if part % 128:
        full = full_others(others)
        grad_normed = arrived.astype(F32) + part_own.astype(F32)
        unit = state * scale
        grad = cot.astype(F32) + norm_back(grad_normed, unit, scale, gain)
        mix = grad.astype(BF)
        outs = [dot(mix, own_w, 1, 1).astype(BF)] + [
            dot(mix, full[count - 1 - r], 1, 1).astype(BF) for r in range(1, count)
        ]
        return outs, grad, mix, jnp.sum(grad_normed * unit, axis=0)
    full_rows = pl.BlockSpec((rows, width), lambda t, ids: (0, 0))
    one_row = pl.BlockSpec((1, width), lambda t, ids: (0, 0))
    weights = pl.BlockSpec((1, less, chans, part), lambda t, ids: (ids[t], 0, 0, 0))
    results = pl.pallas_call(
        functools.partial(gated_body, count),
        grid_spec=pltpu.PrefetchScalarGridSpec(
            num_scalar_prefetch=1,
            grid=(groups,),
            in_specs=[
                pl.BlockSpec((chans, 2 * part), lambda t, ids: (0, t)),
                weights,
                weights,
                full_rows,
                full_rows,
                full_rows,
                pl.BlockSpec((rows, 1), lambda t, ids: (0, 0)),
                full_rows,
                one_row,
            ],
            out_specs=[pl.BlockSpec((rows, chans), lambda t, ids: (0, 0))] * count
            + [full_rows, full_rows, one_row],
            scratch_shapes=[pltpu.VMEM((rows, chans), F32)] * count,
        ),
        out_shape=[jax.ShapeDtypeStruct((rows, chans), BF)] * count
        + [
            jax.ShapeDtypeStruct((rows, width), F32),
            jax.ShapeDtypeStruct((rows, width), BF),
            jax.ShapeDtypeStruct((1, width), F32),
        ],
        compiler_params=params(60),
        cost_estimate=cost(),
        name="gated_rows",
    )(plane_ids(), own_w, *others, arrived, part_own, state, scale, cot, gain.reshape(1, width))
    return results[:count], results[count], results[count + 1], results[count + 2][0]


def on_device(
    tokens,
    norm_gains,
    conv_weight,
    in_weight,
    out_weight,
    gate_up_weight,
    down_weight,
    starts,
    cotangent,
):
    shard_rows, width = tokens.shape
    chan_count = lax.axis_size("chan")
    seq_count = lax.axis_size("seq")
    seq_rows = shard_rows * chan_count
    chan_cols = conv_weight.shape[1]
    chan_index = lax.axis_index("chan")
    seq_index = lax.axis_index("seq")
    relative = jnp.arange(chan_count, dtype=jnp.int32)
    owner = (chan_index - relative) % chan_count
    positions = (
        seq_index * seq_rows
        + owner[:, None] * shard_rows
        + jnp.arange(shard_rows, dtype=jnp.int32)[None, :]
    )
    keep_one, keep_two = keep_masks(positions, starts)
    next_one, unused_one = keep_masks(positions + 1, starts)
    unused_two, next_two = keep_masks(positions + 2, starts)
    gain_one = norm_gains[0].astype(F32)
    gain_two = norm_gains[1].astype(F32)
    conv_taps = conv_weight.astype(F32)
    bits = group_bits()
    orders = (bits[::-1], bits)

    part = width // seq_count
    w_own = lax.dynamic_slice_in_dim(out_weight, seq_index * part, part, 1)
    w_one = turned(w_own, "chan", 1)
    w_three = turned(w_own, "chan", 3)
    tok_one = turned(tokens, "chan", 1)
    w_two = turned(after(w_one, w_three, tok_one), "chan", 1)
    tok_three = turned(after(tokens, w_three, tok_one), "chan", 3)
    others = jnp.stack([w_one, w_two, w_three])[None]
    halves = [others[:, :, : chan_cols // 2], others[:, :, chan_cols // 2 :]]
    first_arrived = [
        swapped(half, "seq", 2 * order[0]) for half, order in zip(halves, orders)
    ]
    tok_two = turned(after(tok_one, w_two), "chan", 1)
    second_arrived = []
    for place, order in enumerate(orders):
        held = jnp.concatenate(
            [halves[place], after(first_arrived[place], tok_three)], axis=0
        )
        for bit in order[1:-1]:
            held = jnp.concatenate([held, swapped(held, "seq", 2 * bit)], axis=0)
        halves[place] = held
        second_arrived.append(swapped(held, "seq", 2 * order[-1]))
    grad_out = lax.all_gather(after(cotangent, tok_three), "chan", axis=0, tiled=True)
    tok_blocks = [tokens, tok_one, tok_two, tok_three]
    for place, order in enumerate(orders):
        held = jnp.concatenate([halves[place], after(second_arrived[place], tok_two)], axis=0)
        split = held.reshape((2,) * len(order) + held.shape[1:])
        axes = [len(order) - 1 - order.index(bit) for bit in bits]
        held = jnp.transpose(split, (*axes, *range(len(order), split.ndim))).reshape(held.shape)
        halves[place] = held
    held = jnp.concatenate(halves, axis=2)
    others = (held, swapped(held, "seq", 1))
    masks = jnp.concatenate(
        [
            mask.reshape(seq_rows, 1)
            for mask in (keep_one, keep_two, next_one, next_two)
        ]
        + [jnp.zeros((seq_rows, 124), F32)],
        axis=1,
    )
    *projected, mixed_in, normed_one, scale_all = in_projection(
        [after(tokens, held, masks)] + tok_blocks[1:], gain_one, in_weight
    )

    def at_edge(edge_rows, device):
        return lax.dynamic_index_in_dim(edge_rows, (chan_index - device) % chan_count, 0, False)

    def is_owner(device):
        return (owner == device)[:, None, None]

    ends = jnp.stack(
        [mixed_in[(r + 1) * shard_rows - 2 : (r + 1) * shard_rows] for r in range(chan_count)]
    )
    rim_rows = passed_along(at_edge(ends, chan_count - 1), "seq", 1)
    before = jnp.where(is_owner(0), rim_rows[None], jnp.roll(ends, -1, axis=0)).astype(F32)
    conv_out, gated_mix = conv_forward(
        projected[1], mixed_in, before, conv_taps, masks, chan_count
    )
    gated_mix = [after(rows, grad_out) for rows in gated_mix]
    gated_rows_own = [gated_mix[0]] + [
        turned(gated_mix[r], "chan", -r) for r in range(1, chan_count)
    ]
    state_own, normed_two_own, scale_two, gated_joined = mixer_rows(
        gated_rows_own, out_weight, others, tokens, gain_two
    )
    n_one = turned(normed_two_own, "chan", 1)
    normed_one_slices = own_slices(
        after(normed_one, normed_two_own), jnp.arange(chan_count, dtype=jnp.int32)
    )
    cot_slices = own_slices(after(grad_out, normed_two_own), owner)
    n_one = after(n_one, normed_one_slices[0], cot_slices[0])
    gated_plane = lax.all_gather(
        after(gated_joined, n_one),
        "seq",
        axis=0,
        tiled=True,
    )
    n_two = turned(n_one, "chan", 1)
    n_three = turned(after(normed_two_own, n_one), "chan", 3)
    hidden_a, pair_a, ffn_parts, grad_two_parts = feed_forward(
        owner,
        [normed_two_own, n_one],
        grad_out,
        gate_up_weight,
        down_weight,
        0,
    )
    ffn_parts, grad_two_parts, hidden_a, pair_a = [
        after(value, n_two, n_three)
        if not isinstance(value, (list, tuple))
        else [after(one, n_two, n_three) for one in value]
        for value in (ffn_parts, grad_two_parts, hidden_a, pair_a)
    ]
    run = turned(grad_two_parts[1], "chan", 1)
    ffn_one = turned(ffn_parts[1], "chan", -1)
    hidden_a_rec = swapped(hidden_a, "seq", 1)
    pair_a_rec = swapped(pair_a, "seq", 1)
    hidden_b, pair_b, ffn_more, grad_more = feed_forward(
        owner,
        [n_two, n_three],
        grad_out,
        gate_up_weight,
        down_weight,
        2,
    )
    ffn_parts = list(ffn_parts) + list(ffn_more)
    grad_two_parts = list(grad_two_parts) + list(grad_more)

    total = ring_sum(run, grad_two_parts[2])
    hidden_b, pair_b = [
        after(units, total, ffn_one, hidden_a_rec, pair_a_rec) for units in (hidden_b, pair_b)
    ]
    hidden_b_rec = swapped(hidden_b, "seq", 1)
    pair_b_rec = swapped(after(pair_b, hidden_b_rec), "seq", 1)
    run = turned(total, "chan", 1)
    normed_two_slices = own_slices(
        [normed_two_own, n_one, n_two, after(n_three, total)], None, False
    )
    down = Joined(
        (after(cot_slices[0], normed_two_slices[0]), cot_slices[1]),
        ([hidden_a, hidden_b], [hidden_a_rec, hidden_b_rec]),
        orders,
        part,
        tall=True,
    )
    total = ring_sum(after(run, down.made), grad_two_parts[3])
    down.send()
    run = turned(total, "chan", 1)
    gate_up = whole_product(
        (after(normed_two_slices[0], total), normed_two_slices[1]),
        ([pair_a, pair_b], [pair_a_rec, pair_b_rec]),
        part,
    )
    run = after(run, gate_up, *down.arrived)
    gate_up_mine = plane_sum(after(gate_up, gated_plane, run))
    ffn_two = turned(after(ffn_parts[2], run), "chan", -1)

    grad_gated_rows, grad_state_own, grad_mix_own, gain_two_part = gated_rows(
        run,
        grad_two_parts[0],
        state_own,
        scale_two,
        cotangent,
        gain_two,
        out_weight,
        others,
    )
    grad_gated_rows = list(grad_gated_rows)
    grad_gated_rows[1:] = [
        after(rows, ffn_two) for rows in grad_gated_rows[1:]
    ]
    gg = [grad_gated_rows[0]] + [
        turned(grad_gated_rows[r], "chan", r) for r in range(1, chan_count)
    ]
    mixes = spread_slices(after(grad_mix_own, *grad_gated_rows[1:]))
    mixes = [mixes[0]] + [swapped(mixes[q], "seq", q) for q in range(1, seq_count)]
    ffn_two = turned(after(ffn_two, *gg), "chan", -1)
    ffn_three = turned(after(ffn_parts[3], *gg), "chan", -3)
    heads = jnp.stack(
        [
            (
                gg[r][:2].astype(F32) * projected[1][r * shard_rows : r * shard_rows + 2]
            ).astype(BF)
            for r in range(chan_count)
        ]
    )
    rim_back = passed_along(at_edge(heads, 0), "seq", -1)
    rim_back = after(rim_back, *mixes)
    behind = jnp.where(is_owner(chan_count - 1), rim_back[None], jnp.roll(heads, 1, axis=0))
    grad_triple, tap_part = conv_backward(
        gg, *projected, conv_out, mixed_in, before, behind.astype(F32), conv_taps, masks
    )
    grad_one_parts, gain_one_part = mixer_back(grad_triple, in_weight, tok_blocks, scale_all)
    grad_one_parts = [after(rows, ffn_two, ffn_three) for rows in grad_one_parts]
    run = turned(grad_one_parts[1], "chan", 1)
    small = after(
        jnp.concatenate([gain_one_part, gain_two_part, tap_part.reshape(-1)]), grad_one_parts[1]
    )
    small_rec = swapped(small, "seq", 1)
    triple_rec = swapped(after(grad_triple, grad_one_parts[1]), "seq", 1)
    into = Joined(
        (after(normed_one_slices[0], grad_one_parts[1]), normed_one_slices[1]),
        ([grad_triple], [triple_rec]),
        orders,
        part,
    )
    small = small + small_rec
    small_rec = swapped(small, "seq", 2)
    small = small + after(small_rec, into.made)
    into.send(small)
    total = ring_sum(after(run, small), grad_one_parts[2])
    run = turned(total, "chan", 1)
    small_rec = swapped(after(small, total), "seq", 4)
    out_parts = rows_product(after(gated_plane, total), mixes, chan_count)
    out_run = turned(out_parts[3], "chan", 1)
    down.add(out_parts)
    total = ring_sum(after(run, down.made, out_run), grad_one_parts[3])
    out_total = ring_sum(after(out_run, total), out_parts[2])
    run = turned(total, "chan", 1)
    out_run = turned(out_total, "chan", 1)
    down.send(total)
    into.add(out_total)
    into.send()
    gate_up_grad = final_sums(
        [[(after(gate_up_mine, into.made), 0)], [(gate_up_mine, 1)]],
        False,
        (2, part, hidden_a.shape[2]),
    )
    run = after(run, gate_up_grad)
    out_total = ring_sum(after(out_run, gate_up_grad), out_parts[1])
    out_run = turned(out_total, "chan", 1)
    small = small + after(small_rec, out_total)
    if seq_count > 8:
        small = summed(small, "seq", 8)
    gains = small[: 2 * width]
    gains_rec = swapped(gains, "chan", 1)
    down_grad = final_sums(down.finish(out_total), True, (hidden_a.shape[2], part))
    gains = gains + after(gains_rec, down_grad)
    gains = gains + swapped(gains, "chan", 2)
    in_grad = triple_sums(into.finish(down_grad), (3, part, chan_cols))
    out_grad = out_run.astype(F32) + out_parts[0].astype(F32)

    grad_one_own = run.astype(F32) + grad_one_parts[0].astype(F32)
    input_grad = grad_state_own + norm_back(
        grad_one_own, tokens.astype(F32) * scale_all[:shard_rows], scale_all[:shard_rows], gain_one
    )
    block_output = (state_own + ((ffn_one.astype(F32) + ffn_two.astype(F32)) + (ffn_three.astype(F32) + ffn_parts[0].astype(F32)))).astype(BF)
    gains_grad = gains.reshape(2, width)
    conv_grad = small[2 * width :].reshape(3, chan_cols)
    return (
        block_output,
        input_grad,
        gains_grad,
        conv_grad,
        in_grad,
        out_grad,
        gate_up_grad,
        down_grad,
    )


def solution(mesh):
    placed = (
        P(("seq", "chan"), None),
        P(),
        P(None, "chan"),
        P(None, None, "chan"),
        P("chan", None),
        P(None, None, "chan"),
        P("chan", None),
        P(),
        P(("seq", "chan"), None),
    )
    return jax.shard_map(
        on_device,
        mesh=mesh,
        in_specs=placed,
        out_specs=(
            P(("seq", "chan"), None),
            P(("seq", "chan"), None),
            P(),
            P(None, "chan"),
            P(None, "seq", "chan"),
            P("chan", "seq"),
            P(None, "seq", "chan"),
            P("chan", "seq"),
        ),
        check_vma=False,
    )
```

```python
import functools

import jax
import jax.numpy as jnp
from jax import lax
from jax.experimental import pallas as pl
from jax.experimental.pallas import tpu as pltpu
from jax.sharding import PartitionSpec as P

EPS = 1e-05
BF = jnp.bfloat16
F32 = jnp.float32
MIB = 2**20
VMEM = 48


def params(mebibytes):
    return pltpu.CompilerParams(vmem_limit_bytes=mebibytes * MIB)


def cost():
    return pl.CostEstimate(flops=1024, bytes_accessed=1024, transcendentals=0)


def dot(a, b, dim_a, dim_b):
    return lax.dot_general(a, b, (((dim_a,), (dim_b,)), ((), ())), preferred_element_type=F32)


def after(value, *earlier):
    return lax.optimization_barrier((value,) + earlier)[0]


def passed_along(block, axis, distance):
    devices = range(lax.axis_size(axis))
    route = [(i - distance, i) for i in devices if i - distance in devices]
    return lax.ppermute(block, axis, route)


def turned(block, axis, distance):
    count = lax.axis_size(axis)
    return lax.ppermute(block, axis, [(i, (i + distance) % count) for i in range(count)])


def swapped(block, axis, bit):
    return lax.ppermute(block, axis, [(i, i ^ bit) for i in range(lax.axis_size(axis))])


def summed(block, axis, bit=1):
    while bit < lax.axis_size(axis):
        block = block + swapped(block, axis, bit)
        bit *= 2
    return block


def keep_masks(positions, starts):
    at_start = jnp.any(positions[..., None] == starts, axis=-1)
    prev_start = jnp.any((positions - 1)[..., None] == starts, axis=-1)
    keep_one = ((positions >= 1) & jnp.logical_not(at_start)).astype(F32)[..., None]
    keep_two = ((positions >= 2) & jnp.logical_not(at_start) & jnp.logical_not(prev_start)).astype(
        F32
    )[..., None]
    return (keep_one, keep_two)


def unit_rows(values):
    inv_scale = lax.rsqrt(jnp.mean(values * values, axis=-1, keepdims=True) + EPS)
    return (values * inv_scale, inv_scale)


def norm_back(grad_normed, unit_vals, inv_scale, gain_row):
    weighted = grad_normed * gain_row
    return inv_scale * (
        weighted - unit_vals * jnp.mean(weighted * unit_vals, axis=-1, keepdims=True)
    )


def group_bits():
    groups = lax.axis_size("seq") // 2
    bits = []
    while groups > 1:
        groups //= 2
        bits.append(groups)
    return bits


def ffn_body(count, ids, *refs):
    normed = refs[:count]
    cots = refs[count : 2 * count]
    gate_up_w, down_w = refs[2 * count : 2 * count + 2]
    outs = refs[2 * count + 2 :]
    hidden_ref, pair_ref = outs[:2]
    ffn_refs, grad_refs = outs[2 : 2 + count], outs[2 + count : 2 + 2 * count]
    normed_all, cot_all, ffn_acc, grad_acc = outs[2 + 2 * count :]
    step = pl.program_id(0)
    rows = normed[0].shape[0]

    @pl.when(step == 0)
    def _():
        for place in range(count):
            normed_all[pl.ds(place * rows, rows), :] = normed[place][...]
            cot_all[pl.ds(place * rows, rows), :] = cots[place][...]

    gate = dot(normed_all[...], gate_up_w[0], 1, 0)
    up = dot(normed_all[...], gate_up_w[1], 1, 0)
    grad_hidden = dot(cot_all[...], down_w[...], 1, 1)
    sig = jax.nn.sigmoid(gate)
    activated = gate * sig
    hidden = (activated * up).astype(BF)
    hidden_ref[0] = hidden
    grad_gate = (grad_hidden * up * sig * (1.0 + gate * (1.0 - sig))).astype(BF)
    grad_up = (grad_hidden * activated).astype(BF)
    pair_ref[0] = grad_gate
    pair_ref[1] = grad_up
    ffn_part = dot(hidden, down_w[...], 1, 0)
    grad_part = dot(grad_gate, gate_up_w[0], 1, 1) + dot(grad_up, gate_up_w[1], 1, 1)

    @pl.when(step == 0)
    def _():
        ffn_acc[...] = ffn_part
        grad_acc[...] = grad_part

    @pl.when(step > 0)
    def _():
        ffn_acc[...] += ffn_part
        grad_acc[...] += grad_part

    @pl.when(step == pl.num_programs(0) - 1)
    def _():
        for place in range(count):
            own = pl.ds(place * rows, rows)
            ffn_refs[place][...] = ffn_acc[own, :].astype(BF)
            grad_refs[place][...] = grad_acc[own, :].astype(BF)


def feed_forward(owner, normed, cots, gate_up_weight, down_weight, first, tile=512):
    count = len(normed)
    rows, width = normed[0].shape
    units = down_weight.shape[0]
    here = count * rows
    block = pl.BlockSpec((rows, width), lambda j, ids: (0, 0))
    results = pl.pallas_call(
        functools.partial(ffn_body, count),
        grid_spec=pltpu.PrefetchScalarGridSpec(
            num_scalar_prefetch=1,
            grid=(units // tile,),
            in_specs=[block] * count
            + [
                pl.BlockSpec((rows, width), lambda j, ids, r=first + r: (ids[r], 0))
                for r in range(count)
            ]
            + [
                pl.BlockSpec((2, width, tile), lambda j, ids: (0, 0, j)),
                pl.BlockSpec((tile, width), lambda j, ids: (j, 0)),
            ],
            out_specs=[
                pl.BlockSpec((1, here, tile), lambda j, ids: (0, 0, j)),
                pl.BlockSpec((2, here, tile), lambda j, ids: (0, 0, j)),
            ]
            + [block] * (2 * count),
            scratch_shapes=[
                pltpu.VMEM((here, width), BF),
                pltpu.VMEM((here, width), BF),
                pltpu.VMEM((here, width), F32),
                pltpu.VMEM((here, width), F32),
            ],
        ),
        out_shape=[
            jax.ShapeDtypeStruct((1, here, units), BF),
            jax.ShapeDtypeStruct((2, here, units), BF),
        ]
        + [jax.ShapeDtypeStruct((rows, width), BF)] * (2 * count),
        compiler_params=params(VMEM),
        cost_estimate=cost(),
        name="feed_forward",
    )(owner, *normed, *([cots] * count), gate_up_weight, down_weight)
    return results[0], results[1], results[2 : 2 + count], results[2 + count :]


def slices_body(count, groups, part, apart, ids, *refs):
    ins, outs = refs[:-2], refs[-2:]
    rows = outs[0].shape[0] // count
    for r in range(count):
        here = pl.ds(r * rows, rows)
        if apart:
            source, there = ins[r], slice(None)
        else:
            source = ins[0]
            there = pl.ds(pl.multiple_of(ids[2 * groups + r] * rows, rows), rows)
        for half in range(2):
            for slot in range(groups):
                start = pl.multiple_of(ids[half * groups + slot] * part, part)
                outs[half][here, slot * part : (slot + 1) * part] = source[
                    there, pl.ds(start, part)
                ]


def own_slices(blocks, owner=None, relative=True):
    seq = lax.axis_size("seq")
    groups = seq // 2
    place = lax.axis_index("seq")
    core, group = place % 2, place // 2
    chips = jnp.arange(groups, dtype=jnp.int32)
    if relative:
        chips = jnp.bitwise_xor(group, chips)
    mine, other = 2 * chips + core, 2 * chips + 1 - core
    apart = owner is None
    if apart:
        count = len(blocks)
        owner = jnp.zeros((count,), jnp.int32)
        rows = blocks[0].shape[0]
    else:
        count = owner.shape[0]
        rows = blocks.shape[0] // count
        blocks = [blocks]
    width = blocks[0].shape[1]
    part = width // seq
    if part % 128:
        if apart:
            full = jnp.concatenate(blocks, axis=0)
        else:
            full = jnp.concatenate(
                [
                    lax.dynamic_slice_in_dim(blocks[0], owner[r] * rows, rows, 0)
                    for r in range(count)
                ],
                axis=0,
            )
        full = full.reshape(count * rows, seq, part)
        picked = [
            jnp.take(full, ids, axis=1).reshape(count * rows, groups * part)
            for ids in (mine, other)
        ]
    else:
        ids = jnp.concatenate([mine, other, owner]).astype(jnp.int32)
        picked = pl.pallas_call(
            functools.partial(slices_body, count, groups, part, apart),
            in_specs=[pl.BlockSpec(memory_space=pltpu.SMEM)]
            + [pl.BlockSpec(memory_space=pltpu.VMEM)] * len(blocks),
            out_specs=[pl.BlockSpec(memory_space=pltpu.VMEM)] * 2,
            out_shape=[jax.ShapeDtypeStruct((count * rows, groups * part), BF)] * 2,
            compiler_params=params(VMEM),
            cost_estimate=cost(),
            name="own_slices",
        )(ids, *blocks)
    return picked[0], swapped(picked[1], "seq", 1)


def turn_rows(lhs, turned_lhs, part):
    for start in range(0, lhs.shape[1], part):
        columns = slice(start, start + part)
        turned_lhs[columns, :] = lhs[:, columns].astype(F32).T.astype(BF)


def wide_dot(turned_lhs, columns, units):
    total, start = None, 0
    for piece in units:
        end = start + piece.shape[1]
        part = dot(turned_lhs[columns, start:end], piece[0], 1, 0)
        total = part if total is None else total + part
        start = end
    return total


def tall_dot(lhs, units):
    total, start = None, 0
    for piece in units:
        end = start + piece.shape[1]
        part = dot(piece[0], lhs[start:end, :], 0, 0)
        total = part if total is None else total + part
        start = end
    return total


def product_body(slots, part, tiles, tall, pieces, *refs):
    own, rec = refs[:2]
    units_own, units_rec = refs[2 : 2 + pieces], refs[2 + pieces : 2 + 2 * pieces]
    outs = refs[2 + 2 * pieces : 6 + 2 * pieces]
    step = pl.program_id(0)
    if not tall:
        own_t, rec_t = refs[6 + 2 * pieces :]

        @pl.when(step == 0)
        def _():
            turn_rows(own, own_t, part)
            turn_rows(rec, rec_t, part)

    for half in range(2):

        @pl.when((step < tiles) if half == 0 else (step >= tiles))
        def _():
            if tall:
                total = tall_dot(own, units_own) + tall_dot(rec, units_rec)
            for kind in range(2):
                out = outs[2 * half + kind]
                for place, slot in enumerate(slots[half][kind]):
                    columns = slice(slot * part, (slot + 1) * part)
                    if tall:
                        out[place] = total[:, columns].astype(BF)
                    else:
                        out[place] = (
                            wide_dot(own_t, columns, units_own)
                            + wide_dot(rec_t, columns, units_rec)
                        ).astype(BF)


class Joined:
    def __init__(self, lhs, units, orders, part, tall=False):
        rows, slotted = lhs[0].shape
        groups = slotted // part
        kinds, _, wide = units[0][0].shape
        tile = next(t for t in (512, 256, 128) if (kinds * wide // 2) % t == 0 and wide % t == 0)
        each = wide // tile
        tiles = kinds * each // 2
        slots = tuple(self.slots(order) for order in orders)
        whole = pl.BlockSpec((rows, slotted), lambda j: (0, 0))
        columns = [
            pl.BlockSpec((1, piece.shape[1], tile), lambda j: (j // each, 0, j % each))
            for piece in (*units[0], *units[1])
        ]
        here = groups // 2
        shapes, specs = [], []
        for half in range(2):
            for kind in range(2):

                def at(j, half=half):
                    return (
                        jnp.minimum(j, tiles - 1) if half == 0 else jnp.maximum(j - tiles, 0)
                    )

                if tall:
                    shape, block = (here, tiles * tile, part), (here, tile, part)
                    specs.append(pl.BlockSpec(block, lambda j, at=at: (0, at(j), 0)))
                else:
                    shape, block = (here, part, tiles * tile), (here, part, tile)
                    specs.append(pl.BlockSpec(block, lambda j, at=at: (0, 0, at(j))))
                shapes.append(jax.ShapeDtypeStruct(shape, BF))
        outs = pl.pallas_call(
            functools.partial(product_body, slots, part, tiles, tall, len(units[0])),
            grid=(2 * tiles,),
            in_specs=[whole, whole, *columns],
            out_specs=specs,
            out_shape=shapes,
            scratch_shapes=[] if tall else [pltpu.VMEM((slotted, rows), BF)] * 2,
            compiler_params=params(58),
            cost_estimate=cost(),
            name="product",
        )(*lhs, *units[0], *units[1])
        self.orders, self.tall = orders, tall
        self.sent = [outs[0], outs[2]]
        self.kept = [[outs[1]], [outs[3]]]
        self.made = outs[0]
        self.done = 0

    def slots(self, order):
        slots = [0]
        for bit in reversed(order):
            slots = slots + [slot + bit for slot in slots]
        half = len(slots) // 2
        return tuple(slots[half:]), tuple(slots[:half])

    def send(self, *earlier):
        self.arrived = []
        for half in range(2):
            bit = 2 * self.orders[half][self.done]
            sent = after(self.sent[half], *earlier) if earlier else self.sent[half]
            arrived = swapped(sent, "seq", bit)
            self.arrived.append(arrived)
            self.kept[half].append(arrived)
        self.done += 1

    def add(self, *earlier):
        kept = [list(arrays) for arrays in self.kept]
        if earlier:
            kept[0][0] = after(kept[0][0], *earlier)
        left = len(self.orders[0]) - self.done
        self.sent = upper_sums(kept, 2 ** (left - 1))
        self.made = self.sent[0]

    def finish(self, *earlier):
        while self.done < len(self.orders[0]):
            self.add(*earlier)
            self.send()
        kept = [list(arrays) for arrays in self.kept]
        if earlier:
            kept[0][0] = after(kept[0][0], *earlier)
        return kept


def whole_body(part, pieces, own, rec, *refs):
    units_own, units_rec = refs[:pieces], refs[pieces : 2 * pieces]
    out, own_t, rec_t = refs[2 * pieces :]

    @pl.when(pl.program_id(0) == 0)
    def _():
        turn_rows(own, own_t, part)
        turn_rows(rec, rec_t, part)

    for slot in range(out.shape[0]):
        columns = slice(slot * part, (slot + 1) * part)
        out[slot, 0] = (
            wide_dot(own_t, columns, units_own) + wide_dot(rec_t, columns, units_rec)
        ).astype(BF)


def whole_product(lhs, units, part):
    rows, slotted = lhs[0].shape
    groups = slotted // part
    kinds, _, wide = units[0][0].shape
    tile = min(512, wide)
    each = wide // tile
    whole = pl.BlockSpec((rows, slotted), lambda j: (0, 0))
    columns = [
        pl.BlockSpec((1, piece.shape[1], tile), lambda j: (j // each, 0, j % each))
        for piece in (*units[0], *units[1])
    ]
    return pl.pallas_call(
        functools.partial(whole_body, part, len(units[0])),
        grid=(kinds * each,),
        in_specs=[whole, whole, *columns],
        out_specs=pl.BlockSpec(
            (groups, 1, part, tile), lambda j: (0, j // each, 0, j % each)
        ),
        out_shape=jax.ShapeDtypeStruct((groups, kinds, part, wide), BF),
        scratch_shapes=[pltpu.VMEM((slotted, rows), BF)] * 2,
        compiler_params=params(58),
        cost_estimate=cost(),
        name="whole_product",
    )(*lhs, *units[0], *units[1])


def plane_sum(products):
    groups = products.shape[0]
    flat = products.reshape(-1, products.shape[-1])
    members = [[2 * group + core for group in range(groups)] for core in range(2)]
    mine = lax.psum_scatter(
        flat, "seq", scatter_dimension=0, axis_index_groups=members, tiled=True
    )
    return mine.reshape(products.shape[1:])


def sums_body(counts, tiles, *refs):
    ins, outs = refs[: sum(counts)], refs[sum(counts) :]
    step = pl.program_id(0)
    start = 0
    for source, count in enumerate(counts):
        arrays = ins[start : start + count]
        start += count
        out = outs[source] if len(outs) > 1 else outs[0]

        @pl.when(step // tiles == source)
        def _():
            total = arrays[0][...].astype(F32)
            for array in arrays[1:]:
                total = total + array[...].astype(F32)
            out[...] = total.reshape(out.shape).astype(out.dtype)


def source_tile(step, source, tiles):
    return jnp.clip(step - source * tiles, 0, tiles - 1)


def upper_sums(sources, here):
    _, rows, columns = sources[0][0].shape
    tiles = 2
    block = (here, rows // tiles, columns)
    in_specs, arrays = [], []
    for source, parts in enumerate(sources):
        for array in parts:
            in_specs.append(
                pl.BlockSpec(block, lambda j, s=source: (1, source_tile(j, s, tiles), 0))
            )
            arrays.append(array)
    return pl.pallas_call(
        functools.partial(sums_body, [len(parts) for parts in sources], tiles),
        grid=(len(sources) * tiles,),
        in_specs=in_specs,
        out_specs=[
            pl.BlockSpec(block, lambda j, s=source: (0, source_tile(j, s, tiles), 0))
            for source in range(len(sources))
        ],
        out_shape=[jax.ShapeDtypeStruct((here, rows, columns), BF)] * len(sources),
        compiler_params=params(58),
        cost_estimate=cost(),
        name="upper_sums",
    )(*arrays)


def final_sums(sources, tall, shape):
    sources = [[part if isinstance(part, tuple) else (part, 0) for part in parts] for parts in sources]
    _, rows, columns = sources[0][0][0].shape
    if tall:
        tile = min(512, rows)
        tiles = rows // tile
        block, out_block = (1, tile, columns), (tile, columns)
        out_spec = pl.BlockSpec(out_block, lambda j: (j, 0))

        def at(j, s, slot):
            return (slot, source_tile(j, s, tiles), 0)
    else:
        tile = next(
            t for t in (2048, 1024, 512, 256, 128) if columns % t == 0 and shape[2] % t == 0
        )
        tiles = columns // tile
        each = shape[2] // tile
        block, out_block = (1, rows, tile), (1, rows, tile)
        out_spec = pl.BlockSpec(out_block, lambda j: (j // each, 0, j % each))

        def at(j, s, slot):
            return (slot, 0, source_tile(j, s, tiles))

    in_specs, arrays = [], []
    for source, parts in enumerate(sources):
        for array, slot in parts:
            in_specs.append(pl.BlockSpec(block, lambda j, s=source, slot=slot: at(j, s, slot)))
            arrays.append(array)
    return pl.pallas_call(
        functools.partial(sums_body, [len(parts) for parts in sources], tiles),
        grid=(len(sources) * tiles,),
        in_specs=in_specs,
        out_specs=out_spec,
        out_shape=jax.ShapeDtypeStruct(shape, F32),
        compiler_params=params(58),
        cost_estimate=cost(),
        name="final_sums",
    )(*arrays)


def triple_body(counts, *refs):
    out = refs[-1]
    kinds, _, wide = out.shape
    start = 0
    column = 0
    for count in counts:
        arrays = refs[start : start + count]
        start += count
        width = arrays[0].shape[2]
        done = 0
        while done < width:
            kind, at = column // wide, column % wide
            step = min(width - done, wide - at)
            total = arrays[0][0, :, done : done + step].astype(F32)
            for array in arrays[1:]:
                total = total + array[0, :, done : done + step].astype(F32)
            out[kind, :, at : at + step] = total
            done += step
            column += step


def triple_sums(sources, shape):
    arrays = [array for parts in sources for array in parts]
    return pl.pallas_call(
        functools.partial(triple_body, [len(parts) for parts in sources]),
        grid=(1,),
        in_specs=[
            pl.BlockSpec((1,) + array.shape[1:], lambda j: (0, 0, 0)) for array in arrays
        ],
        out_specs=pl.BlockSpec(shape, lambda j: (0, 0, 0)),
        out_shape=jax.ShapeDtypeStruct(shape, F32),
        compiler_params=params(VMEM),
        cost_estimate=cost(),
        name="triple_sums",
    )(*arrays)


def ring_body(a, b, out):
    out[...] = (a[...].astype(F32) + b[...].astype(F32)).astype(BF)


def ring_sum(arrived, own):
    rows, width = own.shape
    spec = pl.BlockSpec((rows // 2, width), lambda j: (j, 0))
    return pl.pallas_call(
        ring_body,
        grid=(2,),
        in_specs=[spec, spec],
        out_specs=spec,
        out_shape=jax.ShapeDtypeStruct((rows, width), BF),
        compiler_params=params(VMEM),
        cost_estimate=cost(),
        name="ring_sum",
    )(arrived, own)


def rows_body(count, rows, ids, gated, *refs):
    mixes, out, mix_all = refs[:count], refs[count], refs[count + 1]

    @pl.when(pl.program_id(0) == 0)
    def _():
        for place in range(count):
            there = pl.ds(pl.multiple_of(ids[place] * rows, rows), rows)
            mix_all[there, :] = mixes[place][...]

    out[0] = dot(gated[...], mix_all[...], 0, 0).astype(BF)


def rows_product(gated_plane, mixes, count):
    rows, part = mixes[0].shape
    chans = gated_plane.shape[1] // count
    ids = jnp.bitwise_xor(
        lax.axis_index("seq"), jnp.arange(len(mixes), dtype=jnp.int32)
    ).astype(jnp.int32)
    all_rows = rows * len(mixes)
    return pl.pallas_call(
        functools.partial(rows_body, len(mixes), rows),
        grid_spec=pltpu.PrefetchScalarGridSpec(
            num_scalar_prefetch=1,
            grid=(count,),
            in_specs=[pl.BlockSpec((all_rows, chans), lambda r, ids: (0, r))]
            + [pl.BlockSpec((rows, part), lambda r, ids: (0, 0))] * len(mixes),
            out_specs=pl.BlockSpec((1, chans, part), lambda r, ids: (r, 0, 0)),
            scratch_shapes=[pltpu.VMEM((all_rows, part), BF)],
        ),
        out_shape=jax.ShapeDtypeStruct((count, chans, part), BF),
        compiler_params=params(60),
        cost_estimate=cost(),
        name="rows_product",
    )(ids, gated_plane, *mixes)


def spread_body(slots, part, ids, rows_ref, *outs):
    for slot in range(slots):
        start = pl.multiple_of(ids[slot] * part, part)
        outs[slot][...] = rows_ref[:, pl.ds(start, part)]


def spread_slices(rows):
    seq = lax.axis_size("seq")
    part = rows.shape[1] // seq
    ids = jnp.bitwise_xor(lax.axis_index("seq"), jnp.arange(seq, dtype=jnp.int32))
    ids = ids.astype(jnp.int32)
    if part % 128:
        slices = [lax.dynamic_slice_in_dim(rows, ids[q] * part, part, 1) for q in range(seq)]
    else:
        slices = pl.pallas_call(
            functools.partial(spread_body, seq, part),
            in_specs=[
                pl.BlockSpec(memory_space=pltpu.SMEM),
                pl.BlockSpec(memory_space=pltpu.VMEM),
            ],
            out_specs=[pl.BlockSpec(memory_space=pltpu.VMEM)] * seq,
            out_shape=[jax.ShapeDtypeStruct((rows.shape[0], part), BF)] * seq,
            compiler_params=params(VMEM),
            cost_estimate=cost(),
            name="spread_slices",
        )(ids, rows)
    return slices


def project_body(count, *refs):
    toks = refs[:count]
    gain_ref, weights, first_ref, second_ref, third_ref, mixed, normed, scale_ref = refs[count:]
    rows = toks[0].shape[0]

    @pl.when(pl.program_id(0) == 0)
    def _():
        for place in range(count):
            here = pl.ds(place * rows, rows)
            values = toks[place][...].astype(F32)
            scale = lax.rsqrt(jnp.mean(values * values, axis=-1, keepdims=True) + EPS)
            normed[here, :] = (values * scale * gain_ref[...]).astype(BF)
            scale_ref[here, :] = scale

    first = dot(normed[...], weights[0], 1, 0)
    third = dot(normed[...], weights[2], 1, 0)
    first_ref[...] = first
    second_ref[...] = dot(normed[...], weights[1], 1, 0)
    third_ref[...] = third
    mixed[...] = (first * third).astype(BF)


def in_projection(toks, gain, weights, tile=256):
    count = len(toks)
    rows, width = toks[0].shape
    kinds, _, chans = weights.shape
    all_rows = count * rows
    block = pl.BlockSpec((rows, width), lambda j: (0, 0))
    return pl.pallas_call(
        functools.partial(project_body, count),
        grid=(chans // tile,),
        in_specs=[block] * count
        + [
            pl.BlockSpec((1, width), lambda j: (0, 0)),
            pl.BlockSpec((kinds, width, tile), lambda j: (0, 0, j)),
        ],
        out_specs=[
            *([pl.BlockSpec((all_rows, tile), lambda j: (0, j))] * (kinds + 1)),
            pl.BlockSpec((all_rows, width), lambda j: (0, 0)),
            pl.BlockSpec((all_rows, 1), lambda j: (0, 0)),
        ],
        out_shape=[
            *([jax.ShapeDtypeStruct((all_rows, chans), F32)] * kinds),
            jax.ShapeDtypeStruct((all_rows, chans), BF),
            jax.ShapeDtypeStruct((all_rows, width), BF),
            jax.ShapeDtypeStruct((all_rows, 1), F32),
        ],
        compiler_params=params(60),
        cost_estimate=cost(),
        name="in_projection",
    )(*toks, gain.reshape(1, width), weights)


def shifted(values, steps, edge):
    rows = values.shape[0]
    moved = pltpu.roll(values, steps % rows, 0)
    place = lax.broadcasted_iota(jnp.int32, values.shape, 0)
    for k in range(abs(steps)):
        at = k if steps > 0 else rows - 1 - k
        row = edge[k : k + 1] if steps > 0 else edge[abs(steps) - 1 - k : abs(steps) - k]
        moved = jnp.where(place == at, row, moved)
    return moved


def conv_body(count, second, mixed, before, taps, masks, conv_ref, *gated):
    rows = second.shape[0] // count
    for place in range(count):
        here = pl.ds(place * rows, rows)
        values = mixed[here, :].astype(F32)
        edge = before[place]
        lag_one = masks[here, 0:1] * shifted(values, 1, edge[1:2])
        lag_two = masks[here, 1:2] * shifted(values, 2, edge)
        conv = taps[0:1, :] * values + taps[1:2, :] * lag_one + taps[2:3, :] * lag_two
        conv_ref[here, :] = conv
        gated[place][...] = (second[here, :] * conv).astype(BF)


def conv_forward(second, mixed, before, taps, masks, count, tile=256):
    all_rows, chans = mixed.shape
    rows = all_rows // count
    wide = pl.BlockSpec((all_rows, tile), lambda j: (0, j))
    results = pl.pallas_call(
        functools.partial(conv_body, count),
        grid=(chans // tile,),
        in_specs=[
            wide,
            wide,
            pl.BlockSpec((count, 2, tile), lambda j: (0, 0, j)),
            pl.BlockSpec((3, tile), lambda j: (0, j)),
            pl.BlockSpec(masks.shape, lambda j: (0, 0)),
        ],
        out_specs=[wide] + [pl.BlockSpec((rows, tile), lambda j: (0, j))] * count,
        out_shape=[jax.ShapeDtypeStruct((all_rows, chans), F32)]
        + [jax.ShapeDtypeStruct((rows, chans), BF)] * count,
        compiler_params=params(60),
        cost_estimate=cost(),
        name="conv_forward",
    )(second, mixed, before, taps, masks)
    return results[0], results[1:]


def conv_back_body(count, *refs):
    grads = refs[:count]
    first, second, third, conv, mixed, before, behind, taps = refs[count : count + 8]
    masks, triple, tap_ref = refs[count + 8 :]
    rows = grads[0].shape[0]
    sums = [None] * 3
    for place in range(count):
        here = pl.ds(place * rows, rows)
        grad = grads[place][...].astype(F32)
        grad_conv = (grad * second[here, :]).astype(BF).astype(F32)
        edge = behind[place]
        grad_mixed = (
            taps[0:1, :] * grad_conv
            + taps[1:2, :] * masks[here, 2:3] * shifted(grad_conv, -1, edge[0:1])
            + taps[2:3, :] * masks[here, 3:4] * shifted(grad_conv, -2, edge)
        )
        triple[0, here, :] = (grad_mixed * third[here, :]).astype(BF)
        triple[1, here, :] = (grad * conv[here, :]).astype(BF)
        triple[2, here, :] = (grad_mixed * first[here, :]).astype(BF)
        values = mixed[here, :].astype(F32)
        lags = before[place]
        for tap, lagged in enumerate(
            (
                values,
                masks[here, 0:1] * shifted(values, 1, lags[1:2]),
                masks[here, 1:2] * shifted(values, 2, lags),
            )
        ):
            part = jnp.sum(grad_conv * lagged, axis=0, keepdims=True)
            sums[tap] = part if sums[tap] is None else sums[tap] + part
    tap_ref[...] = jnp.concatenate(sums, axis=0)


def conv_backward(grads, first, second, third, conv, mixed, before, behind, taps, masks, tile=128):
    count = len(grads)
    all_rows, chans = mixed.shape
    rows = all_rows // count
    wide = pl.BlockSpec((all_rows, tile), lambda j: (0, j))
    edge = pl.BlockSpec((count, 2, tile), lambda j: (0, 0, j))
    three = pl.BlockSpec((3, tile), lambda j: (0, j))
    return pl.pallas_call(
        functools.partial(conv_back_body, count),
        grid=(chans // tile,),
        in_specs=[pl.BlockSpec((rows, tile), lambda j: (0, j))] * count
        + [wide] * 5
        + [edge, edge, three]
        + [pl.BlockSpec(masks.shape, lambda j: (0, 0))],
        out_specs=[pl.BlockSpec((3, all_rows, tile), lambda j: (0, 0, j)), three],
        out_shape=[
            jax.ShapeDtypeStruct((3, all_rows, chans), BF),
            jax.ShapeDtypeStruct((3, chans), F32),
        ],
        compiler_params=params(60),
        cost_estimate=cost(),
        name="conv_backward",
    )(*grads, first, second, third, conv, mixed, before, behind, taps, masks)


def back_body(count, *refs):
    grads, weights = refs[:2]
    toks = refs[2 : 2 + count]
    scale_ref = refs[2 + count]
    outs = refs[3 + count : 3 + 2 * count]
    gains_ref = refs[3 + 2 * count]
    rows = toks[0].shape[0]
    total = dot(grads[0], weights[0], 1, 1)
    for kind in range(1, grads.shape[0]):
        total = total + dot(grads[kind], weights[kind], 1, 1)
    gains = None
    for place in range(count):
        here = total[place * rows : (place + 1) * rows]
        outs[place][...] = here.astype(BF)
        unit = toks[place][...].astype(F32) * scale_ref[pl.ds(place * rows, rows), :]
        part = jnp.sum(here * unit, axis=0, keepdims=True)
        gains = part if gains is None else gains + part
    gains_ref[...] = gains


def mixer_back(grads, weights, toks, scale, tile=512):
    kinds, all_rows, chans = grads.shape
    width = weights.shape[1]
    count = len(toks)
    rows = all_rows // count
    block = pl.BlockSpec((rows, tile), lambda j: (0, j))
    results = pl.pallas_call(
        functools.partial(back_body, count),
        grid=(width // tile,),
        in_specs=[
            pl.BlockSpec((kinds, all_rows, chans), lambda j: (0, 0, 0)),
            pl.BlockSpec((kinds, tile, chans), lambda j: (0, j, 0)),
        ]
        + [block] * count
        + [pl.BlockSpec((all_rows, 1), lambda j: (0, 0))],
        out_specs=[block] * count + [pl.BlockSpec((1, tile), lambda j: (0, j))],
        out_shape=[jax.ShapeDtypeStruct((rows, width), BF)] * count
        + [jax.ShapeDtypeStruct((1, width), F32)],
        compiler_params=params(60),
        cost_estimate=cost(),
        name="mixer_back",
    )(grads, weights, *toks, scale)
    return results[:count], results[count][0]


def full_others(others):
    seq = lax.axis_size("seq")
    stacked = jnp.stack(others, axis=1)
    stacked = stacked.reshape((seq,) + stacked.shape[2:])
    slots = jnp.bitwise_xor(lax.axis_index("seq"), jnp.arange(seq, dtype=jnp.int32))
    full = jnp.transpose(jnp.take(stacked, slots, axis=0), (1, 2, 0, 3))
    return full.reshape(full.shape[:2] + (-1,))


def plane_ids():
    place = lax.axis_index("seq")
    groups = lax.axis_size("seq") // 2
    chips = jnp.bitwise_xor(place // 2, jnp.arange(groups, dtype=jnp.int32))
    return jnp.concatenate([chips, (place % 2)[None]]).astype(jnp.int32)


def core_columns(ids, groups, kind, part, base=0):
    core = ids[groups]
    offset = jnp.where(core == kind, 0, part)
    return pl.ds(pl.multiple_of(base + offset, part), part)


def mixer_body(count, ids, *refs):
    gated = refs[:count]
    own_w, same_w, cross_w, rows_ref, gain_ref = refs[count : count + 5]
    state_ref, normed_ref, scale_ref, joined_ref = refs[count + 5 :]
    step = pl.program_id(0)
    part = same_w.shape[3]
    groups = pl.num_programs(0)
    base = pl.multiple_of(step * 2 * part, 2 * part)
    for kind, other_w in enumerate((same_w, cross_w)):
        inner = core_columns(ids, groups, kind, part)
        total = dot(gated[0][...], own_w[:, inner], 1, 0)
        for place in range(1, count):
            total = total + dot(gated[place][...], other_w[0, count - 1 - place], 1, 0)
        columns = core_columns(ids, groups, kind, part, base)
        state_ref[:, columns] = total + rows_ref[:, columns].astype(F32)

    @pl.when(step == groups - 1)
    def _():
        state = state_ref[...]
        scale = lax.rsqrt(jnp.mean(state * state, axis=-1, keepdims=True) + EPS)
        normed_ref[...] = (state * scale * gain_ref[...]).astype(BF)
        scale_ref[...] = scale
        chans = gated[0].shape[1]
        for place in range(count):
            joined_ref[:, place * chans : (place + 1) * chans] = gated[place][...]


def mixer_rows(gated, own_w, others, input_rows, gain):
    count = len(gated)
    rows, width = input_rows.shape
    chans = gated[0].shape[1]
    groups, _, _, part = others[0].shape
    if part % 128:
        full = full_others(others)
        total = dot(gated[0], own_w, 1, 0)
        for r in range(1, count):
            total = total + dot(gated[r], full[count - 1 - r], 1, 0)
        state = input_rows.astype(F32) + total
        unit, scale = unit_rows(state)
        return state, (unit * gain).astype(BF), scale, jnp.concatenate(gated, axis=1)
    full_rows = pl.BlockSpec((rows, width), lambda t, ids: (0, 0))
    weights = pl.BlockSpec((1, count - 1, chans, part), lambda t, ids: (ids[t], 0, 0, 0))
    return pl.pallas_call(
        functools.partial(mixer_body, count),
        grid_spec=pltpu.PrefetchScalarGridSpec(
            num_scalar_prefetch=1,
            grid=(groups,),
            in_specs=[pl.BlockSpec((rows, chans), lambda t, ids: (0, 0))] * count
            + [
                pl.BlockSpec((chans, 2 * part), lambda t, ids: (0, t)),
                weights,
                weights,
                full_rows,
                pl.BlockSpec((1, width), lambda t, ids: (0, 0)),
            ],
            out_specs=[
                full_rows,
                full_rows,
                pl.BlockSpec((rows, 1), lambda t, ids: (0, 0)),
                pl.BlockSpec((rows, count * chans), lambda t, ids: (0, 0)),
            ],
        ),
        out_shape=[
            jax.ShapeDtypeStruct((rows, width), F32),
            jax.ShapeDtypeStruct((rows, width), BF),
            jax.ShapeDtypeStruct((rows, 1), F32),
            jax.ShapeDtypeStruct((rows, count * chans), BF),
        ],
        compiler_params=params(VMEM),
        cost_estimate=cost(),
        name="mixer_rows",
    )(plane_ids(), *gated, own_w, *others, input_rows, gain.reshape(1, width))


def gated_body(count, ids, *refs):
    own_w, same_w, cross_w, arrived, part_own, state_ref, scale_ref, cot_ref, gain_ref = refs[:9]
    outs = refs[9 : 9 + count]
    grad_ref, mix_ref, gains_ref = refs[9 + count : 12 + count]
    accs = refs[12 + count :]
    step = pl.program_id(0)
    part = same_w.shape[3]
    groups = pl.num_programs(0)

    @pl.when(step == 0)
    def _():
        grad_normed = arrived[...].astype(F32) + part_own[...].astype(F32)
        unit = state_ref[...] * scale_ref[...]
        weighted = grad_normed * gain_ref[...]
        grad = cot_ref[...].astype(F32) + scale_ref[...] * (
            weighted - unit * jnp.mean(weighted * unit, axis=-1, keepdims=True)
        )
        grad_ref[...] = grad
        mix_ref[...] = grad.astype(BF)
        gains_ref[...] = jnp.sum(grad_normed * unit, axis=0, keepdims=True)
        for acc in accs:
            acc[...] = jnp.zeros_like(acc)

    base = pl.multiple_of(step * 2 * part, 2 * part)
    mix = [
        mix_ref[:, core_columns(ids, groups, kind, part, base)] for kind in range(2)
    ]
    accs[0][...] += dot(mix_ref[:, pl.ds(base, 2 * part)], own_w[...], 1, 1)
    for place in range(1, count):
        accs[place][...] += dot(mix[0], same_w[0, count - 1 - place], 1, 1) + dot(
            mix[1], cross_w[0, count - 1 - place], 1, 1
        )

    @pl.when(step == groups - 1)
    def _():
        for out, acc in zip(outs, accs):
            out[...] = acc[...].astype(BF)


def gated_rows(arrived, part_own, state, scale, cot, gain, own_w, others):
    rows, width = state.shape
    chans = own_w.shape[0]
    groups, less, _, part = others[0].shape
    count = less + 1
    if part % 128:
        full = full_others(others)
        grad_normed = arrived.astype(F32) + part_own.astype(F32)
        unit = state * scale
        grad = cot.astype(F32) + norm_back(grad_normed, unit, scale, gain)
        mix = grad.astype(BF)
        outs = [dot(mix, own_w, 1, 1).astype(BF)] + [
            dot(mix, full[count - 1 - r], 1, 1).astype(BF) for r in range(1, count)
        ]
        return outs, grad, mix, jnp.sum(grad_normed * unit, axis=0)
    full_rows = pl.BlockSpec((rows, width), lambda t, ids: (0, 0))
    one_row = pl.BlockSpec((1, width), lambda t, ids: (0, 0))
    weights = pl.BlockSpec((1, less, chans, part), lambda t, ids: (ids[t], 0, 0, 0))
    results = pl.pallas_call(
        functools.partial(gated_body, count),
        grid_spec=pltpu.PrefetchScalarGridSpec(
            num_scalar_prefetch=1,
            grid=(groups,),
            in_specs=[
                pl.BlockSpec((chans, 2 * part), lambda t, ids: (0, t)),
                weights,
                weights,
                full_rows,
                full_rows,
                full_rows,
                pl.BlockSpec((rows, 1), lambda t, ids: (0, 0)),
                full_rows,
                one_row,
            ],
            out_specs=[pl.BlockSpec((rows, chans), lambda t, ids: (0, 0))] * count
            + [full_rows, full_rows, one_row],
            scratch_shapes=[pltpu.VMEM((rows, chans), F32)] * count,
        ),
        out_shape=[jax.ShapeDtypeStruct((rows, chans), BF)] * count
        + [
            jax.ShapeDtypeStruct((rows, width), F32),
            jax.ShapeDtypeStruct((rows, width), BF),
            jax.ShapeDtypeStruct((1, width), F32),
        ],
        compiler_params=params(60),
        cost_estimate=cost(),
        name="gated_rows",
    )(plane_ids(), own_w, *others, arrived, part_own, state, scale, cot, gain.reshape(1, width))
    return results[:count], results[count], results[count + 1], results[count + 2][0]


def on_device(
    tokens,
    norm_gains,
    conv_weight,
    in_weight,
    out_weight,
    gate_up_weight,
    down_weight,
    starts,
    cotangent,
):
    shard_rows, width = tokens.shape
    chan_count = lax.axis_size("chan")
    seq_count = lax.axis_size("seq")
    seq_rows = shard_rows * chan_count
    chan_cols = conv_weight.shape[1]
    chan_index = lax.axis_index("chan")
    seq_index = lax.axis_index("seq")
    relative = jnp.arange(chan_count, dtype=jnp.int32)
    owner = (chan_index - relative) % chan_count
    positions = (
        seq_index * seq_rows
        + owner[:, None] * shard_rows
        + jnp.arange(shard_rows, dtype=jnp.int32)[None, :]
    )
    keep_one, keep_two = keep_masks(positions, starts)
    next_one, unused_one = keep_masks(positions + 1, starts)
    unused_two, next_two = keep_masks(positions + 2, starts)
    gain_one = norm_gains[0].astype(F32)
    gain_two = norm_gains[1].astype(F32)
    conv_taps = conv_weight.astype(F32)
    bits = group_bits()
    orders = (bits[::-1], bits)

    part = width // seq_count
    w_own = lax.dynamic_slice_in_dim(out_weight, seq_index * part, part, 1)
    w_one = turned(w_own, "chan", 1)
    w_three = turned(w_own, "chan", 3)
    tok_one = turned(tokens, "chan", 1)
    w_two = turned(after(w_one, w_three, tok_one), "chan", 1)
    tok_three = turned(after(tokens, w_three, tok_one), "chan", 3)
    others = jnp.stack([w_one, w_two, w_three])[None]
    halves = [others[:, :, : chan_cols // 2], others[:, :, chan_cols // 2 :]]
    first_arrived = [
        swapped(half, "seq", 2 * order[0]) for half, order in zip(halves, orders)
    ]
    tok_two = turned(after(tok_one, w_two), "chan", 1)
    second_arrived = []
    for place, order in enumerate(orders):
        held = jnp.concatenate(
            [halves[place], after(first_arrived[place], tok_three)], axis=0
        )
        for bit in order[1:-1]:
            held = jnp.concatenate([held, swapped(held, "seq", 2 * bit)], axis=0)
        halves[place] = held
        second_arrived.append(swapped(held, "seq", 2 * order[-1]))
    grad_out = lax.all_gather(after(cotangent, tok_three), "chan", axis=0, tiled=True)
    tok_blocks = [tokens, tok_one, tok_two, tok_three]
    for place, order in enumerate(orders):
        held = jnp.concatenate([halves[place], after(second_arrived[place], tok_two)], axis=0)
        split = held.reshape((2,) * len(order) + held.shape[1:])
        axes = [len(order) - 1 - order.index(bit) for bit in bits]
        held = jnp.transpose(split, (*axes, *range(len(order), split.ndim))).reshape(held.shape)
        halves[place] = held
    held = jnp.concatenate(halves, axis=2)
    others = (held, swapped(held, "seq", 1))
    masks = jnp.concatenate(
        [
            mask.reshape(seq_rows, 1)
            for mask in (keep_one, keep_two, next_one, next_two)
        ]
        + [jnp.zeros((seq_rows, 124), F32)],
        axis=1,
    )
    *projected, mixed_in, normed_one, scale_all = in_projection(
        [after(tokens, held, masks)] + tok_blocks[1:], gain_one, in_weight
    )

    def at_edge(edge_rows, device):
        return lax.dynamic_index_in_dim(edge_rows, (chan_index - device) % chan_count, 0, False)

    def is_owner(device):
        return (owner == device)[:, None, None]

    ends = jnp.stack(
        [mixed_in[(r + 1) * shard_rows - 2 : (r + 1) * shard_rows] for r in range(chan_count)]
    )
    rim_rows = passed_along(at_edge(ends, chan_count - 1), "seq", 1)
    before = jnp.where(is_owner(0), rim_rows[None], jnp.roll(ends, -1, axis=0)).astype(F32)
    conv_out, gated_mix = conv_forward(
        projected[1], mixed_in, before, conv_taps, masks, chan_count
    )
    gated_mix = [after(rows, grad_out) for rows in gated_mix]
    gated_rows_own = [gated_mix[0]] + [
        turned(gated_mix[r], "chan", -r) for r in range(1, chan_count)
    ]
    state_own, normed_two_own, scale_two, gated_joined = mixer_rows(
        gated_rows_own, out_weight, others, tokens, gain_two
    )
    n_one = turned(normed_two_own, "chan", 1)
    normed_one_slices = own_slices(
        after(normed_one, normed_two_own), jnp.arange(chan_count, dtype=jnp.int32)
    )
    cot_slices = own_slices(after(grad_out, normed_two_own), owner)
    n_one = after(n_one, normed_one_slices[0], cot_slices[0])
    gated_plane = lax.all_gather(
        after(gated_joined, n_one),
        "seq",
        axis=0,
        tiled=True,
    )
    n_two = turned(n_one, "chan", 1)
    n_three = turned(after(normed_two_own, n_one), "chan", 3)
    hidden_a, pair_a, ffn_parts, grad_two_parts = feed_forward(
        owner,
        [normed_two_own, n_one],
        grad_out,
        gate_up_weight,
        down_weight,
        0,
    )
    ffn_parts, grad_two_parts, hidden_a, pair_a = [
        after(value, n_two, n_three)
        if not isinstance(value, (list, tuple))
        else [after(one, n_two, n_three) for one in value]
        for value in (ffn_parts, grad_two_parts, hidden_a, pair_a)
    ]
    run = turned(grad_two_parts[1], "chan", 1)
    ffn_one = turned(ffn_parts[1], "chan", -1)
    hidden_a_rec = swapped(hidden_a, "seq", 1)
    pair_a_rec = swapped(pair_a, "seq", 1)
    hidden_b, pair_b, ffn_more, grad_more = feed_forward(
        owner,
        [n_two, n_three],
        grad_out,
        gate_up_weight,
        down_weight,
        2,
    )
    ffn_parts = list(ffn_parts) + list(ffn_more)
    grad_two_parts = list(grad_two_parts) + list(grad_more)

    total = ring_sum(run, grad_two_parts[2])
    hidden_b, pair_b = [
        after(units, total, ffn_one, hidden_a_rec, pair_a_rec) for units in (hidden_b, pair_b)
    ]
    hidden_b_rec = swapped(hidden_b, "seq", 1)
    pair_b_rec = swapped(after(pair_b, hidden_b_rec), "seq", 1)
    run = turned(total, "chan", 1)
    down = Joined(
        (after(cot_slices[0], total), cot_slices[1]),
        ([hidden_a, hidden_b], [hidden_a_rec, hidden_b_rec]),
        orders,
        part,
        tall=True,
    )
    normed_two_slices = own_slices(
        [normed_two_own, n_one, n_two, after(n_three, down.made)], None, False
    )
    total = ring_sum(after(run, normed_two_slices[0]), grad_two_parts[3])
    down.send()
    run = turned(total, "chan", 1)
    gate_up = whole_product(
        (after(normed_two_slices[0], total), normed_two_slices[1]),
        ([pair_a, pair_b], [pair_a_rec, pair_b_rec]),
        part,
    )
    run = after(run, gate_up, *down.arrived)
    gate_up_mine = plane_sum(after(gate_up, gated_plane, run))
    ffn_two = turned(after(ffn_parts[2], run), "chan", -1)

    grad_gated_rows, grad_state_own, grad_mix_own, gain_two_part = gated_rows(
        run,
        grad_two_parts[0],
        state_own,
        scale_two,
        cotangent,
        gain_two,
        out_weight,
        others,
    )
    grad_gated_rows = list(grad_gated_rows)
    grad_gated_rows[1:] = [
        after(rows, ffn_two) for rows in grad_gated_rows[1:]
    ]
    gg = [grad_gated_rows[0]] + [
        turned(grad_gated_rows[r], "chan", r) for r in range(1, chan_count)
    ]
    mixes = spread_slices(after(grad_mix_own, *grad_gated_rows[1:]))
    mixes = [mixes[0]] + [swapped(mixes[q], "seq", q) for q in range(1, seq_count)]
    ffn_two = turned(after(ffn_two, *gg), "chan", -1)
    ffn_three = turned(after(ffn_parts[3], *gg), "chan", -3)
    heads = jnp.stack(
        [
            (
                gg[r][:2].astype(F32) * projected[1][r * shard_rows : r * shard_rows + 2]
            ).astype(BF)
            for r in range(chan_count)
        ]
    )
    rim_back = passed_along(at_edge(heads, 0), "seq", -1)
    behind = jnp.where(is_owner(chan_count - 1), rim_back[None], jnp.roll(heads, 1, axis=0))
    grad_triple, tap_part = conv_backward(
        gg, *projected, conv_out, mixed_in, before, after(behind.astype(F32), *mixes), conv_taps, masks
    )
    grad_one_parts, gain_one_part = mixer_back(grad_triple, in_weight, tok_blocks, scale_all)
    grad_one_parts = [after(rows, ffn_two, ffn_three) for rows in grad_one_parts]
    run = turned(grad_one_parts[1], "chan", 1)
    small = after(
        jnp.concatenate([gain_one_part, gain_two_part, tap_part.reshape(-1)]), grad_one_parts[1]
    )
    small_rec = swapped(small, "seq", 1)
    triple_rec = swapped(after(grad_triple, grad_one_parts[1]), "seq", 1)
    into = Joined(
        (after(normed_one_slices[0], grad_one_parts[1]), normed_one_slices[1]),
        ([grad_triple], [triple_rec]),
        orders,
        part,
    )
    small = small + small_rec
    small_rec = swapped(small, "seq", 2)
    small = small + after(small_rec, into.made)
    into.send(small)
    total = ring_sum(after(run, small), grad_one_parts[2])
    run = turned(total, "chan", 1)
    small_rec = swapped(after(small, total), "seq", 4)
    out_parts = rows_product(after(gated_plane, total), mixes, chan_count)
    out_run = turned(out_parts[3], "chan", 1)
    down.add(out_parts)
    total = ring_sum(after(run, down.made, out_run), grad_one_parts[3])
    out_total = ring_sum(after(out_run, total), out_parts[2])
    run = turned(total, "chan", 1)
    out_run = turned(out_total, "chan", 1)
    down.send(total)
    into.add(out_total)
    into.send()
    gate_up_grad = final_sums(
        [[(after(gate_up_mine, into.made), 0)], [(gate_up_mine, 1)]],
        False,
        (2, part, hidden_a.shape[2]),
    )
    run = after(run, gate_up_grad)
    out_total = ring_sum(after(out_run, gate_up_grad), out_parts[1])
    out_run = turned(out_total, "chan", 1)
    small = small + after(small_rec, out_total)
    if seq_count > 8:
        small = summed(small, "seq", 8)
    gains = small[: 2 * width]
    gains_rec = swapped(gains, "chan", 1)
    down_grad = final_sums(down.finish(out_total), True, (hidden_a.shape[2], part))
    gains = gains + after(gains_rec, down_grad)
    gains = gains + swapped(gains, "chan", 2)
    in_grad = triple_sums(into.finish(down_grad), (3, part, chan_cols))
    out_grad = out_run.astype(F32) + out_parts[0].astype(F32)

    grad_one_own = run.astype(F32) + grad_one_parts[0].astype(F32)
    input_grad = grad_state_own + norm_back(
        grad_one_own, tokens.astype(F32) * scale_all[:shard_rows], scale_all[:shard_rows], gain_one
    )
    block_output = (state_own + ((ffn_one.astype(F32) + ffn_two.astype(F32)) + (ffn_three.astype(F32) + ffn_parts[0].astype(F32)))).astype(BF)
    gains_grad = gains.reshape(2, width)
    conv_grad = small[2 * width :].reshape(3, chan_cols)
    return (
        block_output,
        input_grad,
        gains_grad,
        conv_grad,
        in_grad,
        out_grad,
        gate_up_grad,
        down_grad,
    )


def solution(mesh):
    placed = (
        P(("seq", "chan"), None),
        P(),
        P(None, "chan"),
        P(None, None, "chan"),
        P("chan", None),
        P(None, None, "chan"),
        P("chan", None),
        P(),
        P(("seq", "chan"), None),
    )
    return jax.shard_map(
        on_device,
        mesh=mesh,
        in_specs=placed,
        out_specs=(
            P(("seq", "chan"), None),
            P(("seq", "chan"), None),
            P(),
            P(None, "chan"),
            P(None, "seq", "chan"),
            P("chan", "seq"),
            P(None, "seq", "chan"),
            P("chan", "seq"),
        ),
        check_vma=False,
    )
```

```python
import functools

import jax
import jax.numpy as jnp
from jax import lax
from jax.experimental import pallas as pl
from jax.experimental.pallas import tpu as pltpu
from jax.sharding import PartitionSpec as P

EPS = 1e-05
BF = jnp.bfloat16
F32 = jnp.float32
MIB = 2**20
VMEM = 48


def params(mebibytes):
    return pltpu.CompilerParams(vmem_limit_bytes=mebibytes * MIB)


def cost():
    return pl.CostEstimate(flops=1024, bytes_accessed=1024, transcendentals=0)


def dot(a, b, dim_a, dim_b):
    return lax.dot_general(a, b, (((dim_a,), (dim_b,)), ((), ())), preferred_element_type=F32)


def after(value, *earlier):
    return lax.optimization_barrier((value,) + earlier)[0]


def passed_along(block, axis, distance):
    devices = range(lax.axis_size(axis))
    route = [(i - distance, i) for i in devices if i - distance in devices]
    return lax.ppermute(block, axis, route)


def turned(block, axis, distance):
    count = lax.axis_size(axis)
    return lax.ppermute(block, axis, [(i, (i + distance) % count) for i in range(count)])


def swapped(block, axis, bit):
    return lax.ppermute(block, axis, [(i, i ^ bit) for i in range(lax.axis_size(axis))])


def summed(block, axis, bit=1):
    while bit < lax.axis_size(axis):
        block = block + swapped(block, axis, bit)
        bit *= 2
    return block


def keep_masks(positions, starts):
    at_start = jnp.any(positions[..., None] == starts, axis=-1)
    prev_start = jnp.any((positions - 1)[..., None] == starts, axis=-1)
    keep_one = ((positions >= 1) & jnp.logical_not(at_start)).astype(F32)[..., None]
    keep_two = ((positions >= 2) & jnp.logical_not(at_start) & jnp.logical_not(prev_start)).astype(
        F32
    )[..., None]
    return (keep_one, keep_two)


def unit_rows(values):
    inv_scale = lax.rsqrt(jnp.mean(values * values, axis=-1, keepdims=True) + EPS)
    return (values * inv_scale, inv_scale)


def norm_back(grad_normed, unit_vals, inv_scale, gain_row):
    weighted = grad_normed * gain_row
    return inv_scale * (
        weighted - unit_vals * jnp.mean(weighted * unit_vals, axis=-1, keepdims=True)
    )


def group_bits():
    groups = lax.axis_size("seq") // 2
    bits = []
    while groups > 1:
        groups //= 2
        bits.append(groups)
    return bits


def ffn_body(count, ids, *refs):
    normed = refs[:count]
    cots = refs[count : 2 * count]
    gate_up_w, down_w = refs[2 * count : 2 * count + 2]
    outs = refs[2 * count + 2 :]
    hidden_ref, pair_ref = outs[:2]
    ffn_refs, grad_refs = outs[2 : 2 + count], outs[2 + count : 2 + 2 * count]
    normed_all, cot_all, ffn_acc, grad_acc = outs[2 + 2 * count :]
    step = pl.program_id(0)
    rows = normed[0].shape[0]

    @pl.when(step == 0)
    def _():
        for place in range(count):
            normed_all[pl.ds(place * rows, rows), :] = normed[place][...]
            cot_all[pl.ds(place * rows, rows), :] = cots[place][...]

    gate = dot(normed_all[...], gate_up_w[0], 1, 0)
    up = dot(normed_all[...], gate_up_w[1], 1, 0)
    grad_hidden = dot(cot_all[...], down_w[...], 1, 1)
    sig = jax.nn.sigmoid(gate)
    activated = gate * sig
    hidden = (activated * up).astype(BF)
    hidden_ref[0] = hidden
    grad_gate = (grad_hidden * up * sig * (1.0 + gate * (1.0 - sig))).astype(BF)
    grad_up = (grad_hidden * activated).astype(BF)
    pair_ref[0] = grad_gate
    pair_ref[1] = grad_up
    ffn_part = dot(hidden, down_w[...], 1, 0)
    grad_part = dot(grad_gate, gate_up_w[0], 1, 1) + dot(grad_up, gate_up_w[1], 1, 1)

    @pl.when(step == 0)
    def _():
        ffn_acc[...] = ffn_part
        grad_acc[...] = grad_part

    @pl.when(step > 0)
    def _():
        ffn_acc[...] += ffn_part
        grad_acc[...] += grad_part

    @pl.when(step == pl.num_programs(0) - 1)
    def _():
        for place in range(count):
            own = pl.ds(place * rows, rows)
            ffn_refs[place][...] = ffn_acc[own, :].astype(BF)
            grad_refs[place][...] = grad_acc[own, :].astype(BF)


def feed_forward(owner, normed, cots, gate_up_weight, down_weight, first, tile=512):
    count = len(normed)
    rows, width = normed[0].shape
    units = down_weight.shape[0]
    here = count * rows
    block = pl.BlockSpec((rows, width), lambda j, ids: (0, 0))
    results = pl.pallas_call(
        functools.partial(ffn_body, count),
        grid_spec=pltpu.PrefetchScalarGridSpec(
            num_scalar_prefetch=1,
            grid=(units // tile,),
            in_specs=[block] * count
            + [
                pl.BlockSpec((rows, width), lambda j, ids, r=first + r: (ids[r], 0))
                for r in range(count)
            ]
            + [
                pl.BlockSpec((2, width, tile), lambda j, ids: (0, 0, j)),
                pl.BlockSpec((tile, width), lambda j, ids: (j, 0)),
            ],
            out_specs=[
                pl.BlockSpec((1, here, tile), lambda j, ids: (0, 0, j)),
                pl.BlockSpec((2, here, tile), lambda j, ids: (0, 0, j)),
            ]
            + [block] * (2 * count),
            scratch_shapes=[
                pltpu.VMEM((here, width), BF),
                pltpu.VMEM((here, width), BF),
                pltpu.VMEM((here, width), F32),
                pltpu.VMEM((here, width), F32),
            ],
        ),
        out_shape=[
            jax.ShapeDtypeStruct((1, here, units), BF),
            jax.ShapeDtypeStruct((2, here, units), BF),
        ]
        + [jax.ShapeDtypeStruct((rows, width), BF)] * (2 * count),
        compiler_params=params(VMEM),
        cost_estimate=cost(),
        name="feed_forward",
    )(owner, *normed, *([cots] * count), gate_up_weight, down_weight)
    return results[0], results[1], results[2 : 2 + count], results[2 + count :]


def slices_body(count, groups, part, apart, ids, *refs):
    ins, outs = refs[:-2], refs[-2:]
    rows = outs[0].shape[0] // count
    for r in range(count):
        here = pl.ds(r * rows, rows)
        if apart:
            source, there = ins[r], slice(None)
        else:
            source = ins[0]
            there = pl.ds(pl.multiple_of(ids[2 * groups + r] * rows, rows), rows)
        for half in range(2):
            for slot in range(groups):
                start = pl.multiple_of(ids[half * groups + slot] * part, part)
                outs[half][here, slot * part : (slot + 1) * part] = source[
                    there, pl.ds(start, part)
                ]


def own_slices(blocks, owner=None, relative=True):
    seq = lax.axis_size("seq")
    groups = seq // 2
    place = lax.axis_index("seq")
    core, group = place % 2, place // 2
    chips = jnp.arange(groups, dtype=jnp.int32)
    if relative:
        chips = jnp.bitwise_xor(group, chips)
    mine, other = 2 * chips + core, 2 * chips + 1 - core
    apart = owner is None
    if apart:
        count = len(blocks)
        owner = jnp.zeros((count,), jnp.int32)
        rows = blocks[0].shape[0]
    else:
        count = owner.shape[0]
        rows = blocks.shape[0] // count
        blocks = [blocks]
    width = blocks[0].shape[1]
    part = width // seq
    if part % 128:
        if apart:
            full = jnp.concatenate(blocks, axis=0)
        else:
            full = jnp.concatenate(
                [
                    lax.dynamic_slice_in_dim(blocks[0], owner[r] * rows, rows, 0)
                    for r in range(count)
                ],
                axis=0,
            )
        full = full.reshape(count * rows, seq, part)
        picked = [
            jnp.take(full, ids, axis=1).reshape(count * rows, groups * part)
            for ids in (mine, other)
        ]
    else:
        ids = jnp.concatenate([mine, other, owner]).astype(jnp.int32)
        picked = pl.pallas_call(
            functools.partial(slices_body, count, groups, part, apart),
            in_specs=[pl.BlockSpec(memory_space=pltpu.SMEM)]
            + [pl.BlockSpec(memory_space=pltpu.VMEM)] * len(blocks),
            out_specs=[pl.BlockSpec(memory_space=pltpu.VMEM)] * 2,
            out_shape=[jax.ShapeDtypeStruct((count * rows, groups * part), BF)] * 2,
            compiler_params=params(VMEM),
            cost_estimate=cost(),
            name="own_slices",
        )(ids, *blocks)
    return picked[0], swapped(picked[1], "seq", 1)


def turn_rows(lhs, turned_lhs, part):
    for start in range(0, lhs.shape[1], part):
        columns = slice(start, start + part)
        turned_lhs[columns, :] = lhs[:, columns].astype(F32).T.astype(BF)


def wide_dot(turned_lhs, columns, units):
    total, start = None, 0
    for piece in units:
        end = start + piece.shape[1]
        part = dot(turned_lhs[columns, start:end], piece[0], 1, 0)
        total = part if total is None else total + part
        start = end
    return total


def tall_dot(lhs, units):
    total, start = None, 0
    for piece in units:
        end = start + piece.shape[1]
        part = dot(piece[0], lhs[start:end, :], 0, 0)
        total = part if total is None else total + part
        start = end
    return total


def product_body(slots, part, tiles, tall, pieces, *refs):
    own, rec = refs[:2]
    units_own, units_rec = refs[2 : 2 + pieces], refs[2 + pieces : 2 + 2 * pieces]
    outs = refs[2 + 2 * pieces : 6 + 2 * pieces]
    step = pl.program_id(0)
    if not tall:
        own_t, rec_t = refs[6 + 2 * pieces :]

        @pl.when(step == 0)
        def _():
            turn_rows(own, own_t, part)
            turn_rows(rec, rec_t, part)

    for half in range(2):

        @pl.when((step < tiles) if half == 0 else (step >= tiles))
        def _():
            if tall:
                total = tall_dot(own, units_own) + tall_dot(rec, units_rec)
            for kind in range(2):
                out = outs[2 * half + kind]
                for place, slot in enumerate(slots[half][kind]):
                    columns = slice(slot * part, (slot + 1) * part)
                    if tall:
                        out[place] = total[:, columns].astype(BF)
                    else:
                        out[place] = (
                            wide_dot(own_t, columns, units_own)
                            + wide_dot(rec_t, columns, units_rec)
                        ).astype(BF)


class Joined:
    def __init__(self, lhs, units, orders, part, tall=False):
        rows, slotted = lhs[0].shape
        groups = slotted // part
        kinds, _, wide = units[0][0].shape
        tile = next(t for t in (512, 256, 128) if (kinds * wide // 2) % t == 0 and wide % t == 0)
        each = wide // tile
        tiles = kinds * each // 2
        slots = tuple(self.slots(order) for order in orders)
        whole = pl.BlockSpec((rows, slotted), lambda j: (0, 0))
        columns = [
            pl.BlockSpec((1, piece.shape[1], tile), lambda j: (j // each, 0, j % each))
            for piece in (*units[0], *units[1])
        ]
        here = groups // 2
        shapes, specs = [], []
        for half in range(2):
            for kind in range(2):

                def at(j, half=half):
                    return (
                        jnp.minimum(j, tiles - 1) if half == 0 else jnp.maximum(j - tiles, 0)
                    )

                if tall:
                    shape, block = (here, tiles * tile, part), (here, tile, part)
                    specs.append(pl.BlockSpec(block, lambda j, at=at: (0, at(j), 0)))
                else:
                    shape, block = (here, part, tiles * tile), (here, part, tile)
                    specs.append(pl.BlockSpec(block, lambda j, at=at: (0, 0, at(j))))
                shapes.append(jax.ShapeDtypeStruct(shape, BF))
        outs = pl.pallas_call(
            functools.partial(product_body, slots, part, tiles, tall, len(units[0])),
            grid=(2 * tiles,),
            in_specs=[whole, whole, *columns],
            out_specs=specs,
            out_shape=shapes,
            scratch_shapes=[] if tall else [pltpu.VMEM((slotted, rows), BF)] * 2,
            compiler_params=params(58),
            cost_estimate=cost(),
            name="product",
        )(*lhs, *units[0], *units[1])
        self.orders, self.tall = orders, tall
        self.sent = [outs[0], outs[2]]
        self.kept = [[outs[1]], [outs[3]]]
        self.made = outs[0]
        self.done = 0

    def slots(self, order):
        slots = [0]
        for bit in reversed(order):
            slots = slots + [slot + bit for slot in slots]
        half = len(slots) // 2
        return tuple(slots[half:]), tuple(slots[:half])

    def send(self, *earlier):
        self.arrived = []
        for half in range(2):
            bit = 2 * self.orders[half][self.done]
            sent = after(self.sent[half], *earlier) if earlier else self.sent[half]
            arrived = swapped(sent, "seq", bit)
            self.arrived.append(arrived)
            self.kept[half].append(arrived)
        self.done += 1

    def add(self, *earlier):
        kept = [list(arrays) for arrays in self.kept]
        if earlier:
            kept[0][0] = after(kept[0][0], *earlier)
        left = len(self.orders[0]) - self.done
        self.sent = upper_sums(kept, 2 ** (left - 1))
        self.made = self.sent[0]

    def finish(self, *earlier):
        while self.done < len(self.orders[0]):
            self.add(*earlier)
            self.send()
        kept = [list(arrays) for arrays in self.kept]
        if earlier:
            kept[0][0] = after(kept[0][0], *earlier)
        return kept


def whole_body(part, pieces, own, rec, *refs):
    units_own, units_rec = refs[:pieces], refs[pieces : 2 * pieces]
    out, own_t, rec_t = refs[2 * pieces :]

    @pl.when(pl.program_id(0) == 0)
    def _():
        turn_rows(own, own_t, part)
        turn_rows(rec, rec_t, part)

    for slot in range(out.shape[0]):
        columns = slice(slot * part, (slot + 1) * part)
        out[slot, 0] = (
            wide_dot(own_t, columns, units_own) + wide_dot(rec_t, columns, units_rec)
        ).astype(BF)


def whole_product(lhs, units, part):
    rows, slotted = lhs[0].shape
    groups = slotted // part
    kinds, _, wide = units[0][0].shape
    tile = min(512, wide)
    each = wide // tile
    whole = pl.BlockSpec((rows, slotted), lambda j: (0, 0))
    columns = [
        pl.BlockSpec((1, piece.shape[1], tile), lambda j: (j // each, 0, j % each))
        for piece in (*units[0], *units[1])
    ]
    return pl.pallas_call(
        functools.partial(whole_body, part, len(units[0])),
        grid=(kinds * each,),
        in_specs=[whole, whole, *columns],
        out_specs=pl.BlockSpec(
            (groups, 1, part, tile), lambda j: (0, j // each, 0, j % each)
        ),
        out_shape=jax.ShapeDtypeStruct((groups, kinds, part, wide), BF),
        scratch_shapes=[pltpu.VMEM((slotted, rows), BF)] * 2,
        compiler_params=params(58),
        cost_estimate=cost(),
        name="whole_product",
    )(*lhs, *units[0], *units[1])


def plane_sum(products):
    groups = products.shape[0]
    flat = products.reshape(-1, products.shape[-1])
    members = [[2 * group + core for group in range(groups)] for core in range(2)]
    mine = lax.psum_scatter(
        flat, "seq", scatter_dimension=0, axis_index_groups=members, tiled=True
    )
    return mine.reshape(products.shape[1:])


def sums_body(counts, tiles, *refs):
    ins, outs = refs[: sum(counts)], refs[sum(counts) :]
    step = pl.program_id(0)
    start = 0
    for source, count in enumerate(counts):
        arrays = ins[start : start + count]
        start += count
        out = outs[source] if len(outs) > 1 else outs[0]

        @pl.when(step // tiles == source)
        def _():
            total = arrays[0][...].astype(F32)
            for array in arrays[1:]:
                total = total + array[...].astype(F32)
            out[...] = total.reshape(out.shape).astype(out.dtype)


def source_tile(step, source, tiles):
    return jnp.clip(step - source * tiles, 0, tiles - 1)


def upper_sums(sources, here):
    _, rows, columns = sources[0][0].shape
    tiles = 2
    block = (here, rows // tiles, columns)
    in_specs, arrays = [], []
    for source, parts in enumerate(sources):
        for array in parts:
            in_specs.append(
                pl.BlockSpec(block, lambda j, s=source: (1, source_tile(j, s, tiles), 0))
            )
            arrays.append(array)
    return pl.pallas_call(
        functools.partial(sums_body, [len(parts) for parts in sources], tiles),
        grid=(len(sources) * tiles,),
        in_specs=in_specs,
        out_specs=[
            pl.BlockSpec(block, lambda j, s=source: (0, source_tile(j, s, tiles), 0))
            for source in range(len(sources))
        ],
        out_shape=[jax.ShapeDtypeStruct((here, rows, columns), BF)] * len(sources),
        compiler_params=params(58),
        cost_estimate=cost(),
        name="upper_sums",
    )(*arrays)


def final_sums(sources, tall, shape):
    sources = [[part if isinstance(part, tuple) else (part, 0) for part in parts] for parts in sources]
    _, rows, columns = sources[0][0][0].shape
    if tall:
        tile = min(512, rows)
        tiles = rows // tile
        block, out_block = (1, tile, columns), (tile, columns)
        out_spec = pl.BlockSpec(out_block, lambda j: (j, 0))

        def at(j, s, slot):
            return (slot, source_tile(j, s, tiles), 0)
    else:
        tile = next(
            t for t in (2048, 1024, 512, 256, 128) if columns % t == 0 and shape[2] % t == 0
        )
        tiles = columns // tile
        each = shape[2] // tile
        block, out_block = (1, rows, tile), (1, rows, tile)
        out_spec = pl.BlockSpec(out_block, lambda j: (j // each, 0, j % each))

        def at(j, s, slot):
            return (slot, 0, source_tile(j, s, tiles))

    in_specs, arrays = [], []
    for source, parts in enumerate(sources):
        for array, slot in parts:
            in_specs.append(pl.BlockSpec(block, lambda j, s=source, slot=slot: at(j, s, slot)))
            arrays.append(array)
    return pl.pallas_call(
        functools.partial(sums_body, [len(parts) for parts in sources], tiles),
        grid=(len(sources) * tiles,),
        in_specs=in_specs,
        out_specs=out_spec,
        out_shape=jax.ShapeDtypeStruct(shape, F32),
        compiler_params=params(58),
        cost_estimate=cost(),
        name="final_sums",
    )(*arrays)


def triple_body(counts, *refs):
    out = refs[-1]
    kinds, _, wide = out.shape
    start = 0
    column = 0
    for count in counts:
        arrays = refs[start : start + count]
        start += count
        width = arrays[0].shape[2]
        done = 0
        while done < width:
            kind, at = column // wide, column % wide
            step = min(width - done, wide - at)
            total = arrays[0][0, :, done : done + step].astype(F32)
            for array in arrays[1:]:
                total = total + array[0, :, done : done + step].astype(F32)
            out[kind, :, at : at + step] = total
            done += step
            column += step


def triple_sums(sources, shape):
    arrays = [array for parts in sources for array in parts]
    return pl.pallas_call(
        functools.partial(triple_body, [len(parts) for parts in sources]),
        grid=(1,),
        in_specs=[
            pl.BlockSpec((1,) + array.shape[1:], lambda j: (0, 0, 0)) for array in arrays
        ],
        out_specs=pl.BlockSpec(shape, lambda j: (0, 0, 0)),
        out_shape=jax.ShapeDtypeStruct(shape, F32),
        compiler_params=params(VMEM),
        cost_estimate=cost(),
        name="triple_sums",
    )(*arrays)


def ring_body(a, b, out):
    out[...] = (a[...].astype(F32) + b[...].astype(F32)).astype(BF)


def ring_sum(arrived, own):
    rows, width = own.shape
    spec = pl.BlockSpec((rows // 2, width), lambda j: (j, 0))
    return pl.pallas_call(
        ring_body,
        grid=(2,),
        in_specs=[spec, spec],
        out_specs=spec,
        out_shape=jax.ShapeDtypeStruct((rows, width), BF),
        compiler_params=params(VMEM),
        cost_estimate=cost(),
        name="ring_sum",
    )(arrived, own)


def rows_body(count, rows, ids, gated, *refs):
    mixes, out, mix_all = refs[:count], refs[count], refs[count + 1]

    @pl.when(pl.program_id(0) == 0)
    def _():
        for place in range(count):
            there = pl.ds(pl.multiple_of(ids[place] * rows, rows), rows)
            mix_all[there, :] = mixes[place][...]

    out[0] = dot(gated[...], mix_all[...], 0, 0).astype(BF)


def rows_product(gated_plane, mixes, count):
    rows, part = mixes[0].shape
    chans = gated_plane.shape[1] // count
    ids = jnp.bitwise_xor(
        lax.axis_index("seq"), jnp.arange(len(mixes), dtype=jnp.int32)
    ).astype(jnp.int32)
    all_rows = rows * len(mixes)
    return pl.pallas_call(
        functools.partial(rows_body, len(mixes), rows),
        grid_spec=pltpu.PrefetchScalarGridSpec(
            num_scalar_prefetch=1,
            grid=(count,),
            in_specs=[pl.BlockSpec((all_rows, chans), lambda r, ids: (0, r))]
            + [pl.BlockSpec((rows, part), lambda r, ids: (0, 0))] * len(mixes),
            out_specs=pl.BlockSpec((1, chans, part), lambda r, ids: (r, 0, 0)),
            scratch_shapes=[pltpu.VMEM((all_rows, part), BF)],
        ),
        out_shape=jax.ShapeDtypeStruct((count, chans, part), BF),
        compiler_params=params(60),
        cost_estimate=cost(),
        name="rows_product",
    )(ids, gated_plane, *mixes)


def spread_body(slots, part, ids, rows_ref, *outs):
    for slot in range(slots):
        start = pl.multiple_of(ids[slot] * part, part)
        outs[slot][...] = rows_ref[:, pl.ds(start, part)]


def spread_slices(rows):
    seq = lax.axis_size("seq")
    part = rows.shape[1] // seq
    ids = jnp.bitwise_xor(lax.axis_index("seq"), jnp.arange(seq, dtype=jnp.int32))
    ids = ids.astype(jnp.int32)
    if part % 128:
        slices = [lax.dynamic_slice_in_dim(rows, ids[q] * part, part, 1) for q in range(seq)]
    else:
        slices = pl.pallas_call(
            functools.partial(spread_body, seq, part),
            in_specs=[
                pl.BlockSpec(memory_space=pltpu.SMEM),
                pl.BlockSpec(memory_space=pltpu.VMEM),
            ],
            out_specs=[pl.BlockSpec(memory_space=pltpu.VMEM)] * seq,
            out_shape=[jax.ShapeDtypeStruct((rows.shape[0], part), BF)] * seq,
            compiler_params=params(VMEM),
            cost_estimate=cost(),
            name="spread_slices",
        )(ids, rows)
    return slices


def project_body(count, *refs):
    toks = refs[:count]
    gain_ref, weights, first_ref, second_ref, third_ref, mixed, normed, scale_ref = refs[count:]
    rows = toks[0].shape[0]

    @pl.when(pl.program_id(0) == 0)
    def _():
        for place in range(count):
            here = pl.ds(place * rows, rows)
            values = toks[place][...].astype(F32)
            scale = lax.rsqrt(jnp.mean(values * values, axis=-1, keepdims=True) + EPS)
            normed[here, :] = (values * scale * gain_ref[...]).astype(BF)
            scale_ref[here, :] = scale

    first = dot(normed[...], weights[0], 1, 0)
    third = dot(normed[...], weights[2], 1, 0)
    first_ref[...] = first
    second_ref[...] = dot(normed[...], weights[1], 1, 0)
    third_ref[...] = third
    mixed[...] = (first * third).astype(BF)


def in_projection(toks, gain, weights, tile=256):
    count = len(toks)
    rows, width = toks[0].shape
    kinds, _, chans = weights.shape
    all_rows = count * rows
    block = pl.BlockSpec((rows, width), lambda j: (0, 0))
    return pl.pallas_call(
        functools.partial(project_body, count),
        grid=(chans // tile,),
        in_specs=[block] * count
        + [
            pl.BlockSpec((1, width), lambda j: (0, 0)),
            pl.BlockSpec((kinds, width, tile), lambda j: (0, 0, j)),
        ],
        out_specs=[
            *([pl.BlockSpec((all_rows, tile), lambda j: (0, j))] * (kinds + 1)),
            pl.BlockSpec((all_rows, width), lambda j: (0, 0)),
            pl.BlockSpec((all_rows, 1), lambda j: (0, 0)),
        ],
        out_shape=[
            *([jax.ShapeDtypeStruct((all_rows, chans), F32)] * kinds),
            jax.ShapeDtypeStruct((all_rows, chans), BF),
            jax.ShapeDtypeStruct((all_rows, width), BF),
            jax.ShapeDtypeStruct((all_rows, 1), F32),
        ],
        compiler_params=params(60),
        cost_estimate=cost(),
        name="in_projection",
    )(*toks, gain.reshape(1, width), weights)


def shifted(values, steps, edge):
    rows = values.shape[0]
    moved = pltpu.roll(values, steps % rows, 0)
    place = lax.broadcasted_iota(jnp.int32, values.shape, 0)
    for k in range(abs(steps)):
        at = k if steps > 0 else rows - 1 - k
        row = edge[k : k + 1] if steps > 0 else edge[abs(steps) - 1 - k : abs(steps) - k]
        moved = jnp.where(place == at, row, moved)
    return moved


def conv_body(count, second, mixed, before, taps, masks, conv_ref, *gated):
    rows = second.shape[0] // count
    for place in range(count):
        here = pl.ds(place * rows, rows)
        values = mixed[here, :].astype(F32)
        edge = before[place]
        lag_one = masks[here, 0:1] * shifted(values, 1, edge[1:2])
        lag_two = masks[here, 1:2] * shifted(values, 2, edge)
        conv = taps[0:1, :] * values + taps[1:2, :] * lag_one + taps[2:3, :] * lag_two
        conv_ref[here, :] = conv
        gated[place][...] = (second[here, :] * conv).astype(BF)


def conv_forward(second, mixed, before, taps, masks, count, tile=256):
    all_rows, chans = mixed.shape
    rows = all_rows // count
    wide = pl.BlockSpec((all_rows, tile), lambda j: (0, j))
    results = pl.pallas_call(
        functools.partial(conv_body, count),
        grid=(chans // tile,),
        in_specs=[
            wide,
            wide,
            pl.BlockSpec((count, 2, tile), lambda j: (0, 0, j)),
            pl.BlockSpec((3, tile), lambda j: (0, j)),
            pl.BlockSpec(masks.shape, lambda j: (0, 0)),
        ],
        out_specs=[wide] + [pl.BlockSpec((rows, tile), lambda j: (0, j))] * count,
        out_shape=[jax.ShapeDtypeStruct((all_rows, chans), F32)]
        + [jax.ShapeDtypeStruct((rows, chans), BF)] * count,
        compiler_params=params(60),
        cost_estimate=cost(),
        name="conv_forward",
    )(second, mixed, before, taps, masks)
    return results[0], results[1:]


def conv_back_body(count, *refs):
    grads = refs[:count]
    first, second, third, conv, mixed, before, behind, taps = refs[count : count + 8]
    masks, triple, tap_ref = refs[count + 8 :]
    rows = grads[0].shape[0]
    sums = [None] * 3
    for place in range(count):
        here = pl.ds(place * rows, rows)
        grad = grads[place][...].astype(F32)
        grad_conv = (grad * second[here, :]).astype(BF).astype(F32)
        edge = behind[place]
        grad_mixed = (
            taps[0:1, :] * grad_conv
            + taps[1:2, :] * masks[here, 2:3] * shifted(grad_conv, -1, edge[0:1])
            + taps[2:3, :] * masks[here, 3:4] * shifted(grad_conv, -2, edge)
        )
        triple[0, here, :] = (grad_mixed * third[here, :]).astype(BF)
        triple[1, here, :] = (grad * conv[here, :]).astype(BF)
        triple[2, here, :] = (grad_mixed * first[here, :]).astype(BF)
        values = mixed[here, :].astype(F32)
        lags = before[place]
        for tap, lagged in enumerate(
            (
                values,
                masks[here, 0:1] * shifted(values, 1, lags[1:2]),
                masks[here, 1:2] * shifted(values, 2, lags),
            )
        ):
            part = jnp.sum(grad_conv * lagged, axis=0, keepdims=True)
            sums[tap] = part if sums[tap] is None else sums[tap] + part
    tap_ref[...] = jnp.concatenate(sums, axis=0)


def conv_backward(grads, first, second, third, conv, mixed, before, behind, taps, masks, tile=128):
    count = len(grads)
    all_rows, chans = mixed.shape
    rows = all_rows // count
    wide = pl.BlockSpec((all_rows, tile), lambda j: (0, j))
    edge = pl.BlockSpec((count, 2, tile), lambda j: (0, 0, j))
    three = pl.BlockSpec((3, tile), lambda j: (0, j))
    return pl.pallas_call(
        functools.partial(conv_back_body, count),
        grid=(chans // tile,),
        in_specs=[pl.BlockSpec((rows, tile), lambda j: (0, j))] * count
        + [wide] * 5
        + [edge, edge, three]
        + [pl.BlockSpec(masks.shape, lambda j: (0, 0))],
        out_specs=[pl.BlockSpec((3, all_rows, tile), lambda j: (0, 0, j)), three],
        out_shape=[
            jax.ShapeDtypeStruct((3, all_rows, chans), BF),
            jax.ShapeDtypeStruct((3, chans), F32),
        ],
        compiler_params=params(60),
        cost_estimate=cost(),
        name="conv_backward",
    )(*grads, first, second, third, conv, mixed, before, behind, taps, masks)


def back_body(count, *refs):
    grads, weights = refs[:2]
    toks = refs[2 : 2 + count]
    scale_ref = refs[2 + count]
    outs = refs[3 + count : 3 + 2 * count]
    gains_ref = refs[3 + 2 * count]
    rows = toks[0].shape[0]
    total = dot(grads[0], weights[0], 1, 1)
    for kind in range(1, grads.shape[0]):
        total = total + dot(grads[kind], weights[kind], 1, 1)
    gains = None
    for place in range(count):
        here = total[place * rows : (place + 1) * rows]
        outs[place][...] = here.astype(BF)
        unit = toks[place][...].astype(F32) * scale_ref[pl.ds(place * rows, rows), :]
        part = jnp.sum(here * unit, axis=0, keepdims=True)
        gains = part if gains is None else gains + part
    gains_ref[...] = gains


def mixer_back(grads, weights, toks, scale, tile=512):
    kinds, all_rows, chans = grads.shape
    width = weights.shape[1]
    count = len(toks)
    rows = all_rows // count
    block = pl.BlockSpec((rows, tile), lambda j: (0, j))
    results = pl.pallas_call(
        functools.partial(back_body, count),
        grid=(width // tile,),
        in_specs=[
            pl.BlockSpec((kinds, all_rows, chans), lambda j: (0, 0, 0)),
            pl.BlockSpec((kinds, tile, chans), lambda j: (0, j, 0)),
        ]
        + [block] * count
        + [pl.BlockSpec((all_rows, 1), lambda j: (0, 0))],
        out_specs=[block] * count + [pl.BlockSpec((1, tile), lambda j: (0, j))],
        out_shape=[jax.ShapeDtypeStruct((rows, width), BF)] * count
        + [jax.ShapeDtypeStruct((1, width), F32)],
        compiler_params=params(60),
        cost_estimate=cost(),
        name="mixer_back",
    )(grads, weights, *toks, scale)
    return results[:count], results[count][0]


def full_others(others):
    seq = lax.axis_size("seq")
    stacked = jnp.stack(others, axis=1)
    stacked = stacked.reshape((seq,) + stacked.shape[2:])
    slots = jnp.bitwise_xor(lax.axis_index("seq"), jnp.arange(seq, dtype=jnp.int32))
    full = jnp.transpose(jnp.take(stacked, slots, axis=0), (1, 2, 0, 3))
    return full.reshape(full.shape[:2] + (-1,))


def plane_ids():
    place = lax.axis_index("seq")
    groups = lax.axis_size("seq") // 2
    chips = jnp.bitwise_xor(place // 2, jnp.arange(groups, dtype=jnp.int32))
    return jnp.concatenate([chips, (place % 2)[None]]).astype(jnp.int32)


def core_columns(ids, groups, kind, part, base=0):
    core = ids[groups]
    offset = jnp.where(core == kind, 0, part)
    return pl.ds(pl.multiple_of(base + offset, part), part)


def mixer_body(count, ids, *refs):
    gated = refs[:count]
    own_w, same_w, cross_w, rows_ref, gain_ref = refs[count : count + 5]
    state_ref, normed_ref, scale_ref, joined_ref = refs[count + 5 :]
    step = pl.program_id(0)
    part = same_w.shape[3]
    groups = pl.num_programs(0)
    base = pl.multiple_of(step * 2 * part, 2 * part)
    for kind, other_w in enumerate((same_w, cross_w)):
        inner = core_columns(ids, groups, kind, part)
        total = dot(gated[0][...], own_w[:, inner], 1, 0)
        for place in range(1, count):
            total = total + dot(gated[place][...], other_w[0, count - 1 - place], 1, 0)
        columns = core_columns(ids, groups, kind, part, base)
        state_ref[:, columns] = total + rows_ref[:, columns].astype(F32)

    @pl.when(step == groups - 1)
    def _():
        state = state_ref[...]
        scale = lax.rsqrt(jnp.mean(state * state, axis=-1, keepdims=True) + EPS)
        normed_ref[...] = (state * scale * gain_ref[...]).astype(BF)
        scale_ref[...] = scale
        chans = gated[0].shape[1]
        for place in range(count):
            joined_ref[:, place * chans : (place + 1) * chans] = gated[place][...]


def mixer_rows(gated, own_w, others, input_rows, gain):
    count = len(gated)
    rows, width = input_rows.shape
    chans = gated[0].shape[1]
    groups, _, _, part = others[0].shape
    if part % 128:
        full = full_others(others)
        total = dot(gated[0], own_w, 1, 0)
        for r in range(1, count):
            total = total + dot(gated[r], full[count - 1 - r], 1, 0)
        state = input_rows.astype(F32) + total
        unit, scale = unit_rows(state)
        return state, (unit * gain).astype(BF), scale, jnp.concatenate(gated, axis=1)
    full_rows = pl.BlockSpec((rows, width), lambda t, ids: (0, 0))
    weights = pl.BlockSpec((1, count - 1, chans, part), lambda t, ids: (ids[t], 0, 0, 0))
    return pl.pallas_call(
        functools.partial(mixer_body, count),
        grid_spec=pltpu.PrefetchScalarGridSpec(
            num_scalar_prefetch=1,
            grid=(groups,),
            in_specs=[pl.BlockSpec((rows, chans), lambda t, ids: (0, 0))] * count
            + [
                pl.BlockSpec((chans, 2 * part), lambda t, ids: (0, t)),
                weights,
                weights,
                full_rows,
                pl.BlockSpec((1, width), lambda t, ids: (0, 0)),
            ],
            out_specs=[
                full_rows,
                full_rows,
                pl.BlockSpec((rows, 1), lambda t, ids: (0, 0)),
                pl.BlockSpec((rows, count * chans), lambda t, ids: (0, 0)),
            ],
        ),
        out_shape=[
            jax.ShapeDtypeStruct((rows, width), F32),
            jax.ShapeDtypeStruct((rows, width), BF),
            jax.ShapeDtypeStruct((rows, 1), F32),
            jax.ShapeDtypeStruct((rows, count * chans), BF),
        ],
        compiler_params=params(VMEM),
        cost_estimate=cost(),
        name="mixer_rows",
    )(plane_ids(), *gated, own_w, *others, input_rows, gain.reshape(1, width))


def gated_body(count, ids, *refs):
    own_w, same_w, cross_w, arrived, part_own, state_ref, scale_ref, cot_ref, gain_ref = refs[:9]
    outs = refs[9 : 9 + count]
    grad_ref, mix_ref, gains_ref = refs[9 + count : 12 + count]
    accs = refs[12 + count :]
    step = pl.program_id(0)
    part = same_w.shape[3]
    groups = pl.num_programs(0)

    @pl.when(step == 0)
    def _():
        grad_normed = arrived[...].astype(F32) + part_own[...].astype(F32)
        unit = state_ref[...] * scale_ref[...]
        weighted = grad_normed * gain_ref[...]
        grad = cot_ref[...].astype(F32) + scale_ref[...] * (
            weighted - unit * jnp.mean(weighted * unit, axis=-1, keepdims=True)
        )
        grad_ref[...] = grad
        mix_ref[...] = grad.astype(BF)
        gains_ref[...] = jnp.sum(grad_normed * unit, axis=0, keepdims=True)
        for acc in accs:
            acc[...] = jnp.zeros_like(acc)

    base = pl.multiple_of(step * 2 * part, 2 * part)
    mix = [
        mix_ref[:, core_columns(ids, groups, kind, part, base)] for kind in range(2)
    ]
    accs[0][...] += dot(mix_ref[:, pl.ds(base, 2 * part)], own_w[...], 1, 1)
    for place in range(1, count):
        accs[place][...] += dot(mix[0], same_w[0, count - 1 - place], 1, 1) + dot(
            mix[1], cross_w[0, count - 1 - place], 1, 1
        )

    @pl.when(step == groups - 1)
    def _():
        for out, acc in zip(outs, accs):
            out[...] = acc[...].astype(BF)


def gated_rows(arrived, part_own, state, scale, cot, gain, own_w, others):
    rows, width = state.shape
    chans = own_w.shape[0]
    groups, less, _, part = others[0].shape
    count = less + 1
    if part % 128:
        full = full_others(others)
        grad_normed = arrived.astype(F32) + part_own.astype(F32)
        unit = state * scale
        grad = cot.astype(F32) + norm_back(grad_normed, unit, scale, gain)
        mix = grad.astype(BF)
        outs = [dot(mix, own_w, 1, 1).astype(BF)] + [
            dot(mix, full[count - 1 - r], 1, 1).astype(BF) for r in range(1, count)
        ]
        return outs, grad, mix, jnp.sum(grad_normed * unit, axis=0)
    full_rows = pl.BlockSpec((rows, width), lambda t, ids: (0, 0))
    one_row = pl.BlockSpec((1, width), lambda t, ids: (0, 0))
    weights = pl.BlockSpec((1, less, chans, part), lambda t, ids: (ids[t], 0, 0, 0))
    results = pl.pallas_call(
        functools.partial(gated_body, count),
        grid_spec=pltpu.PrefetchScalarGridSpec(
            num_scalar_prefetch=1,
            grid=(groups,),
            in_specs=[
                pl.BlockSpec((chans, 2 * part), lambda t, ids: (0, t)),
                weights,
                weights,
                full_rows,
                full_rows,
                full_rows,
                pl.BlockSpec((rows, 1), lambda t, ids: (0, 0)),
                full_rows,
                one_row,
            ],
            out_specs=[pl.BlockSpec((rows, chans), lambda t, ids: (0, 0))] * count
            + [full_rows, full_rows, one_row],
            scratch_shapes=[pltpu.VMEM((rows, chans), F32)] * count,
        ),
        out_shape=[jax.ShapeDtypeStruct((rows, chans), BF)] * count
        + [
            jax.ShapeDtypeStruct((rows, width), F32),
            jax.ShapeDtypeStruct((rows, width), BF),
            jax.ShapeDtypeStruct((1, width), F32),
        ],
        compiler_params=params(60),
        cost_estimate=cost(),
        name="gated_rows",
    )(plane_ids(), own_w, *others, arrived, part_own, state, scale, cot, gain.reshape(1, width))
    return results[:count], results[count], results[count + 1], results[count + 2][0]


def on_device(
    tokens,
    norm_gains,
    conv_weight,
    in_weight,
    out_weight,
    gate_up_weight,
    down_weight,
    starts,
    cotangent,
):
    shard_rows, width = tokens.shape
    chan_count = lax.axis_size("chan")
    seq_count = lax.axis_size("seq")
    seq_rows = shard_rows * chan_count
    chan_cols = conv_weight.shape[1]
    chan_index = lax.axis_index("chan")
    seq_index = lax.axis_index("seq")
    relative = jnp.arange(chan_count, dtype=jnp.int32)
    owner = (chan_index - relative) % chan_count
    positions = (
        seq_index * seq_rows
        + owner[:, None] * shard_rows
        + jnp.arange(shard_rows, dtype=jnp.int32)[None, :]
    )
    keep_one, keep_two = keep_masks(positions, starts)
    next_one, unused_one = keep_masks(positions + 1, starts)
    unused_two, next_two = keep_masks(positions + 2, starts)
    gain_one = norm_gains[0].astype(F32)
    gain_two = norm_gains[1].astype(F32)
    conv_taps = conv_weight.astype(F32)
    bits = group_bits()
    orders = (bits[::-1], bits)

    part = width // seq_count
    w_own = lax.dynamic_slice_in_dim(out_weight, seq_index * part, part, 1)
    w_one = turned(w_own, "chan", 1)
    w_three = turned(w_own, "chan", 3)
    tok_one = turned(tokens, "chan", 1)
    w_two = turned(after(w_one, w_three, tok_one), "chan", 1)
    tok_three = turned(after(tokens, w_three, tok_one), "chan", 3)
    others = jnp.stack([w_one, w_two, w_three])[None]
    halves = [others[:, :, : chan_cols // 2], others[:, :, chan_cols // 2 :]]
    first_arrived = [
        swapped(half, "seq", 2 * order[0]) for half, order in zip(halves, orders)
    ]
    tok_two = turned(after(tok_one, w_two), "chan", 1)
    second_arrived = []
    for place, order in enumerate(orders):
        held = jnp.concatenate(
            [halves[place], after(first_arrived[place], tok_three)], axis=0
        )
        for bit in order[1:-1]:
            held = jnp.concatenate([held, swapped(held, "seq", 2 * bit)], axis=0)
        halves[place] = held
        second_arrived.append(swapped(held, "seq", 2 * order[-1]))
    grad_out = lax.all_gather(after(cotangent, w_three, tok_one), "chan", axis=0, tiled=True)
    tok_blocks = [tokens, tok_one, tok_two, tok_three]
    for place, order in enumerate(orders):
        held = jnp.concatenate([halves[place], after(second_arrived[place], tok_two)], axis=0)
        split = held.reshape((2,) * len(order) + held.shape[1:])
        axes = [len(order) - 1 - order.index(bit) for bit in bits]
        held = jnp.transpose(split, (*axes, *range(len(order), split.ndim))).reshape(held.shape)
        halves[place] = held
    held = jnp.concatenate(halves, axis=2)
    others = (held, swapped(held, "seq", 1))
    masks = jnp.concatenate(
        [
            mask.reshape(seq_rows, 1)
            for mask in (keep_one, keep_two, next_one, next_two)
        ]
        + [jnp.zeros((seq_rows, 124), F32)],
        axis=1,
    )
    *projected, mixed_in, normed_one, scale_all = in_projection(
        [after(tokens, held, masks)] + tok_blocks[1:], gain_one, in_weight
    )

    def at_edge(edge_rows, device):
        return lax.dynamic_index_in_dim(edge_rows, (chan_index - device) % chan_count, 0, False)

    def is_owner(device):
        return (owner == device)[:, None, None]

    ends = jnp.stack(
        [mixed_in[(r + 1) * shard_rows - 2 : (r + 1) * shard_rows] for r in range(chan_count)]
    )
    rim_rows = passed_along(at_edge(ends, chan_count - 1), "seq", 1)
    before = jnp.where(is_owner(0), rim_rows[None], jnp.roll(ends, -1, axis=0)).astype(F32)
    conv_out, gated_mix = conv_forward(
        projected[1], mixed_in, before, conv_taps, masks, chan_count
    )
    gated_mix = [after(rows, grad_out) for rows in gated_mix]
    gated_rows_own = [gated_mix[0]] + [
        turned(gated_mix[r], "chan", -r) for r in range(1, chan_count)
    ]
    state_own, normed_two_own, scale_two, gated_joined = mixer_rows(
        gated_rows_own, out_weight, others, tokens, gain_two
    )
    n_one = turned(normed_two_own, "chan", 1)
    normed_one_slices = own_slices(
        after(normed_one, normed_two_own), jnp.arange(chan_count, dtype=jnp.int32)
    )
    cot_slices = own_slices(after(grad_out, normed_two_own), owner)
    n_one = after(n_one, normed_one_slices[0], cot_slices[0])
    gated_plane = lax.all_gather(
        after(gated_joined, n_one),
        "seq",
        axis=0,
        tiled=True,
    )
    n_two = turned(n_one, "chan", 1)
    n_three = turned(after(normed_two_own, n_one), "chan", 3)
    hidden_a, pair_a, ffn_parts, grad_two_parts = feed_forward(
        owner,
        [normed_two_own, n_one],
        grad_out,
        gate_up_weight,
        down_weight,
        0,
    )
    ffn_parts, grad_two_parts, hidden_a, pair_a = [
        after(value, n_two, n_three)
        if not isinstance(value, (list, tuple))
        else [after(one, n_two, n_three) for one in value]
        for value in (ffn_parts, grad_two_parts, hidden_a, pair_a)
    ]
    run = turned(grad_two_parts[1], "chan", 1)
    ffn_one = turned(ffn_parts[1], "chan", -1)
    hidden_a_rec = swapped(hidden_a, "seq", 1)
    pair_a_rec = swapped(pair_a, "seq", 1)
    hidden_b, pair_b, ffn_more, grad_more = feed_forward(
        owner,
        [n_two, n_three],
        grad_out,
        gate_up_weight,
        down_weight,
        2,
    )
    ffn_parts = list(ffn_parts) + list(ffn_more)
    grad_two_parts = list(grad_two_parts) + list(grad_more)

    total = ring_sum(run, grad_two_parts[2])
    hidden_b, pair_b = [
        after(units, total, ffn_one, hidden_a_rec, pair_a_rec) for units in (hidden_b, pair_b)
    ]
    hidden_b_rec = swapped(hidden_b, "seq", 1)
    pair_b_rec = swapped(after(pair_b, hidden_b_rec), "seq", 1)
    run = turned(total, "chan", 1)
    down = Joined(
        (after(cot_slices[0], total), cot_slices[1]),
        ([hidden_a, hidden_b], [hidden_a_rec, hidden_b_rec]),
        orders,
        part,
        tall=True,
    )
    normed_two_slices = own_slices(
        [normed_two_own, n_one, n_two, after(n_three, down.made)], None, False
    )
    total = ring_sum(after(run, normed_two_slices[0]), grad_two_parts[3])
    down.send()
    run = turned(total, "chan", 1)
    gate_up = whole_product(
        (after(normed_two_slices[0], total), normed_two_slices[1]),
        ([pair_a, pair_b], [pair_a_rec, pair_b_rec]),
        part,
    )
    run = after(run, gate_up, *down.arrived)
    gate_up_mine = plane_sum(after(gate_up, gated_plane, run))
    ffn_two = turned(after(ffn_parts[2], run), "chan", -1)

    grad_gated_rows, grad_state_own, grad_mix_own, gain_two_part = gated_rows(
        run,
        grad_two_parts[0],
        state_own,
        scale_two,
        cotangent,
        gain_two,
        out_weight,
        others,
    )
    grad_gated_rows = list(grad_gated_rows)
    grad_gated_rows[1:] = [
        after(rows, ffn_two) for rows in grad_gated_rows[1:]
    ]
    gg = [grad_gated_rows[0]] + [
        turned(grad_gated_rows[r], "chan", r) for r in range(1, chan_count)
    ]
    mixes = spread_slices(after(grad_mix_own, *grad_gated_rows[1:]))
    mixes = [mixes[0]] + [swapped(mixes[q], "seq", q) for q in range(1, seq_count)]
    ffn_two = turned(after(ffn_two, *gg), "chan", -1)
    ffn_three = turned(after(ffn_parts[3], *gg), "chan", -3)
    heads = jnp.stack(
        [
            (
                gg[r][:2].astype(F32) * projected[1][r * shard_rows : r * shard_rows + 2]
            ).astype(BF)
            for r in range(chan_count)
        ]
    )
    rim_back = passed_along(at_edge(heads, 0), "seq", -1)
    behind = jnp.where(is_owner(chan_count - 1), rim_back[None], jnp.roll(heads, 1, axis=0))
    grad_triple, tap_part = conv_backward(
        gg, *projected, conv_out, mixed_in, before, after(behind.astype(F32), *mixes), conv_taps, masks
    )
    grad_one_parts, gain_one_part = mixer_back(grad_triple, in_weight, tok_blocks, scale_all)
    grad_one_parts = [after(rows, ffn_two, ffn_three) for rows in grad_one_parts]
    run = turned(grad_one_parts[1], "chan", 1)
    small = after(
        jnp.concatenate([gain_one_part, gain_two_part, tap_part.reshape(-1)]), grad_one_parts[1]
    )
    small_rec = swapped(small, "seq", 1)
    triple_rec = swapped(after(grad_triple, grad_one_parts[1]), "seq", 1)
    into = Joined(
        (after(normed_one_slices[0], grad_one_parts[1]), normed_one_slices[1]),
        ([grad_triple], [triple_rec]),
        orders,
        part,
    )
    small = small + small_rec
    small_rec = swapped(small, "seq", 2)
    small = small + after(small_rec, into.made)
    into.send(small)
    total = ring_sum(after(run, small), grad_one_parts[2])
    run = turned(total, "chan", 1)
    small_rec = swapped(after(small, total), "seq", 4)
    out_parts = rows_product(after(gated_plane, total), mixes, chan_count)
    out_run = turned(out_parts[3], "chan", 1)
    down.add(out_parts)
    total = ring_sum(after(run, down.made, out_run), grad_one_parts[3])
    out_total = ring_sum(after(out_run, total), out_parts[2])
    run = turned(total, "chan", 1)
    out_run = turned(out_total, "chan", 1)
    down.send(total)
    into.add(out_total)
    into.send()
    gate_up_grad = final_sums(
        [[(after(gate_up_mine, into.made), 0)], [(gate_up_mine, 1)]],
        False,
        (2, part, hidden_a.shape[2]),
    )
    run = after(run, gate_up_grad)
    out_total = ring_sum(after(out_run, gate_up_grad), out_parts[1])
    out_run = turned(out_total, "chan", 1)
    small = small + after(small_rec, out_total)
    if seq_count > 8:
        small = summed(small, "seq", 8)
    gains = small[: 2 * width]
    gains_rec = swapped(gains, "chan", 1)
    down_grad = final_sums(down.finish(out_total), True, (hidden_a.shape[2], part))
    gains = gains + after(gains_rec, down_grad)
    gains = gains + swapped(gains, "chan", 2)
    in_grad = triple_sums(into.finish(down_grad), (3, part, chan_cols))
    out_grad = out_run.astype(F32) + out_parts[0].astype(F32)

    grad_one_own = run.astype(F32) + grad_one_parts[0].astype(F32)
    input_grad = grad_state_own + norm_back(
        grad_one_own, tokens.astype(F32) * scale_all[:shard_rows], scale_all[:shard_rows], gain_one
    )
    block_output = (state_own + ((ffn_one.astype(F32) + ffn_two.astype(F32)) + (ffn_three.astype(F32) + ffn_parts[0].astype(F32)))).astype(BF)
    gains_grad = gains.reshape(2, width)
    conv_grad = small[2 * width :].reshape(3, chan_cols)
    return (
        block_output,
        input_grad,
        gains_grad,
        conv_grad,
        in_grad,
        out_grad,
        gate_up_grad,
        down_grad,
    )


def solution(mesh):
    placed = (
        P(("seq", "chan"), None),
        P(),
        P(None, "chan"),
        P(None, None, "chan"),
        P("chan", None),
        P(None, None, "chan"),
        P("chan", None),
        P(),
        P(("seq", "chan"), None),
    )
    return jax.shard_map(
        on_device,
        mesh=mesh,
        in_specs=placed,
        out_specs=(
            P(("seq", "chan"), None),
            P(("seq", "chan"), None),
            P(),
            P(None, "chan"),
            P(None, "seq", "chan"),
            P("chan", "seq"),
            P(None, "seq", "chan"),
            P("chan", "seq"),
        ),
        check_vma=False,
    )
```
